256 devices in a mesh: mem: 16 (over z_hi, x, core), lat: 4 (over z_lo), lon: 4 (over y).
Axes of the slice: x: 4, y: 4, z: 8 (z_hi: 2, z_lo: 4; z = z_hi * 4 + z_lo), core: 2. Of those that a mesh axis runs over, the one named last changes fastest.
Arguments:
- control: bfloat16 [64, 256, 128, 128], P('mem', 'lat', 'lon'), may hold values from -21 to 21
- ensemble: bfloat16 [64, 256, 128, 128], P('mem', 'lat', 'lon'), may hold values from -3 to 3
- precision: float32 [256, 128, 128], P('lat', 'lon'), may hold values from 0.5 to 8
- lat_taps: float32 [9], replicated, may hold values from 0.05 to 0.3
- lon_taps: float32 [9], replicated, may hold values from 0.05 to 0.3
- vertical: bfloat16 [128, 128], replicated, may hold values from -0.5 to 0.5
Outputs:
- hessian: float32 [64, 256, 128, 128], P('mem', 'lat', 'lon')
- curvature: float32 [], replicated
The draws below stay inside these ranges and needn't reach their ends.
All inputs are finite; a program needn't handle non-finite values.
Results may differ from the reference program's by a relative error of at most 0.0038.
Values may be sent and summed in bfloat16 or wider, within the bound.
No kernel may reach another device: no remote copies, remote signals or barrier semaphores. Data moves between devices by JAX's collectives and lax.ppermute only.
A program may use at most 64 MiB of HBM per device.

```python
import math
import jax
import jax.numpy as jnp
from jax import lax

LV = 128
TAPS = 9
MEMBERS = 64
NLAT = 256
NLON = 128


def draw_control(key, part):
    first_key = jax.random.fold_in(jax.random.fold_in(key, 11), 0)
    shape = (MEMBERS, NLAT, NLON, LV)
    member_pos = jnp.arange(MEMBERS, dtype=jnp.float32) / max(MEMBERS - 1, 1)
    lat_pos = jnp.arange(NLAT, dtype=jnp.float32) / max(NLAT - 1, 1)
    lon_pos = jnp.arange(NLON, dtype=jnp.float32) / max(NLON - 1, 1)
    exponent = member_pos[:, None, None, None] + lat_pos[None, :, None, None] + lon_pos[None, None, :, None]
    scaling = jnp.exp(0.5 * jnp.log(3.0) * exponent)
    base = jax.random.normal(first_key, shape, jnp.float32)
    base = jnp.clip(base, -4.0, 4.0)
    return (base * scaling).astype(jnp.bfloat16)


def block_scale(stream_key, dims, cuts, low, largest):
    level = 1.0
    for axis_at, shards_of in cuts:
        heights = jax.random.uniform(jax.random.fold_in(jax.random.fold_in(stream_key, 6), axis_at), (shards_of,), jnp.float32, low / len(cuts), largest / len(cuts))
        level = level * jnp.repeat(jnp.exp(heights), dims[axis_at] // shards_of).reshape((-1,) + (1,) * (len(dims) - 1 - axis_at))
    return level


def centred(key, dims, deviation, reach, shards=(), held_as=jnp.bfloat16):
    values = deviation * jax.random.normal(key, dims, jnp.float32)
    if shards:
        values = values * block_scale(key, dims, shards, -0.22, 0.18)
    return jnp.clip(values, -reach, reach).astype(held_as)


def setup_inputs(seed: int = 0) -> dict:
    streams_of = jax.random.split(jax.random.key(seed), 7)
    control = draw_control(jax.random.fold_in(streams_of[6], 71), 0)
    ensemble = centred(streams_of[1], (MEMBERS, NLAT, NLON, LV), 0.5, 3.0, ((0, 16), (1, 4), (2, 4)))
    precision = jnp.clip(jnp.exp(math.log(8.0) - 2.7725887 * jax.random.uniform(streams_of[2], (NLAT, NLON, LV), jnp.float32) ** block_scale(streams_of[2], (NLAT, NLON, LV), ((0, 4), (1, 4)), -0.2, 0.2)), 0.5, 8.0)
    lat_taps = jnp.clip(jnp.exp(jax.random.uniform(streams_of[3], (TAPS,), jnp.float32, math.log(0.05), math.log(0.3))), 0.05, 0.3)
    lon_taps = jnp.clip(jnp.exp(jax.random.uniform(streams_of[4], (TAPS,), jnp.float32, math.log(0.05), math.log(0.3))), 0.05, 0.3)
    vertical = centred(streams_of[5], (LV, LV), LV ** -0.5, 0.5)
    return dict(control=control, ensemble=ensemble, precision=precision, lat_taps=lat_taps, lon_taps=lon_taps, vertical=vertical)


def smooth_member(values, first_taps, second_taps):
    padded = jnp.pad(values, ((4, 4), (0, 0), (0, 0)))
    padded = jnp.concatenate([padded[:, -4:], padded, padded[:, :4]], axis=1)
    across = first_taps[0] * padded[0:NLAT]
    for offset in range(1, TAPS):
        across = across + first_taps[offset] * padded[offset:offset + NLAT]
    result = second_taps[0] * across[:, 0:NLON]
    for offset in range(1, TAPS):
        result = result + second_taps[offset] * across[:, offset:offset + NLON]
    return result


def reference(control, ensemble, precision, lat_taps, lon_taps, vertical):
    def forward(running, inputs):
        member, spread = inputs
        smoothed = smooth_member(member, lat_taps, lon_taps).astype(jnp.bfloat16)
        leveled = jnp.dot(smoothed.reshape(-1, LV), vertical, preferred_element_type=jnp.float32).reshape(smoothed.shape)
        return running + spread * leveled, None

    increment, unused = lax.scan(forward, jnp.zeros((NLAT, NLON, LV), jnp.float32), (control, ensemble))
    weighted = precision * increment

    def adjoint(inputs):
        member, spread = inputs
        member_part = (spread * weighted).astype(jnp.bfloat16)
        adjoint_lev = jnp.dot(member_part.reshape(-1, LV), vertical.T, preferred_element_type=jnp.float32)
        adjoint_lev = adjoint_lev.reshape(member_part.shape).astype(jnp.bfloat16)
        back = smooth_member(adjoint_lev, lat_taps[::-1], lon_taps[::-1])
        hessian = member + back
        return hessian, jnp.sum(member * hessian)

    hessian, terms = lax.map(adjoint, (control, ensemble))
    curvature = jnp.sum(terms) / (MEMBERS * NLAT * NLON * LV)
    return hessian, curvature
```

```python
import functools

import jax
import jax.numpy as jnp
from jax import lax
from jax.experimental import pallas as pl
from jax.experimental.pallas import tpu as pltpu
from jax.sharding import Mesh
from jax.sharding import PartitionSpec as P

MEM = ("zh", "x", "core")
BF = jnp.bfloat16
F32 = jnp.float32
HALO = 4
TAPS = 9
ROWS = 8
VMEM = pl.BlockSpec(memory_space=pltpu.VMEM)
SMEM = pl.BlockSpec(memory_space=pltpu.SMEM)


def ring(axis, step):
    n = lax.axis_size(axis)
    return [(i, (i + step) % n) for i in range(n)]


def line(axis, step):
    n = lax.axis_size(axis)
    return [(i, i + step) for i in range(n) if 0 <= i + step < n]


def params():
    return pltpu.CompilerParams(vmem_limit_bytes=40 * 2**20)


def cost(flops, size):
    return pl.CostEstimate(flops=flops, bytes_accessed=size, transcendentals=0)


def band_kernel(cols, lat_taps, lon_taps, fwd, rev):
    width = fwd.shape[1]
    span = ROWS + 2 * HALO
    centre, side = span * cols, span * HALO
    k = lax.broadcasted_iota(jnp.int32, (cols, width), 1)
    j = lax.broadcasted_iota(jnp.int32, (cols, width), 0)
    west = k - centre
    east = west - side
    in_centre, in_west = k < centre, west < side
    p = jnp.where(in_centre, k // cols, jnp.where(in_west, west // HALO, east // HALO))
    q = jnp.where(in_centre, k % cols + HALO, jnp.where(in_west, west % HALO, east % HALO + cols + HALO))
    b = q - j
    fwd_b, rev_b = (jnp.zeros((cols, width), F32),) * 2
    for t in range(TAPS):
        fwd_b = jnp.where(b == t, lon_taps[t], fwd_b)
        rev_b = jnp.where(b == t, lon_taps[TAPS - 1 - t], rev_b)
    for i in range(ROWS):
        a = p - i
        fwd_a, rev_a = (jnp.zeros((cols, width), F32),) * 2
        for t in range(TAPS):
            fwd_a = jnp.where(a == t, lat_taps[t], fwd_a)
            rev_a = jnp.where(a == t, lat_taps[TAPS - 1 - t], rev_a)
        for out, value in ((fwd, fwd_a * fwd_b), (rev, rev_a * rev_b)):
            high = value.astype(BF)
            low = (value - high.astype(F32)).astype(BF)
            out[i * cols : (i + 1) * cols, :] = high
            out[(ROWS + i) * cols : (ROWS + i + 1) * cols, :] = low


def bands(lat_taps, lon_taps, cols):
    span = ROWS + 2 * HALO
    shape = jax.ShapeDtypeStruct((2 * ROWS * cols, span * (cols + 2 * HALO)), BF)
    return pl.pallas_call(
        functools.partial(band_kernel, cols),
        out_shape=(shape, shape),
        in_specs=[SMEM, SMEM],
        out_specs=(VMEM, VMEM),
        compiler_params=params(),
        cost_estimate=cost(2_000_000, 4 * shape.shape[0] * shape.shape[1]),
        name="bands",
    )(lat_taps, lon_taps)


def around(own, south, north, west, east, member, block, cols):
    blocks = own.shape[1] // (ROWS * cols)
    lo = (block * ROWS - HALO) * cols
    hi = (block * ROWS + ROWS + HALO) * cols
    parts = []
    if block == 0:
        parts.append(south[member])
    parts.append(own[member, max(lo, 0) : min(hi, own.shape[1]), :])
    if block == blocks - 1:
        parts.append(north[member])
    side = slice(block * ROWS * HALO, (block * ROWS + ROWS + 2 * HALO) * HALO)
    parts += [west[member, side, :], east[member, side, :]]
    return jnp.concatenate(parts, axis=0)


def filtered(band, own, south, north, west, east, members, block, cols):
    cells = jnp.concatenate(
        [around(own, south, north, west, east, m, block, cols) for m in members], axis=1
    )
    both = jnp.dot(band[...], cells, preferred_element_type=F32)
    size = both.shape[0] // 2
    both = both[:size] + both[size:]
    levels = own.shape[2]
    return [both[:, n * levels : (n + 1) * levels] for n in range(len(members))]


def forward_kernel(cols, own, south, north, west, east, band, vertical, ensemble, keep, send, square):
    members = own.shape[0]
    size = ROWS * cols
    blocks = own.shape[1] // size
    core = lax.axis_index("core")
    total = jnp.zeros((8, own.shape[2]), F32)
    for block in range(blocks):
        rows = slice(block * size, (block + 1) * size)
        increment = jnp.zeros((size, own.shape[2]), F32)
        for first in range(0, members, 2):
            pair = range(first, first + 2)
            for m, value in zip(pair, filtered(band, own, south, north, west, east, pair, block, cols)):
                leveled = jnp.dot(value.astype(BF), vertical[...], preferred_element_type=F32)
                increment = increment + ensemble[m, rows, :].astype(F32) * leveled
                c = own[m, rows, :].astype(F32)
                total = total + jnp.sum((c * c).reshape(size // 8, 8, own.shape[2]), axis=0)
        half, at = block // (blocks // 2), block % (blocks // 2)
        place = slice(at * size, (at + 1) * size)
        increment = increment.astype(BF)

        @pl.when(core == half)
        def _():
            keep[place, :] = increment

        @pl.when(core != half)
        def _():
            send[place, :] = increment

    square[...] = total


def forward(own, south, north, west, east, band, vertical, ensemble, cols):
    members, cells, levels = own.shape
    half = jax.ShapeDtypeStruct((cells // 2, levels), BF)
    return pl.pallas_call(
        functools.partial(forward_kernel, cols),
        out_shape=(half, half, jax.ShapeDtypeStruct((8, levels), F32)),
        in_specs=[VMEM] * 8,
        out_specs=(VMEM,) * 3,
        compiler_params=params(),
        cost_estimate=cost(4_000_000_000, 6_000_000),
        name="forward",
    )(own, south, north, west, east, band, vertical, ensemble)


def level_kernel(weighted, ensemble, vertical, adjoint):
    size = 256
    for start in range(0, weighted.shape[0], size):
        rows = slice(start, start + size)
        w = weighted[rows, :].astype(F32)
        for m in range(ensemble.shape[0]):
            part = (ensemble[m, rows, :].astype(F32) * w).astype(BF)
            adjoint[m, rows, :] = lax.dot_general(
                part, vertical[...], (((1,), (1,)), ((), ())), preferred_element_type=F32
            ).astype(BF)


def level(weighted, ensemble, vertical):
    return pl.pallas_call(
        level_kernel,
        out_shape=jax.ShapeDtypeStruct(ensemble.shape, BF),
        in_specs=[VMEM] * 3,
        out_specs=VMEM,
        compiler_params=params(),
        cost_estimate=cost(300_000_000, 4_500_000),
        name="level",
    )(weighted, ensemble, vertical)


def backward_kernel(cols, own, south, north, west, east, band, control, hessian):
    members = own.shape[0]
    size = ROWS * cols
    for block in range(own.shape[1] // size):
        rows = slice(block * size, (block + 1) * size)
        for first in range(0, members, 2):
            pair = range(first, first + 2)
            for m, value in zip(pair, filtered(band, own, south, north, west, east, pair, block, cols)):
                hessian[m, rows, :] = control[m, rows, :].astype(F32) + value


def backward(own, south, north, west, east, band, control, cols):
    return pl.pallas_call(
        functools.partial(backward_kernel, cols),
        out_shape=jax.ShapeDtypeStruct(control.shape, F32),
        in_specs=[VMEM] * 7,
        out_specs=VMEM,
        compiler_params=params(),
        cost_estimate=cost(3_500_000_000, 9_000_000),
        name="backward",
    )(own, south, north, west, east, band, control)


def halo(tile):
    members, rows, cols, levels = tile.shape
    south = lax.ppermute(tile[:, rows - HALO :], "lat", line("lat", 1))
    north = lax.ppermute(tile[:, :HALO], "lat", line("lat", -1))

    def side(lo):
        cut = slice(lo, lo + HALO)
        return jnp.concatenate([south[:, :, cut], tile[:, :, cut], north[:, :, cut]], axis=1).reshape(
            members, (rows + 2 * HALO) * HALO, levels
        )

    west = lax.ppermute(side(cols - HALO), "lon", ring("lon", 1))
    east = lax.ppermute(side(0), "lon", ring("lon", -1))
    flat = (members, HALO * cols, levels)
    return south.reshape(flat), north.reshape(flat), west, east


def split3(value):
    parts = []
    for _ in range(3):
        part = lax.reduce_precision(value, 8, 7)
        parts.append(part.astype(BF))
        value = value - part
    return jnp.concatenate(parts + [jnp.zeros((13, value.shape[1]), BF)], axis=0)


def join3(rows):
    rows = rows.astype(F32)
    return (rows[0:1] + rows[1:2]) + rows[2:3]


def total_of_four(value, axis):
    n = lax.axis_size(axis)
    value = value + lax.ppermute(value, axis, [(i, i ^ 1) for i in range(n)])
    return value + lax.ppermute(value, axis, [(i, n - 1 - i) for i in range(n)])


def per_device(control, ensemble, precision, lat_taps, lon_taps, vertical):
    members, tile_rows, tile_cols, levels = control.shape
    cells = tile_rows * tile_cols
    entries = control.size * lax.axis_size(MEM) * lax.axis_size("lat") * lax.axis_size("lon")
    core, x = lax.axis_index("core"), lax.axis_index("x")
    flat = (members, cells, levels)
    own, spread = control.reshape(flat), ensemble.reshape(flat)
    share = cells // 8

    south, north, west, east = halo(control)
    band, band_back = bands(lat_taps, lon_taps, tile_cols)
    keep, send, square = forward(own, south, north, west, east, band, vertical, spread, tile_cols)

    got = lax.ppermute(send, "core", ring("core", 1))
    half = (keep.astype(F32) + got.astype(F32)).astype(BF).reshape(4, share, levels)

    def pick(step):
        return lax.dynamic_index_in_dim(half, (x + step) % 4, 0, keepdims=False)

    one, three, two = [lax.ppermute(pick(k), "x", ring("x", k)) for k in (1, 3, 2)]
    part = ((one.astype(F32) + three.astype(F32)) + (pick(0).astype(F32) + two.astype(F32))).astype(BF)
    square = jnp.sum(square, axis=0, keepdims=True)
    message = jnp.concatenate([part, split3(square)], axis=0)
    other = lax.ppermute(message, "zh", ring("zh", 1))
    increment = message[:share].astype(F32) + other[:share].astype(F32)
    squares = join3(message[share:]) + join3(other[share:])
    start = (core * 4 + x) * share
    mine = lax.dynamic_slice_in_dim(precision.reshape(cells, levels), start, share, 0)
    weighted = mine * increment
    inner = squares + jnp.sum(weighted * increment, axis=0, keepdims=True)

    message = jnp.concatenate([weighted.astype(BF), split3(inner)], axis=0)
    three, two, one = [lax.ppermute(message, "x", ring("x", k)) for k in (3, 2, 1)]
    inner = (join3(one[share:]) + join3(three[share:])) + (join3(message[share:]) + join3(two[share:]))
    shares = [v[:share] for v in (message, three, two, one)]
    shares = lax.dynamic_slice_in_dim(jnp.stack(shares + shares), (4 - x) % 4, 4, 0).reshape(cells // 2, levels)
    message = jnp.concatenate([shares, split3(inner)], axis=0)
    other = lax.ppermute(message, "core", ring("core", 1))
    inner = join3(message[cells // 2 :]) + join3(other[cells // 2 :])
    first = jnp.where(core == 0, message[: cells // 2], other[: cells // 2])
    second = jnp.where(core == 0, other[: cells // 2], message[: cells // 2])
    weighted = jnp.concatenate([first, second], axis=0)

    adjoint = level(weighted, spread, vertical)
    south, north, west, east = halo(adjoint.reshape(control.shape))
    inner = total_of_four(total_of_four(inner, "lat"), "lon")
    hessian = backward(adjoint, south, north, west, east, band_back, own, tile_cols)
    return hessian.reshape(control.shape), jnp.sum(inner) / entries


def solution(mesh):
    split = Mesh(
        mesh.devices.reshape(2, 4, 2, mesh.shape["lat"], mesh.shape["lon"]),
        ("zh", "x", "core", "lat", "lon"),
    )
    return jax.shard_map(
        per_device,
        mesh=split,
        in_specs=(
            P(MEM, "lat", "lon", None),
            P(MEM, "lat", "lon", None),
            P("lat", "lon", None),
            P(),
            P(),
            P(),
        ),
        out_specs=(P(MEM, "lat", "lon", None), P()),
        check_vma=False,
    )
```

```python
import functools

import jax
import jax.numpy as jnp
from jax import lax
from jax.experimental import pallas as pl
from jax.experimental.pallas import tpu as pltpu
from jax.sharding import Mesh
from jax.sharding import PartitionSpec as P

MEM = ("zh", "x", "core")
BF = jnp.bfloat16
F32 = jnp.float32
HALO = 4
TAPS = 9
ROWS = 8
VMEM = pl.BlockSpec(memory_space=pltpu.VMEM)
SMEM = pl.BlockSpec(memory_space=pltpu.SMEM)
HBM = pl.BlockSpec(memory_space=pltpu.HBM)
EXTRA = 16


def swap(axis, bits):
    return [(i, i ^ bits) for i in range(lax.axis_size(axis))]


def params(mib=12):
    return pltpu.CompilerParams(vmem_limit_bytes=mib * 2**20)


def cost(flops, size):
    return pl.CostEstimate(flops=flops, bytes_accessed=size, transcendentals=0)


def is_odd(axis):
    return lax.rem(lax.axis_index(axis), 2) == 1


def taps_at(index, taps, flip):
    value = jnp.zeros(index.shape, F32)
    for t in range(TAPS):
        value = jnp.where(index == t, taps[TAPS - 1 - t if flip else t], value)
    return value


def put_halves(out, row, value):
    high = value.astype(BF)
    size = value.shape[0]
    out[row : row + size, :] = high
    out[row + out.shape[0] // 2 : row + out.shape[0] // 2 + size, :] = (value - high.astype(F32)).astype(BF)


def band_kernel(cols, lat_taps, lon_taps, centre, centre_back, side, side_back):
    k = lax.broadcasted_iota(jnp.int32, (cols, centre.shape[1]), 1)
    j = lax.broadcasted_iota(jnp.int32, (cols, centre.shape[1]), 0)
    row, shift = k // cols, k % cols - j + HALO
    k2 = lax.broadcasted_iota(jnp.int32, (16, side.shape[1]), 1)
    j2 = lax.broadcasted_iota(jnp.int32, (16, side.shape[1]), 0)
    half = side.shape[1] // 2
    in_west = k2 < half
    row2 = jnp.where(in_west, k2, k2 - half) // HALO
    column = k2 % HALO
    target = jnp.where(j2 < 8, j2, j2 + cols - 16)
    shift2 = jnp.where(in_west, column, column + cols + HALO) - target
    for flip, wide, narrow in ((False, centre, side), (True, centre_back, side_back)):
        across = taps_at(shift, lon_taps, flip)
        across2 = taps_at(shift2, lon_taps, flip)
        for i in range(ROWS):
            put_halves(wide, i * cols, taps_at(row - i, lat_taps, flip) * across)
            put_halves(narrow, i * 16, taps_at(row2 - i, lat_taps, flip) * across2)


def bands(lat_taps, lon_taps, cols):
    span = ROWS + 2 * HALO
    wide = jax.ShapeDtypeStruct((2 * ROWS * cols, span * cols), BF)
    narrow = jax.ShapeDtypeStruct((2 * ROWS * 16, 2 * span * HALO), BF)
    return pl.pallas_call(
        functools.partial(band_kernel, cols),
        out_shape=(wide, wide, narrow, narrow),
        in_specs=[SMEM, SMEM],
        out_specs=(VMEM,) * 4,
        compiler_params=params(),
        cost_estimate=cost(2_000_000, 1_200_000),
        name="bands",
    )(lat_taps, lon_taps)


def south_north(first, second, rows):
    odd = is_odd("lat")
    at = lax.axis_index("lat")
    zero = jnp.zeros((rows.stop - rows.start, first.shape[1]), BF)
    one, two = first[rows, :], second[rows, :]
    south = jnp.where(at == 0, zero, jnp.where(odd, one, two))
    north = jnp.where(at == lax.axis_size("lat") - 1, zero, jnp.where(odd, two, one))
    return south, north


def centre_kernel(cols, with_square, own, first, second, band, out, *square):
    members, cells, levels = own.shape
    size, edge = ROWS * cols, HALO * cols
    total = jnp.zeros((8, levels), F32)
    for start in range(0, members, 2):
        pair = (start, start + 1)
        edges = [south_north(first, second, slice(m * edge, (m + 1) * edge)) for m in pair]
        for row in range(0, cells, size):
            lo, hi = max(row - edge, 0), min(row + size + edge, cells)
            parts = []
            for m, (south, north) in zip(pair, edges):
                part = [south] if row == 0 else []
                part.append(own[m, lo:hi, :])
                if row + size == cells:
                    part.append(north)
                parts.append(jnp.concatenate(part, axis=0) if len(part) > 1 else part[0])
                if with_square:
                    c = own[m, row : row + size, :].astype(F32)
                    total = total + jnp.sum((c * c).reshape(size // 8, 8, levels), axis=0)
            both = jnp.dot(band[...], jnp.concatenate(parts, axis=1), preferred_element_type=F32)
            both = both[:size] + both[size:]
            for n, m in enumerate(pair):
                out[m, row : row + size, :] = both[:, n * levels : (n + 1) * levels]
    if with_square:
        square[0][...] = total


def centre(own, first, second, band, cols, with_square):
    members, cells, levels = own.shape
    shapes = [jax.ShapeDtypeStruct(own.shape, F32)]
    if with_square:
        shapes.append(jax.ShapeDtypeStruct((8, levels), F32))
    return pl.pallas_call(
        functools.partial(centre_kernel, cols, with_square),
        out_shape=shapes,
        in_specs=[VMEM] * 4,
        out_specs=[VMEM] * len(shapes),
        compiler_params=params(),
        cost_estimate=cost(3_000_000_000, 7_000_000),
        name="centre_forward" if with_square else "centre_back",
    )(own, first, second, band)


def side_rows(cells, cols):
    return (cells // cols + 2 * HALO) * HALO


def sides(band, first, second, pair, row, cols, stride):
    odd = is_odd("lon")
    count = (ROWS + 2 * HALO) * HALO
    parts = []
    for m in pair:
        at = slice(m * stride + row // cols * HALO, m * stride + row // cols * HALO + count)
        one, two = first[at, :], second[at, :]
        parts.append(jnp.concatenate([jnp.where(odd, one, two), jnp.where(odd, two, one)], axis=0))
    both = jnp.dot(band[...], jnp.concatenate(parts, axis=1), preferred_element_type=F32)
    size = both.shape[0] // 2
    both = both[:size] + both[size:]
    levels = both.shape[1] // len(pair)
    return [both[:, n * levels : (n + 1) * levels] for n in range(len(pair))]


def with_sides(value, side, cols):
    levels = value.shape[1]
    value = value.reshape(ROWS, cols, levels)
    side = side.reshape(ROWS, 16, levels)
    return jnp.concatenate(
        [value[:, :8] + side[:, :8], value[:, 8 : cols - 8], value[:, cols - 8 :] + side[:, 8:]], axis=1
    ).reshape(ROWS * cols, levels)


def forward_kernel(cols, inner, first, second, band, vertical, ensemble, keep, send):
    members, cells, levels = inner.shape
    size = ROWS * cols
    blocks = cells // size
    core = lax.axis_index("core")
    for block in range(blocks):
        row = block * size
        rows = slice(row, row + size)
        increment = jnp.zeros((size, levels), F32)
        for start in range(0, members, 2):
            pair = (start, start + 1)
            for m, side in zip(pair, sides(band, first, second, pair, row, cols, side_rows(cells, cols))):
                smoothed = with_sides(inner[m, rows, :], side, cols).astype(BF)
                leveled = jnp.dot(smoothed, vertical[...], preferred_element_type=F32)
                increment = increment + ensemble[m, rows, :].astype(F32) * leveled
        half, at = block // (blocks // 2), block % (blocks // 2)
        place = slice(at * size, (at + 1) * size)
        increment = increment.astype(BF)

        @pl.when(core == half)
        def _():
            keep[place, :] = increment

        @pl.when(core != half)
        def _():
            send[place, :] = increment


def forward(inner, first, second, band, vertical, ensemble, cols):
    members, cells, levels = inner.shape
    half = jax.ShapeDtypeStruct((cells // 2, levels), BF)
    return pl.pallas_call(
        functools.partial(forward_kernel, cols),
        out_shape=(half, half),
        in_specs=[VMEM] * 6,
        out_specs=(VMEM,) * 2,
        compiler_params=params(),
        cost_estimate=cost(1_500_000_000, 7_000_000),
        name="forward",
    )(inner, first, second, band, vertical, ensemble)


def put_sums(message, sums):
    row = lax.broadcasted_iota(jnp.int32, (EXTRA, sums.shape[1]), 0)
    parts = jnp.zeros(row.shape, F32)
    for n in range(3):
        part = sums.astype(BF).astype(F32)
        parts = jnp.where(row == n, part, parts)
        sums = sums - part
    message[message.shape[0] - EXTRA :, :] = parts.astype(BF)


def get_sums(message):
    return jnp.sum(message[message.shape[0] - EXTRA :, :].astype(F32), axis=0, keepdims=True)


def share_of(bits):
    return lax.axis_index("x") ^ bits


def call(kernel, name, shapes, inputs, in_specs=None, scratch=(), flops=1_000_000, size=1_000_000, out_specs=None, mib=12):
    return pl.pallas_call(
        kernel,
        out_shape=tuple(shapes),
        in_specs=in_specs or [VMEM] * len(inputs),
        out_specs=out_specs or (VMEM,) * len(shapes),
        scratch_shapes=scratch,
        compiler_params=params(mib),
        cost_estimate=cost(flops, size),
        name=name,
    )(*inputs)


def edges_kernel(edge, share, control, precision, first, second, mine, done):
    members, cells, _ = control.shape
    start = jnp.where(is_odd("lat"), 0, (cells - edge) // 128) * 128
    copies = []
    for out, at in ((first, start), (second, cells - edge - start)):
        at = pl.multiple_of(at, 128)
        for m in range(members):
            copies.append((control.at[m, pl.ds(at, edge), :], out.at[pl.ds(m * edge, edge), :]))
    at = pl.multiple_of((lax.axis_index("core") * 4 + lax.axis_index("x")) * share, share)
    copies.append((precision.at[pl.ds(at, share), :], mine))
    copies = [pltpu.make_async_copy(*pair, done.at[n]) for n, pair in enumerate(copies)]
    for copy in copies:
        copy.start()
    for copy in copies:
        copy.wait()


def edges(control, precision, edge):
    members, cells, levels = control.shape
    message = jax.ShapeDtypeStruct((members * edge, levels), BF)
    share = cells // 8
    return call(
        functools.partial(edges_kernel, edge, share),
        "edges",
        (message, message, jax.ShapeDtypeStruct((share, levels), F32)),
        (control, precision),
        in_specs=[HBM, HBM],
        scratch=(pltpu.SemaphoreType.DMA((2 * members + 1,)),),
        mib=56,
    )


def picker(lat_rows, cols):
    count = lat_rows * HALO
    row = lax.broadcasted_iota(jnp.int32, (2 * count, lat_rows * cols), 0)
    cell = lax.broadcasted_iota(jnp.int32, (2 * count, lat_rows * cols), 1)
    low = row < count
    at = jnp.where(low, row, row - count)
    wanted = at // HALO * cols + at % HALO + jnp.where(low, 0, cols - HALO)
    return jnp.where(cell == wanted, 1.0, 0.0).astype(BF)


def lon_kernel(cols, tile, first, second, *refs):
    members, cells, levels = tile.shape
    if len(refs) > 2:
        sums, far, west_out, east_out, total = refs
        value = (sums[0:1, :] + get_sums(first)) + (far[0:1, :] + get_sums(second))
        total[...] = jnp.broadcast_to(value, total.shape)
        put_sums(west_out, value)
        put_sums(east_out, value)
    else:
        west_out, east_out = refs
    odd = is_odd("lon")
    edge, block = HALO * cols, 16
    stride = side_rows(cells, cols)
    narrow, wide = picker(HALO, cols), picker(block, cols)

    def put(pick, parts, pair, at):
        got = jnp.dot(pick, jnp.concatenate(parts, axis=1), preferred_element_type=F32).astype(BF)
        half = got.shape[0] // 2
        low, high = got[:half], got[half:]
        one, two = jnp.where(odd, low, high), jnp.where(odd, high, low)
        for n, m in enumerate(pair):
            lanes = slice(n * levels, (n + 1) * levels)
            place = slice(m * stride + at, m * stride + at + half)
            west_out[place, :] = one[:, lanes]
            east_out[place, :] = two[:, lanes]

    for start in range(0, members, 2):
        pair = (start, start + 1)
        ends = [south_north(first, second, slice(m * edge, (m + 1) * edge)) for m in pair]
        put(narrow, [south for south, _ in ends], pair, 0)
        for row in range(0, cells, block * cols):
            put(wide, [tile[m, row : row + block * cols, :] for m in pair], pair, row // cols * HALO + HALO * HALO)
        put(narrow, [north for _, north in ends], pair, stride - HALO * HALO)


def lon_messages(tile, first, second, cols, *sums):
    members, cells, levels = tile.shape
    extra = EXTRA if sums else 0
    message = jax.ShapeDtypeStruct((members * side_rows(cells, cols) + extra, levels), BF)
    shapes = [message, message] + [jax.ShapeDtypeStruct(v.shape, F32) for v in sums[:1]]
    return call(
        functools.partial(lon_kernel, cols),
        "lon_messages",
        shapes,
        (tile, first, second, *sums),
        flops=200_000_000,
        size=3_000_000,
    )


def shares_kernel(keep, got, *shares):
    size = shares[0].shape[0]
    for bits, out in enumerate(shares):
        rows = pl.ds(pl.multiple_of(share_of(bits) * size, size), size)
        out[...] = (keep[rows, :].astype(F32) + got[rows, :].astype(F32)).astype(BF)


def part_kernel(zero, one, two, three, square, message):
    size = zero.shape[0]
    message[:size, :] = (
        (zero[...].astype(F32) + one[...].astype(F32)) + (two[...].astype(F32) + three[...].astype(F32))
    ).astype(BF)
    put_sums(message, jnp.sum(square[...], axis=0, keepdims=True))


def weight_kernel(message, other, mine, out):
    size = mine.shape[0]
    increment = message[:size, :].astype(F32) + other[:size, :].astype(F32)
    weighted = mine[...] * increment
    out[:size, :] = weighted.astype(BF)
    put_sums(out, (get_sums(message) + get_sums(other)) + jnp.sum(weighted * increment, axis=0, keepdims=True))


def gather_kernel(zero, one, two, three, out):
    size = zero.shape[0] - EXTRA
    for n, ref in enumerate((zero, one, two, three)):
        out[n * size : (n + 1) * size, :] = ref[:size, :]
    put_sums(out, (get_sums(zero) + get_sums(one)) + (get_sums(two) + get_sums(three)))


def level_kernel(mine, other, ensemble, vertical, adjoint, first, second, sums):
    members, cells, levels = adjoint.shape
    share = cells // 8
    edge = (first.shape[0] - EXTRA) // members
    core = lax.axis_index("core")
    for which, half in ((mine, core), (other, 1 - core)):
        for k in range(4):
            rows = pl.ds(pl.multiple_of((half * 4 + share_of(k)) * share, share), share)
            w = which[k * share : (k + 1) * share, :].astype(F32)
            for m in range(members):
                part = (ensemble[m, rows, :].astype(F32) * w).astype(BF)
                adjoint[m, rows, :] = lax.dot_general(
                    part, vertical[...], (((1,), (1,)), ((), ())), preferred_element_type=F32
                ).astype(BF)
    odd = is_odd("lat")
    for m in range(members):
        low, high = adjoint[m, :edge, :], adjoint[m, cells - edge :, :]
        first[m * edge : (m + 1) * edge, :] = jnp.where(odd, low, high)
        second[m * edge : (m + 1) * edge, :] = jnp.where(odd, high, low)
    value = get_sums(mine) + get_sums(other)
    put_sums(first, value)
    put_sums(second, value)
    sums[...] = jnp.broadcast_to(value, sums.shape)


def backward_kernel(cols, entries, inner, first, second, band, control, sums, far, hessian, curvature, result, done):
    members, cells, levels = inner.shape
    size = ROWS * cols
    copies = []
    for start in range(0, members, 2):
        pair = (start, start + 1)
        for row in range(0, cells, size):
            rows = slice(row, row + size)
            for m, side in zip(pair, sides(band, first, second, pair, row, cols, side_rows(cells, cols))):
                result[m, rows, :] = control[m, rows, :].astype(F32) + with_sides(inner[m, rows, :], side, cols)
            if (row + size) % (cells // 4) == 0:
                for m in pair:
                    part = pl.ds(row + size - cells // 4, cells // 4)
                    copy = pltpu.make_async_copy(
                        result.at[m, part, :], hessian.at[m, part, :], done.at[len(copies)]
                    )
                    copy.start()
                    copies.append(copy)
    value = (sums[0:1, :] + get_sums(first)) + (far[0:1, :] + get_sums(second))
    curvature[0, 0] = jnp.sum(value) / entries
    for copy in copies:
        copy.wait()


def exchange(first, second, axis):
    return lax.ppermute(first, axis, swap(axis, 1)), lax.ppermute(second, axis, swap(axis, 3))


def per_device(control, ensemble, precision, lat_taps, lon_taps, vertical):
    members, tile_rows, cols, levels = control.shape
    cells = tile_rows * cols
    entries = control.size * lax.axis_size(MEM) * lax.axis_size("lat") * lax.axis_size("lon")
    own, spread = control.reshape(members, cells, levels), ensemble.reshape(members, cells, levels)
    share = cells // 8
    row = jax.ShapeDtypeStruct((8, levels), F32)

    def rows(count):
        return jax.ShapeDtypeStruct((count, levels), BF)

    first, second, mine = edges(own, precision.reshape(cells, levels), HALO * cols)
    one, two = exchange(first, second, "lat")
    west, east = exchange(*lon_messages(own, one, two, cols), "lon")
    band, band_back, band_side, band_side_back = bands(lat_taps, lon_taps, cols)
    inner, square = centre(own, one, two, band, cols, True)
    keep, send = forward(inner, west, east, band_side, vertical, spread, cols)

    got = lax.ppermute(send, "core", swap("core", 1))
    zero, one, two, three = call(shares_kernel, "shares", [rows(share)] * 4, (keep, got))
    two, one, three = [lax.ppermute(v, "x", swap("x", k)) for v, k in ((two, 2), (one, 1), (three, 3))]
    (message,) = call(part_kernel, "part", [rows(share + EXTRA)], (zero, one, two, three, square))
    other = lax.ppermute(message, "zh", swap("zh", 1))
    (zero,) = call(weight_kernel, "weight", [rows(share + EXTRA)], (message, other, mine))
    two, one, three = [lax.ppermute(zero, "x", swap("x", k)) for k in (2, 1, 3)]
    (message,) = call(gather_kernel, "gather", [rows(cells // 2 + EXTRA)], (zero, one, two, three))
    other = lax.ppermute(message, "core", swap("core", 1))

    edge = rows(members * HALO * cols + EXTRA)
    adjoint, first, second, sums = call(
        level_kernel,
        "level",
        [jax.ShapeDtypeStruct(own.shape, BF), edge, edge, row],
        (message, other, spread, vertical),
        flops=300_000_000,
        size=4_500_000,
    )
    one, two = exchange(first, second, "lat")
    far = lax.ppermute(sums, "lat", swap("lat", 2))
    west, east, sums = lon_messages(adjoint, one, two, cols, sums, far)
    west, east = exchange(west, east, "lon")
    far = lax.ppermute(sums, "lon", swap("lon", 2))
    inner = centre(adjoint, one, two, band_back, cols, False)[0]
    hessian, curvature = call(
        functools.partial(backward_kernel, cols, entries),
        "backward",
        [jax.ShapeDtypeStruct(own.shape, F32), jax.ShapeDtypeStruct((1, 1), F32)],
        (inner, west, east, band_side_back, own, sums, far),
        scratch=(pltpu.VMEM(own.shape, F32), pltpu.SemaphoreType.DMA((4 * members,))),
        out_specs=(pl.BlockSpec(memory_space=pl.ANY), SMEM),
        flops=1_000_000_000,
        size=9_000_000,
    )
    return hessian.reshape(control.shape), curvature.reshape(())


def solution(mesh):
    split = Mesh(
        mesh.devices.reshape(2, 4, 2, mesh.shape["lat"], mesh.shape["lon"]),
        ("zh", "x", "core", "lat", "lon"),
    )
    return jax.shard_map(
        per_device,
        mesh=split,
        in_specs=(
            P(MEM, "lat", "lon", None),
            P(MEM, "lat", "lon", None),
            P("lat", "lon", None),
            P(),
            P(),
            P(),
        ),
        out_specs=(P(MEM, "lat", "lon", None), P()),
        check_vma=False,
    )
```

```python
import functools

import jax
import jax.numpy as jnp
from jax import lax
from jax.experimental import pallas as pl
from jax.experimental.pallas import tpu as pltpu
from jax.sharding import Mesh
from jax.sharding import PartitionSpec as P

MEM = ("zh", "x", "core")
BF = jnp.bfloat16
F32 = jnp.float32
HALO = 4
TAPS = 9
ROWS = 8
VMEM = pl.BlockSpec(memory_space=pltpu.VMEM)
SMEM = pl.BlockSpec(memory_space=pltpu.SMEM)
EXTRA = 16


def swap(axis, bits):
    return [(i, i ^ bits) for i in range(lax.axis_size(axis))]


def params(mib=12):
    return pltpu.CompilerParams(vmem_limit_bytes=mib * 2**20)


def cost(flops, size):
    return pl.CostEstimate(flops=flops, bytes_accessed=size, transcendentals=0)


def is_odd(axis):
    return lax.rem(lax.axis_index(axis), 2) == 1


def taps_at(index, taps, flip):
    value = jnp.zeros(index.shape, F32)
    for t in range(TAPS):
        value = jnp.where(index == t, taps[TAPS - 1 - t if flip else t], value)
    return value


def put_halves(out, row, value):
    high = value.astype(BF)
    size = value.shape[0]
    out[row : row + size, :] = high
    out[row + out.shape[0] // 2 : row + out.shape[0] // 2 + size, :] = (value - high.astype(F32)).astype(BF)


def band_kernel(cols, lat_taps, lon_taps, centre, centre_back, side, side_back):
    k = lax.broadcasted_iota(jnp.int32, (cols, centre.shape[1]), 1)
    j = lax.broadcasted_iota(jnp.int32, (cols, centre.shape[1]), 0)
    row, shift = k // cols, k % cols - j + HALO
    k2 = lax.broadcasted_iota(jnp.int32, (16, side.shape[1]), 1)
    j2 = lax.broadcasted_iota(jnp.int32, (16, side.shape[1]), 0)
    half = side.shape[1] // 2
    in_west = k2 < half
    row2 = jnp.where(in_west, k2, k2 - half) // HALO
    column = k2 % HALO
    target = jnp.where(j2 < 8, j2, j2 + cols - 16)
    shift2 = jnp.where(in_west, column, column + cols + HALO) - target
    for flip, wide, narrow in ((False, centre, side), (True, centre_back, side_back)):
        across = taps_at(shift, lon_taps, flip)
        across2 = taps_at(shift2, lon_taps, flip)
        for i in range(ROWS):
            put_halves(wide, i * cols, taps_at(row - i, lat_taps, flip) * across)
            put_halves(narrow, i * 16, taps_at(row2 - i, lat_taps, flip) * across2)


def bands(lat_taps, lon_taps, cols):
    span = ROWS + 2 * HALO
    wide = jax.ShapeDtypeStruct((2 * ROWS * cols, span * cols), BF)
    narrow = jax.ShapeDtypeStruct((2 * ROWS * 16, 2 * span * HALO), BF)
    return pl.pallas_call(
        functools.partial(band_kernel, cols),
        out_shape=(wide, wide, narrow, narrow),
        in_specs=[SMEM, SMEM],
        out_specs=(VMEM,) * 4,
        compiler_params=params(),
        cost_estimate=cost(2_000_000, 1_200_000),
        name="bands",
    )(lat_taps, lon_taps)


def south_north(first, second, rows):
    odd = is_odd("lat")
    at = lax.axis_index("lat")
    zero = jnp.zeros((rows.stop - rows.start, first.shape[1]), BF)
    one, two = first[rows, :], second[rows, :]
    south = jnp.where(at == 0, zero, jnp.where(odd, one, two))
    north = jnp.where(at == lax.axis_size("lat") - 1, zero, jnp.where(odd, two, one))
    return south, north


def centre_kernel(cols, with_square, own, first, second, band, out, *square):
    members, cells, levels = own.shape
    size, edge = ROWS * cols, HALO * cols
    total = jnp.zeros((8, levels), F32)
    for start in range(0, members, 2):
        pair = (start, start + 1)
        edges = [south_north(first, second, slice(m * edge, (m + 1) * edge)) for m in pair]
        for row in range(0, cells, size):
            lo, hi = max(row - edge, 0), min(row + size + edge, cells)
            parts = []
            for m, (south, north) in zip(pair, edges):
                part = [south] if row == 0 else []
                part.append(own[m, lo:hi, :])
                if row + size == cells:
                    part.append(north)
                parts.append(jnp.concatenate(part, axis=0) if len(part) > 1 else part[0])
                if with_square:
                    c = own[m, row : row + size, :].astype(F32)
                    total = total + jnp.sum((c * c).reshape(size // 8, 8, levels), axis=0)
            both = jnp.dot(band[...], jnp.concatenate(parts, axis=1), preferred_element_type=F32)
            both = both[:size] + both[size:]
            for n, m in enumerate(pair):
                out[m, row : row + size, :] = both[:, n * levels : (n + 1) * levels]
    if with_square:
        square[0][...] = total


def centre(own, first, second, band, cols, with_square):
    members, cells, levels = own.shape
    shapes = [jax.ShapeDtypeStruct(own.shape, F32)]
    if with_square:
        shapes.append(jax.ShapeDtypeStruct((8, levels), F32))
    return pl.pallas_call(
        functools.partial(centre_kernel, cols, with_square),
        out_shape=shapes,
        in_specs=[VMEM] * 4,
        out_specs=[VMEM] * len(shapes),
        compiler_params=params(),
        cost_estimate=cost(3_000_000_000, 7_000_000),
        name="centre_forward" if with_square else "centre_back",
    )(own, first, second, band)


def beside(own, corner, member, row, cols, cells):
    length = cells // cols * HALO
    edge = HALO * HALO
    lo = member * length + row // cols * HALO - edge
    hi = lo + (ROWS + 2 * HALO) * HALO
    parts = [own[max(lo, member * length) : min(hi, (member + 1) * length), :]]
    if row == 0:
        parts.insert(0, corner[2 * member * edge : (2 * member + 1) * edge, :])
    if row + ROWS * cols == cells:
        parts.append(corner[(2 * member + 1) * edge : (2 * member + 2) * edge, :])
    return jnp.concatenate(parts, axis=0) if len(parts) > 1 else parts[0]


def sides(band, strips, corners, pair, row, cols, cells):
    odd = is_odd("lon")
    parts = []
    for m in pair:
        one, two = (beside(own, corner, m, row, cols, cells) for own, corner in zip(strips, corners))
        parts.append(jnp.concatenate([jnp.where(odd, one, two), jnp.where(odd, two, one)], axis=0))
    both = jnp.dot(band[...], jnp.concatenate(parts, axis=1), preferred_element_type=F32)
    size = both.shape[0] // 2
    both = both[:size] + both[size:]
    levels = both.shape[1] // len(pair)
    return [both[:, n * levels : (n + 1) * levels] for n in range(len(pair))]


def with_sides(value, side, cols):
    levels = value.shape[1]
    value = value.reshape(ROWS, cols, levels)
    side = side.reshape(ROWS, 16, levels)
    return jnp.concatenate(
        [value[:, :8] + side[:, :8], value[:, 8 : cols - 8], value[:, cols - 8 :] + side[:, 8:]], axis=1
    ).reshape(ROWS * cols, levels)


def forward_kernel(cols, inner, first, second, first_corner, second_corner, band, vertical, ensemble, keep, send):
    members, cells, levels = inner.shape
    size = ROWS * cols
    blocks = cells // size
    core = lax.axis_index("core")
    for block in range(blocks):
        row = block * size
        rows = slice(row, row + size)
        increment = jnp.zeros((size, levels), F32)
        for start in range(0, members, 2):
            pair = (start, start + 1)
            for m, side in zip(pair, sides(band, (first, second), (first_corner, second_corner), pair, row, cols, cells)):
                smoothed = with_sides(inner[m, rows, :], side, cols).astype(BF)
                leveled = jnp.dot(smoothed, vertical[...], preferred_element_type=F32)
                increment = increment + ensemble[m, rows, :].astype(F32) * leveled
        half, at = block // (blocks // 2), block % (blocks // 2)
        place = slice(at * size, (at + 1) * size)
        increment = increment.astype(BF)

        @pl.when(core == half)
        def _():
            keep[place, :] = increment

        @pl.when(core != half)
        def _():
            send[place, :] = increment


def forward(inner, strips, corners, band, vertical, ensemble, cols):
    members, cells, levels = inner.shape
    half = jax.ShapeDtypeStruct((cells // 2, levels), BF)
    return pl.pallas_call(
        functools.partial(forward_kernel, cols),
        out_shape=(half, half),
        in_specs=[VMEM] * 8,
        out_specs=(VMEM,) * 2,
        compiler_params=params(),
        cost_estimate=cost(1_500_000_000, 7_000_000),
        name="forward",
    )(inner, *strips, *corners, band, vertical, ensemble)


def put_sums(message, sums):
    row = lax.broadcasted_iota(jnp.int32, (EXTRA, sums.shape[1]), 0)
    parts = jnp.zeros(row.shape, F32)
    for n in range(3):
        part = sums.astype(BF).astype(F32)
        parts = jnp.where(row == n, part, parts)
        sums = sums - part
    message[message.shape[0] - EXTRA :, :] = parts.astype(BF)


def get_sums(message):
    return jnp.sum(message[message.shape[0] - EXTRA :, :].astype(F32), axis=0, keepdims=True)


def share_of(bits):
    return lax.axis_index("x") ^ bits


def call(kernel, name, shapes, inputs, in_specs=None, scratch=(), flops=1_000_000, size=1_000_000, out_specs=None, mib=12):
    return pl.pallas_call(
        kernel,
        out_shape=tuple(shapes),
        in_specs=in_specs or [VMEM] * len(inputs),
        out_specs=out_specs or (VMEM,) * len(shapes),
        scratch_shapes=scratch,
        compiler_params=params(mib),
        cost_estimate=cost(flops, size),
        name=name,
    )(*inputs)


def picker(lat_rows, cols):
    count = lat_rows * HALO
    row = lax.broadcasted_iota(jnp.int32, (2 * count, lat_rows * cols), 0)
    cell = lax.broadcasted_iota(jnp.int32, (2 * count, lat_rows * cols), 1)
    low = row < count
    at = jnp.where(low, row, row - count)
    wanted = at // HALO * cols + at % HALO + jnp.where(low, 0, cols - HALO)
    return jnp.where(cell == wanted, 1.0, 0.0).astype(BF)


def put_picked(pick, parts, place, out, odd):
    got = jnp.dot(pick, jnp.concatenate(parts, axis=1), preferred_element_type=F32).astype(BF)
    half = got.shape[0] // 2
    levels = got.shape[1] // len(parts)
    low, high = got[:half], got[half:]
    for ref, value in zip(out, (jnp.where(odd, low, high), jnp.where(odd, high, low))):
        for n, at in enumerate(place):
            ref[at : at + half, :] = value[:, n * levels : (n + 1) * levels]


def strips_kernel(cols, tile, *out):
    members, cells, _ = tile.shape
    odd = is_odd("lon")
    block = 16
    pick = picker(block, cols)
    length = cells // cols * HALO
    for start in range(0, members, 2):
        pair = (start, start + 1)
        for row in range(0, cells, block * cols):
            parts = [tile[m, row : row + block * cols, :] for m in pair]
            put_picked(pick, parts, [m * length + row // cols * HALO for m in pair], out, odd)


def strips(tile, cols):
    members, cells, levels = tile.shape
    message = jax.ShapeDtypeStruct((members * (cells // cols) * HALO, levels), BF)
    return call(
        functools.partial(strips_kernel, cols), "strips", [message] * 2, (tile,), flops=300_000_000, size=3_000_000
    )


def corners_kernel(cols, members, first, second, *refs):
    if len(refs) > 2:
        sums, far, *out, total = refs
        value = (sums[0:1, :] + get_sums(first)) + (far[0:1, :] + get_sums(second))
        total[...] = jnp.broadcast_to(value, total.shape)
        for ref in out:
            put_sums(ref, value)
    else:
        out = refs
    odd = is_odd("lon")
    edge, corner = HALO * cols, HALO * HALO
    pick = picker(HALO, cols)
    for start in range(0, members, 2):
        pair = (start, start + 1)
        ends = [south_north(first, second, slice(m * edge, (m + 1) * edge)) for m in pair]
        for n in range(2):
            put_picked(pick, [end[n] for end in ends], [(2 * m + n) * corner for m in pair], out, odd)


def corners(first, second, cols, members, *sums):
    extra = EXTRA if sums else 0
    message = jax.ShapeDtypeStruct((members * 2 * HALO * HALO + extra, first.shape[1]), BF)
    shapes = [message, message] + [jax.ShapeDtypeStruct(v.shape, F32) for v in sums[:1]]
    return call(functools.partial(corners_kernel, cols, members), "corners", shapes, (first, second, *sums))


def shares_kernel(keep, got, *shares):
    size = shares[0].shape[0]
    for bits, out in enumerate(shares):
        rows = pl.ds(pl.multiple_of(share_of(bits) * size, size), size)
        out[...] = (keep[rows, :].astype(F32) + got[rows, :].astype(F32)).astype(BF)


def part_kernel(zero, one, two, three, square, message):
    size = zero.shape[0]
    message[:size, :] = (
        (zero[...].astype(F32) + one[...].astype(F32)) + (two[...].astype(F32) + three[...].astype(F32))
    ).astype(BF)
    put_sums(message, jnp.sum(square[...], axis=0, keepdims=True))


def weight_kernel(message, other, precision, out):
    size = precision.shape[0] // 8
    share = lax.axis_index("core") * 4 + lax.axis_index("x")
    mine = precision[pl.ds(pl.multiple_of(share * size, size), size), :]
    increment = message[:size, :].astype(F32) + other[:size, :].astype(F32)
    weighted = mine * increment
    out[:size, :] = weighted.astype(BF)
    put_sums(out, (get_sums(message) + get_sums(other)) + jnp.sum(weighted * increment, axis=0, keepdims=True))


def gather_kernel(zero, one, two, three, out):
    size = zero.shape[0] - EXTRA
    for n, ref in enumerate((zero, one, two, three)):
        out[n * size : (n + 1) * size, :] = ref[:size, :]
    put_sums(out, (get_sums(zero) + get_sums(one)) + (get_sums(two) + get_sums(three)))


def level_kernel(mine, other, ensemble, vertical, adjoint, first, second, sums):
    members, cells, levels = adjoint.shape
    share = cells // 8
    edge = (first.shape[0] - EXTRA) // members
    core = lax.axis_index("core")
    for which, half in ((mine, core), (other, 1 - core)):
        for k in range(4):
            rows = pl.ds(pl.multiple_of((half * 4 + share_of(k)) * share, share), share)
            w = which[k * share : (k + 1) * share, :].astype(F32)
            for m in range(members):
                part = (ensemble[m, rows, :].astype(F32) * w).astype(BF)
                adjoint[m, rows, :] = lax.dot_general(
                    part, vertical[...], (((1,), (1,)), ((), ())), preferred_element_type=F32
                ).astype(BF)
    odd = is_odd("lat")
    for m in range(members):
        low, high = adjoint[m, :edge, :], adjoint[m, cells - edge :, :]
        first[m * edge : (m + 1) * edge, :] = jnp.where(odd, low, high)
        second[m * edge : (m + 1) * edge, :] = jnp.where(odd, high, low)
    value = get_sums(mine) + get_sums(other)
    put_sums(first, value)
    put_sums(second, value)
    sums[...] = jnp.broadcast_to(value, sums.shape)


def backward_kernel(
    cols, entries, inner, first, second, first_corner, second_corner, band, control, sums, far,
    hessian, curvature, result, done,
):
    members, cells, levels = inner.shape
    size = ROWS * cols
    copies = []
    for start in range(0, members, 2):
        pair = (start, start + 1)
        for row in range(0, cells, size):
            rows = slice(row, row + size)
            for m, side in zip(pair, sides(band, (first, second), (first_corner, second_corner), pair, row, cols, cells)):
                result[m, rows, :] = control[m, rows, :].astype(F32) + with_sides(inner[m, rows, :], side, cols)
            if (row + size) % (cells // 4) == 0:
                for m in pair:
                    part = pl.ds(row + size - cells // 4, cells // 4)
                    copy = pltpu.make_async_copy(
                        result.at[m, part, :], hessian.at[m, part, :], done.at[len(copies)]
                    )
                    copy.start()
                    copies.append(copy)
    value = (sums[0:1, :] + get_sums(first_corner)) + (far[0:1, :] + get_sums(second_corner))
    curvature[0, 0] = jnp.sum(value) / entries
    for copy in copies:
        copy.wait()


def exchange(first, second, axis):
    return lax.ppermute(first, axis, swap(axis, 1)), lax.ppermute(second, axis, swap(axis, 3))


def per_device(control, ensemble, precision, lat_taps, lon_taps, vertical):
    members, tile_rows, cols, levels = control.shape
    cells = tile_rows * cols
    entries = control.size * lax.axis_size(MEM) * lax.axis_size("lat") * lax.axis_size("lon")
    own, spread = control.reshape(members, cells, levels), ensemble.reshape(members, cells, levels)
    share = cells // 8
    row = jax.ShapeDtypeStruct((8, levels), F32)

    def rows(count):
        return jax.ShapeDtypeStruct((count, levels), BF)

    odd = is_odd("lat")
    low, high = control[:, :HALO].reshape(-1, levels), control[:, tile_rows - HALO :].reshape(-1, levels)
    one, two = exchange(jnp.where(odd, low, high), jnp.where(odd, high, low), "lat")
    beside_it = exchange(*strips(own, cols), "lon")
    corner = exchange(*corners(one, two, cols, members), "lon")
    band, band_back, band_side, band_side_back = bands(lat_taps, lon_taps, cols)
    inner, square = centre(own, one, two, band, cols, True)
    keep, send = forward(inner, beside_it, corner, band_side, vertical, spread, cols)

    got = lax.ppermute(send, "core", swap("core", 1))
    zero, one, two, three = call(shares_kernel, "shares", [rows(share)] * 4, (keep, got))
    two, one, three = [lax.ppermute(v, "x", swap("x", k)) for v, k in ((two, 2), (one, 1), (three, 3))]
    (message,) = call(part_kernel, "part", [rows(share + EXTRA)], (zero, one, two, three, square))
    other = lax.ppermute(message, "zh", swap("zh", 1))
    (zero,) = call(weight_kernel, "weight", [rows(share + EXTRA)], (message, other, precision.reshape(cells, levels)))
    two, one, three = [lax.ppermute(zero, "x", swap("x", k)) for k in (2, 1, 3)]
    (message,) = call(gather_kernel, "gather", [rows(cells // 2 + EXTRA)], (zero, one, two, three))
    other = lax.ppermute(message, "core", swap("core", 1))

    edge = rows(members * HALO * cols + EXTRA)
    adjoint, first, second, sums = call(
        level_kernel,
        "level",
        [jax.ShapeDtypeStruct(own.shape, BF), edge, edge, row],
        (message, other, spread, vertical),
        flops=300_000_000,
        size=4_500_000,
    )
    one, two = exchange(first, second, "lat")
    far = lax.ppermute(sums, "lat", swap("lat", 2))
    beside_it = exchange(*strips(adjoint, cols), "lon")
    *corner, sums = corners(one, two, cols, members, sums, far)
    corner = exchange(*corner, "lon")
    far = lax.ppermute(sums, "lon", swap("lon", 2))
    inner = centre(adjoint, one, two, band_back, cols, False)[0]
    hessian, curvature = call(
        functools.partial(backward_kernel, cols, entries),
        "backward",
        [jax.ShapeDtypeStruct(own.shape, F32), jax.ShapeDtypeStruct((1, 1), F32)],
        (inner, *beside_it, *corner, band_side_back, own, sums, far),
        scratch=(pltpu.VMEM(own.shape, F32), pltpu.SemaphoreType.DMA((4 * members,))),
        out_specs=(pl.BlockSpec(memory_space=pl.ANY), SMEM),
        flops=1_000_000_000,
        size=9_000_000,
    )
    return hessian.reshape(control.shape), curvature.reshape(())


def solution(mesh):
    split = Mesh(
        mesh.devices.reshape(2, 4, 2, mesh.shape["lat"], mesh.shape["lon"]),
        ("zh", "x", "core", "lat", "lon"),
    )
    return jax.shard_map(
        per_device,
        mesh=split,
        in_specs=(
            P(MEM, "lat", "lon", None),
            P(MEM, "lat", "lon", None),
            P("lat", "lon", None),
            P(),
            P(),
            P(),
        ),
        out_specs=(P(MEM, "lat", "lon", None), P()),
        check_vma=False,
    )
```

```python
import functools

import jax
import jax.numpy as jnp
from jax import lax
from jax.experimental import pallas as pl
from jax.experimental.pallas import tpu as pltpu
from jax.sharding import Mesh
from jax.sharding import PartitionSpec as P

MEM = ("zh", "x", "core")
BF = jnp.bfloat16
F32 = jnp.float32
HALO = 4
TAPS = 9
ROWS = 8
VMEM = pl.BlockSpec(memory_space=pltpu.VMEM)
SMEM = pl.BlockSpec(memory_space=pltpu.SMEM)
EXTRA = 16


def swap(axis, bits):
    return [(i, i ^ bits) for i in range(lax.axis_size(axis))]


def params(mib=12):
    return pltpu.CompilerParams(vmem_limit_bytes=mib * 2**20)


def cost(flops, size):
    return pl.CostEstimate(flops=flops, bytes_accessed=size, transcendentals=0)


def is_odd(axis):
    return lax.rem(lax.axis_index(axis), 2) == 1


def taps_at(index, taps, flip):
    value = jnp.zeros(index.shape, F32)
    for t in range(TAPS):
        value = jnp.where(index == t, taps[TAPS - 1 - t if flip else t], value)
    return value


def put_halves(out, row, value):
    high = value.astype(BF)
    size = value.shape[0]
    out[row : row + size, :] = high
    out[row + out.shape[0] // 2 : row + out.shape[0] // 2 + size, :] = (value - high.astype(F32)).astype(BF)


def band_kernel(cols, flip, lat_taps, lon_taps, *refs):
    wide, narrow = refs[-2:]
    k = lax.broadcasted_iota(jnp.int32, (cols, wide.shape[1]), 1)
    j = lax.broadcasted_iota(jnp.int32, (cols, wide.shape[1]), 0)
    row, shift = k // cols, k % cols - j + HALO
    k2 = lax.broadcasted_iota(jnp.int32, (16, narrow.shape[1]), 1)
    j2 = lax.broadcasted_iota(jnp.int32, (16, narrow.shape[1]), 0)
    half = narrow.shape[1] // 2
    in_west = k2 < half
    row2 = jnp.where(in_west, k2, k2 - half) // HALO
    column = k2 % HALO
    target = jnp.where(j2 < 8, j2, j2 + cols - 16)
    shift2 = jnp.where(in_west, column, column + cols + HALO) - target
    across = taps_at(shift, lon_taps, flip)
    across2 = taps_at(shift2, lon_taps, flip)
    for i in range(ROWS):
        put_halves(wide, i * cols, taps_at(row - i, lat_taps, flip) * across)
        put_halves(narrow, i * 16, taps_at(row2 - i, lat_taps, flip) * across2)


def bands(lat_taps, lon_taps, cols, flip, *after):
    span = ROWS + 2 * HALO
    wide = jax.ShapeDtypeStruct((2 * ROWS * cols, span * cols), BF)
    narrow = jax.ShapeDtypeStruct((2 * ROWS * 16, 2 * span * HALO), BF)
    return pl.pallas_call(
        functools.partial(band_kernel, cols, flip),
        out_shape=(wide, narrow),
        in_specs=[SMEM, SMEM] + [VMEM] * len(after),
        out_specs=(VMEM,) * 2,
        compiler_params=params(),
        cost_estimate=cost(2_000_000, 600_000),
        name="bands_back" if flip else "bands",
    )(lat_taps, lon_taps, *after)


def south_north(first, second, rows):
    odd = is_odd("lat")
    at = lax.axis_index("lat")
    zero = jnp.zeros((rows.stop - rows.start, first.shape[1]), BF)
    one, two = first[rows, :], second[rows, :]
    south = jnp.where(at == 0, zero, jnp.where(odd, one, two))
    north = jnp.where(at == lax.axis_size("lat") - 1, zero, jnp.where(odd, two, one))
    return south, north


def centre_kernel(cols, with_square, own, first, second, band, out, *square):
    members, cells, levels = own.shape
    size, edge = ROWS * cols, HALO * cols
    total = jnp.zeros((8, levels), F32)
    for start in range(0, members, 2):
        pair = (start, start + 1)
        edges = [south_north(first, second, slice(m * edge, (m + 1) * edge)) for m in pair]
        for row in range(0, cells, size):
            lo, hi = max(row - edge, 0), min(row + size + edge, cells)
            parts = []
            for m, (south, north) in zip(pair, edges):
                part = [south] if row == 0 else []
                part.append(own[m, lo:hi, :])
                if row + size == cells:
                    part.append(north)
                parts.append(jnp.concatenate(part, axis=0) if len(part) > 1 else part[0])
                if with_square:
                    c = own[m, row : row + size, :].astype(F32)
                    total = total + jnp.sum((c * c).reshape(size // 8, 8, levels), axis=0)
            both = jnp.dot(band[...], jnp.concatenate(parts, axis=1), preferred_element_type=F32)
            both = both[:size] + both[size:]
            for n, m in enumerate(pair):
                out[m, row : row + size, :] = both[:, n * levels : (n + 1) * levels]
    if with_square:
        square[0][...] = total


def centre(own, first, second, band, cols, with_square):
    members, cells, levels = own.shape
    shapes = [jax.ShapeDtypeStruct(own.shape, F32)]
    if with_square:
        shapes.append(jax.ShapeDtypeStruct((8, levels), F32))
    return pl.pallas_call(
        functools.partial(centre_kernel, cols, with_square),
        out_shape=shapes,
        in_specs=[VMEM] * 4,
        out_specs=[VMEM] * len(shapes),
        compiler_params=params(),
        cost_estimate=cost(3_000_000_000, 7_000_000),
        name="centre_forward" if with_square else "centre_back",
    )(own, first, second, band)


def joined(strips, corners, out, members, cols, cells):
    odd = is_odd("lon")
    edge = HALO * HALO
    length = cells // cols * HALO
    for m in range(members):
        at = m * (length + 2 * edge)
        for place, refs, start, size in (
            (at, corners, 2 * m * edge, edge),
            (at + edge, strips, m * length, length),
            (at + edge + length, corners, (2 * m + 1) * edge, edge),
        ):
            one, two = (ref[start : start + size, :] for ref in refs)
            out[0][place : place + size, :] = jnp.where(odd, one, two)
            out[1][place : place + size, :] = jnp.where(odd, two, one)


def side_rows(cells, cols):
    return (cells // cols + 2 * HALO) * HALO


def sides(band, west, east, pair, block, stride):
    count = (ROWS + 2 * HALO) * HALO
    parts = []
    for m in pair:
        at = pl.ds(pl.multiple_of(m * stride + block * ROWS * HALO, 32), count)
        parts.append(jnp.concatenate([west[at, :], east[at, :]], axis=0))
    both = jnp.dot(band[...], jnp.concatenate(parts, axis=1), preferred_element_type=F32)
    size = both.shape[0] // 2
    both = both[:size] + both[size:]
    levels = both.shape[1] // len(pair)
    return [both[:, n * levels : (n + 1) * levels] for n in range(len(pair))]


def with_sides(value, side, cols):
    levels = value.shape[1]
    value = value.reshape(ROWS, cols, levels)
    side = side.reshape(ROWS, 16, levels)
    return jnp.concatenate(
        [value[:, :8] + side[:, :8], value[:, 8 : cols - 8], value[:, cols - 8 :] + side[:, 8:]], axis=1
    ).reshape(ROWS * cols, levels)


def half_forward(cols, half, inner, west, east, band, vertical, ensemble, out):
    members, cells, levels = inner.shape
    size = ROWS * cols
    count = cells // size // 2
    stride = side_rows(cells, cols)
    for n in range(count):
        block = half * count + n
        rows = pl.ds(pl.multiple_of(block * size, size), size)
        increment = jnp.zeros((size, levels), F32)
        for start in range(0, members, 2):
            pair = (start, start + 1)
            for m, side in zip(pair, sides(band, west, east, pair, block, stride)):
                smoothed = with_sides(inner[m, rows, :], side, cols).astype(BF)
                leveled = jnp.dot(smoothed, vertical[...], preferred_element_type=F32)
                increment = increment + ensemble[m, rows, :].astype(F32) * leveled
        out[n * size : (n + 1) * size, :] = increment.astype(BF)


def send_kernel(cols, inner, one, two, one_corner, two_corner, band, vertical, ensemble, out, west, east):
    members, cells, _ = inner.shape
    joined((one, two), (one_corner, two_corner), (west, east), members, cols, cells)
    half_forward(cols, 1 - lax.axis_index("core"), inner, west, east, band, vertical, ensemble, out)


def keep_kernel(cols, inner, west, east, band, vertical, ensemble, out):
    half_forward(cols, lax.axis_index("core"), inner, west, east, band, vertical, ensemble, out)


def put_sums(message, sums):
    row = lax.broadcasted_iota(jnp.int32, (EXTRA, sums.shape[1]), 0)
    parts = jnp.zeros(row.shape, F32)
    for n in range(3):
        part = sums.astype(BF).astype(F32)
        parts = jnp.where(row == n, part, parts)
        sums = sums - part
    message[message.shape[0] - EXTRA :, :] = parts.astype(BF)


def get_sums(message):
    return jnp.sum(message[message.shape[0] - EXTRA :, :].astype(F32), axis=0, keepdims=True)


def share_of(bits):
    return lax.axis_index("x") ^ bits


def call(kernel, name, shapes, inputs, in_specs=None, scratch=(), flops=1_000_000, size=1_000_000, out_specs=None, mib=12):
    return pl.pallas_call(
        kernel,
        out_shape=tuple(shapes),
        in_specs=in_specs or [VMEM] * len(inputs),
        out_specs=out_specs or (VMEM,) * len(shapes),
        scratch_shapes=scratch,
        compiler_params=params(mib),
        cost_estimate=cost(flops, size),
        name=name,
    )(*inputs)


def edges_kernel(tile, first, second):
    members, cells, _ = tile.shape
    edge = first.shape[0] // members
    odd = is_odd("lat")
    for m in range(members):
        low, high = tile[m, :edge, :], tile[m, cells - edge :, :]
        first[m * edge : (m + 1) * edge, :] = jnp.where(odd, low, high)
        second[m * edge : (m + 1) * edge, :] = jnp.where(odd, high, low)


def picker(lat_rows, cols):
    count = lat_rows * HALO
    row = lax.broadcasted_iota(jnp.int32, (2 * count, lat_rows * cols), 0)
    cell = lax.broadcasted_iota(jnp.int32, (2 * count, lat_rows * cols), 1)
    low = row < count
    at = jnp.where(low, row, row - count)
    wanted = at // HALO * cols + at % HALO + jnp.where(low, 0, cols - HALO)
    return jnp.where(cell == wanted, 1.0, 0.0).astype(BF)


def put_picked(pick, parts, place, out, odd):
    got = jnp.dot(pick, jnp.concatenate(parts, axis=1), preferred_element_type=F32).astype(BF)
    half = got.shape[0] // 2
    levels = got.shape[1] // len(parts)
    low, high = got[:half], got[half:]
    for ref, value in zip(out, (jnp.where(odd, low, high), jnp.where(odd, high, low))):
        for n, at in enumerate(place):
            ref[at : at + half, :] = value[:, n * levels : (n + 1) * levels]


def strips_kernel(cols, tile, *out):
    members, cells, _ = tile.shape
    odd = is_odd("lon")
    block = 16
    pick = picker(block, cols)
    length = cells // cols * HALO
    for start in range(0, members, 2):
        pair = (start, start + 1)
        for row in range(0, cells, block * cols):
            parts = [tile[m, row : row + block * cols, :] for m in pair]
            put_picked(pick, parts, [m * length + row // cols * HALO for m in pair], out, odd)


def strips(tile, cols):
    members, cells, levels = tile.shape
    message = jax.ShapeDtypeStruct((members * (cells // cols) * HALO, levels), BF)
    return call(
        functools.partial(strips_kernel, cols), "strips", [message] * 2, (tile,), flops=300_000_000, size=3_000_000
    )


def corners_kernel(cols, members, first, second, *refs):
    if len(refs) > 2:
        sums, far, *out, total = refs
        value = (sums[0:1, :] + get_sums(first)) + (far[0:1, :] + get_sums(second))
        total[...] = jnp.broadcast_to(value, total.shape)
        for ref in out:
            put_sums(ref, value)
    else:
        out = refs
    odd = is_odd("lon")
    edge, corner = HALO * cols, HALO * HALO
    pick = picker(HALO, cols)
    for start in range(0, members, 2):
        pair = (start, start + 1)
        ends = [south_north(first, second, slice(m * edge, (m + 1) * edge)) for m in pair]
        for n in range(2):
            put_picked(pick, [end[n] for end in ends], [(2 * m + n) * corner for m in pair], out, odd)


def corners(first, second, cols, members, *sums):
    extra = EXTRA if sums else 0
    message = jax.ShapeDtypeStruct((members * 2 * HALO * HALO + extra, first.shape[1]), BF)
    shapes = [message, message] + [jax.ShapeDtypeStruct(v.shape, F32) for v in sums[:1]]
    return call(functools.partial(corners_kernel, cols, members), "corners", shapes, (first, second, *sums))


def shares_kernel(keep, got, *shares):
    size = shares[0].shape[0]
    for bits, out in enumerate(shares):
        rows = pl.ds(pl.multiple_of(share_of(bits) * size, size), size)
        out[...] = (keep[rows, :].astype(F32) + got[rows, :].astype(F32)).astype(BF)


def part_kernel(zero, one, two, three, square, message):
    size = zero.shape[0]
    message[:size, :] = (
        (zero[...].astype(F32) + one[...].astype(F32)) + (two[...].astype(F32) + three[...].astype(F32))
    ).astype(BF)
    put_sums(message, jnp.sum(square[...], axis=0, keepdims=True))


def weight_kernel(message, other, precision, _, out):
    size = precision.shape[0] // 8
    share = lax.axis_index("core") * 4 + lax.axis_index("x")
    mine = precision[pl.ds(pl.multiple_of(share * size, size), size), :]
    increment = message[:size, :].astype(F32) + other[:size, :].astype(F32)
    weighted = mine * increment
    out[:size, :] = weighted.astype(BF)
    put_sums(out, (get_sums(message) + get_sums(other)) + jnp.sum(weighted * increment, axis=0, keepdims=True))


def gather_kernel(zero, one, two, three, out):
    size = zero.shape[0] - EXTRA
    for n, ref in enumerate((zero, one, two, three)):
        out[n * size : (n + 1) * size, :] = ref[:size, :]
    put_sums(out, (get_sums(zero) + get_sums(one)) + (get_sums(two) + get_sums(three)))


def adjoint_of(ensemble, weighted, vertical):
    return lax.dot_general(
        (ensemble.astype(F32) * weighted).astype(BF),
        vertical[...],
        (((1,), (1,)), ((), ())),
        preferred_element_type=F32,
    ).astype(BF)


def level_edges_kernel(mine, other, ensemble, vertical, first, second):
    members, cells, _ = ensemble.shape
    share = cells // 8
    edge = (first.shape[0] - EXTRA) // members
    core, odd = lax.axis_index("core"), is_odd("lat")
    south = pl.ds(pl.multiple_of(share_of(0) * share, edge), edge)
    north = pl.ds(pl.multiple_of(share_of(3) * share + share - edge, edge), edge)
    low_weight = jnp.where(core == 0, mine[south, :], other[south, :]).astype(F32)
    high_weight = jnp.where(core == 0, other[north, :], mine[north, :]).astype(F32)
    for m in range(members):
        low = adjoint_of(ensemble[m, :edge, :], low_weight, vertical)
        high = adjoint_of(ensemble[m, cells - edge :, :], high_weight, vertical)
        first[m * edge : (m + 1) * edge, :] = jnp.where(odd, low, high)
        second[m * edge : (m + 1) * edge, :] = jnp.where(odd, high, low)
    value = get_sums(mine) + get_sums(other)
    put_sums(first, value)
    put_sums(second, value)


def level_kernel(mine, other, ensemble, vertical, adjoint, sums):
    sums[...] = jnp.broadcast_to(get_sums(mine) + get_sums(other), sums.shape)
    members, cells, _ = adjoint.shape
    share = cells // 8
    core = lax.axis_index("core")
    for which, half in ((mine, core), (other, 1 - core)):
        for k in range(4):
            rows = pl.ds(pl.multiple_of((half * 4 + share_of(k)) * share, share), share)
            weighted = which[k * share : (k + 1) * share, :].astype(F32)
            for m in range(members):
                adjoint[m, rows, :] = adjoint_of(ensemble[m, rows, :], weighted, vertical)


def backward_kernel(
    cols, entries, inner, one, two, one_corner, two_corner, band, control, sums, far,
    hessian, curvature, result, west, east, done,
):
    members, cells, levels = inner.shape
    size = ROWS * cols
    joined((one, two), (one_corner, two_corner), (west, east), members, cols, cells)
    copies = []
    for start in range(0, members, 2):
        pair = (start, start + 1)
        for row in range(0, cells, size):
            rows = slice(row, row + size)
            for m, side in zip(pair, sides(band, west, east, pair, row // size, side_rows(cells, cols))):
                result[m, rows, :] = control[m, rows, :].astype(F32) + with_sides(inner[m, rows, :], side, cols)
            if (row + size) % (cells // 4) == 0:
                for m in pair:
                    part = pl.ds(row + size - cells // 4, cells // 4)
                    copy = pltpu.make_async_copy(
                        result.at[m, part, :], hessian.at[m, part, :], done.at[len(copies)]
                    )
                    copy.start()
                    copies.append(copy)
    value = (sums[0:1, :] + get_sums(one_corner)) + (far[0:1, :] + get_sums(two_corner))
    curvature[0, 0] = jnp.sum(value) / entries
    for copy in copies:
        copy.wait()


def exchange(first, second, axis):
    return lax.ppermute(first, axis, swap(axis, 1)), lax.ppermute(second, axis, swap(axis, 3))


def per_device(control, ensemble, precision, lat_taps, lon_taps, vertical):
    members, tile_rows, cols, levels = control.shape
    cells = tile_rows * cols
    entries = control.size * lax.axis_size(MEM) * lax.axis_size("lat") * lax.axis_size("lon")
    own, spread = control.reshape(members, cells, levels), ensemble.reshape(members, cells, levels)
    share = cells // 8
    row = jax.ShapeDtypeStruct((8, levels), F32)

    def rows(count):
        return jax.ShapeDtypeStruct((count, levels), BF)

    edge = HALO * cols
    first, second = call(edges_kernel, "edges", [rows(members * edge)] * 2, (own,))
    one, two = exchange(first, second, "lat")
    beside_it = exchange(*strips(own, cols), "lon")
    corner = exchange(*corners(one, two, cols, members), "lon")
    band, band_side = bands(lat_taps, lon_taps, cols, False)
    inner, square = centre(own, one, two, band, cols, True)
    joint = rows(members * side_rows(cells, cols))
    send, west, east = call(
        functools.partial(send_kernel, cols),
        "forward_send",
        [rows(cells // 2), joint, joint],
        (inner, *beside_it, *corner, band_side, vertical, spread),
        flops=700_000_000,
        size=3_000_000,
    )
    (keep,) = call(
        functools.partial(keep_kernel, cols),
        "forward_keep",
        [rows(cells // 2)],
        (inner, west, east, band_side, vertical, spread),
        flops=700_000_000,
        size=3_000_000,
    )

    got = lax.ppermute(send, "core", swap("core", 1))
    zero, one, two, three = call(shares_kernel, "shares", [rows(share)] * 4, (keep, got))
    two, one, three = [lax.ppermute(v, "x", swap("x", k)) for v, k in ((two, 2), (one, 1), (three, 3))]
    band_back, band_side_back = bands(lat_taps, lon_taps, cols, True, three)
    (message,) = call(part_kernel, "part", [rows(share + EXTRA)], (zero, one, two, three, square))
    other = lax.ppermute(message, "zh", swap("zh", 1))
    (zero,) = call(weight_kernel, "weight", [rows(share + EXTRA)], (message, other, precision.reshape(cells, levels), band_side_back))
    two, one, three = [lax.ppermute(zero, "x", swap("x", k)) for k in (2, 1, 3)]
    (message,) = call(gather_kernel, "gather", [rows(cells // 2 + EXTRA)], (zero, one, two, three))
    other = lax.ppermute(message, "core", swap("core", 1))

    message_shape = rows(members * edge + EXTRA)
    first, second = call(
        level_edges_kernel, "level_edges", [message_shape, message_shape], (message, other, spread, vertical)
    )
    adjoint, sums = call(
        level_kernel,
        "level",
        [jax.ShapeDtypeStruct(own.shape, BF), row],
        (message, other, spread, vertical),
        flops=300_000_000,
        size=4_500_000,
    )
    one, two = exchange(first, second, "lat")
    far = lax.ppermute(sums, "lat", swap("lat", 2))
    beside_it = exchange(*strips(adjoint, cols), "lon")
    *corner, sums = corners(one, two, cols, members, sums, far)
    corner = exchange(*corner, "lon")
    far = lax.ppermute(sums, "lon", swap("lon", 2))
    inner = centre(adjoint, one, two, band_back, cols, False)[0]
    hessian, curvature = call(
        functools.partial(backward_kernel, cols, entries),
        "backward",
        [jax.ShapeDtypeStruct(own.shape, F32), jax.ShapeDtypeStruct((1, 1), F32)],
        (inner, *beside_it, *corner, band_side_back, own, sums, far),
        scratch=(
            pltpu.VMEM(own.shape, F32),
            pltpu.VMEM((members * side_rows(cells, cols), levels), BF),
            pltpu.VMEM((members * side_rows(cells, cols), levels), BF),
            pltpu.SemaphoreType.DMA((4 * members,)),
        ),
        out_specs=(pl.BlockSpec(memory_space=pl.ANY), SMEM),
        flops=1_000_000_000,
        size=9_000_000,
    )
    return hessian.reshape(control.shape), curvature.reshape(())


def solution(mesh):
    split = Mesh(
        mesh.devices.reshape(2, 4, 2, mesh.shape["lat"], mesh.shape["lon"]),
        ("zh", "x", "core", "lat", "lon"),
    )
    return jax.shard_map(
        per_device,
        mesh=split,
        in_specs=(
            P(MEM, "lat", "lon", None),
            P(MEM, "lat", "lon", None),
            P("lat", "lon", None),
            P(),
            P(),
            P(),
        ),
        out_specs=(P(MEM, "lat", "lon", None), P()),
        check_vma=False,
    )
```

```python
import functools

import jax
import jax.numpy as jnp
from jax import lax
from jax.experimental import pallas as pl
from jax.experimental.pallas import tpu as pltpu
from jax.sharding import Mesh
from jax.sharding import PartitionSpec as P

MEM = ("zh", "x", "core")
BF = jnp.bfloat16
F32 = jnp.float32
HALO = 4
TAPS = 9
ROWS = 8
VMEM = pl.BlockSpec(memory_space=pltpu.VMEM)
SMEM = pl.BlockSpec(memory_space=pltpu.SMEM)
EXTRA = 16


def swap(axis, bits):
    return [(i, i ^ bits) for i in range(lax.axis_size(axis))]


def params(mib=12):
    return pltpu.CompilerParams(vmem_limit_bytes=mib * 2**20)


def cost(flops, size):
    return pl.CostEstimate(flops=flops, bytes_accessed=size, transcendentals=0)


def is_odd(axis):
    return lax.rem(lax.axis_index(axis), 2) == 1


def taps_at(index, taps, flip):
    value = jnp.zeros(index.shape, F32)
    for t in range(TAPS):
        value = jnp.where(index == t, taps[TAPS - 1 - t if flip else t], value)
    return value


def put_halves(out, row, value):
    high = value.astype(BF)
    size = value.shape[0]
    out[row : row + size, :] = high
    out[row + out.shape[0] // 2 : row + out.shape[0] // 2 + size, :] = (value - high.astype(F32)).astype(BF)


def band_kernel(cols, flip, lat_taps, lon_taps, *refs):
    wide, narrow = refs[-2:]
    k = lax.broadcasted_iota(jnp.int32, (cols, wide.shape[1]), 1)
    j = lax.broadcasted_iota(jnp.int32, (cols, wide.shape[1]), 0)
    row, shift = k // cols, k % cols - j + HALO
    k2 = lax.broadcasted_iota(jnp.int32, (16, narrow.shape[1]), 1)
    j2 = lax.broadcasted_iota(jnp.int32, (16, narrow.shape[1]), 0)
    half = narrow.shape[1] // 2
    in_west = k2 < half
    row2 = jnp.where(in_west, k2, k2 - half) // HALO
    column = k2 % HALO
    target = jnp.where(j2 < 8, j2, j2 + cols - 16)
    shift2 = jnp.where(in_west, column, column + cols + HALO) - target
    across = taps_at(shift, lon_taps, flip)
    across2 = taps_at(shift2, lon_taps, flip)
    for i in range(ROWS):
        put_halves(wide, i * cols, taps_at(row - i, lat_taps, flip) * across)
        put_halves(narrow, i * 16, taps_at(row2 - i, lat_taps, flip) * across2)


def bands(lat_taps, lon_taps, cols, flip, *after):
    span = ROWS + 2 * HALO
    wide = jax.ShapeDtypeStruct((2 * ROWS * cols, span * cols), BF)
    narrow = jax.ShapeDtypeStruct((2 * ROWS * 16, 2 * span * HALO), BF)
    return pl.pallas_call(
        functools.partial(band_kernel, cols, flip),
        out_shape=(wide, narrow),
        in_specs=[SMEM, SMEM] + [VMEM] * len(after),
        out_specs=(VMEM,) * 2,
        compiler_params=params(),
        cost_estimate=cost(2_000_000, 600_000),
        name="bands_back" if flip else "bands",
    )(lat_taps, lon_taps, *after)


def south_north(first, second, rows):
    odd = is_odd("lat")
    at = lax.axis_index("lat")
    zero = jnp.zeros((rows.stop - rows.start, first.shape[1]), BF)
    one, two = first[rows, :], second[rows, :]
    south = jnp.where(at == 0, zero, jnp.where(odd, one, two))
    north = jnp.where(at == lax.axis_size("lat") - 1, zero, jnp.where(odd, two, one))
    return south, north


def centre_blocks(cols, own, first, second, band):
    members, cells, levels = own.shape
    size, edge = ROWS * cols, HALO * cols
    for start in range(0, members, 2):
        pair = (start, start + 1)
        edges = [south_north(first, second, slice(m * edge, (m + 1) * edge)) for m in pair]
        for row in range(0, cells, size):
            lo, hi = max(row - edge, 0), min(row + size + edge, cells)
            parts = []
            for m, (south, north) in zip(pair, edges):
                part = [south] if row == 0 else []
                part.append(own[m, lo:hi, :])
                if row + size == cells:
                    part.append(north)
                parts.append(jnp.concatenate(part, axis=0) if len(part) > 1 else part[0])
            both = jnp.dot(band[...], jnp.concatenate(parts, axis=1), preferred_element_type=F32)
            both = both[:size] + both[size:]
            for n, m in enumerate(pair):
                yield m, row, both[:, n * levels : (n + 1) * levels]


def centre_kernel(cols, own, first, second, band, out, square):
    levels = own.shape[2]
    size = ROWS * cols
    total = jnp.zeros((8, levels), F32)
    for m, row, value in centre_blocks(cols, own, first, second, band):
        out[m, row : row + size, :] = value
        c = own[m, row : row + size, :].astype(F32)
        total = total + jnp.sum((c * c).reshape(size // 8, 8, levels), axis=0)
    square[...] = total


def centre_back_kernel(cols, own, first, second, band, control, sums, hessian, outer, same, middle, done):
    members, cells, levels = own.shape
    size = ROWS * cols
    batch = 2 * ROWS
    copies = []
    for m, row, value in centre_blocks(cols, own, first, second, band):
        value = (control[m, row : row + size, :].astype(F32) + value).reshape(ROWS, cols, levels)
        at = row // cols
        rows = slice(at, at + ROWS)
        middle[m, rows, :, :] = value[:, 8 : cols - 8]
        outer[m, rows, :8, :] = value[:, :8]
        outer[m, rows, 8:, :] = value[:, cols - 8 :]
        if (at + ROWS) % batch == 0:
            rows = pl.ds(at + ROWS - batch, batch)
            copy = pltpu.make_async_copy(
                middle.at[m, rows], hessian.at[m, rows, pl.ds(8, cols - 16), :], done.at[len(copies)]
            )
            copy.start()
            copies.append(copy)
    same[...] = sums[...]
    for copy in copies:
        copy.wait()


def joined(strips, corners, out, members, cols, cells):
    odd = is_odd("lon")
    edge = HALO * HALO
    length = cells // cols * HALO
    for m in range(members):
        at = m * (length + 2 * edge)
        for place, refs, start, size in (
            (at, corners, 2 * m * edge, edge),
            (at + edge, strips, m * length, length),
            (at + edge + length, corners, (2 * m + 1) * edge, edge),
        ):
            one, two = (ref[start : start + size, :] for ref in refs)
            out[0][place : place + size, :] = jnp.where(odd, one, two)
            out[1][place : place + size, :] = jnp.where(odd, two, one)


def side_rows(cells, cols):
    return (cells // cols + 2 * HALO) * HALO


def sides(band, west, east, pair, block, stride):
    count = (ROWS + 2 * HALO) * HALO
    parts = []
    for m in pair:
        at = pl.ds(pl.multiple_of(m * stride + block * ROWS * HALO, 32), count)
        parts.append(jnp.concatenate([west[at, :], east[at, :]], axis=0))
    both = jnp.dot(band[...], jnp.concatenate(parts, axis=1), preferred_element_type=F32)
    size = both.shape[0] // 2
    both = both[:size] + both[size:]
    levels = both.shape[1] // len(pair)
    return [both[:, n * levels : (n + 1) * levels] for n in range(len(pair))]


def with_sides(value, side, cols):
    levels = value.shape[1]
    value = value.reshape(ROWS, cols, levels)
    side = side.reshape(ROWS, 16, levels)
    return jnp.concatenate(
        [value[:, :8] + side[:, :8], value[:, 8 : cols - 8], value[:, cols - 8 :] + side[:, 8:]], axis=1
    ).reshape(ROWS * cols, levels)


def half_forward(cols, half, inner, west, east, band, vertical, ensemble, out):
    members, cells, levels = inner.shape
    size = ROWS * cols
    count = cells // size // 2
    stride = side_rows(cells, cols)
    for n in range(count):
        block = half * count + n
        rows = pl.ds(pl.multiple_of(block * size, size), size)
        increment = jnp.zeros((size, levels), F32)
        for start in range(0, members, 2):
            pair = (start, start + 1)
            for m, side in zip(pair, sides(band, west, east, pair, block, stride)):
                smoothed = with_sides(inner[m, rows, :], side, cols).astype(BF)
                leveled = jnp.dot(smoothed, vertical[...], preferred_element_type=F32)
                increment = increment + ensemble[m, rows, :].astype(F32) * leveled
        out[n * size : (n + 1) * size, :] = increment.astype(BF)


def send_kernel(cols, inner, one, two, one_corner, two_corner, band, vertical, ensemble, out, west, east):
    members, cells, _ = inner.shape
    joined((one, two), (one_corner, two_corner), (west, east), members, cols, cells)
    half_forward(cols, 1 - lax.axis_index("core"), inner, west, east, band, vertical, ensemble, out)


def keep_kernel(cols, inner, west, east, band, vertical, ensemble, out):
    half_forward(cols, lax.axis_index("core"), inner, west, east, band, vertical, ensemble, out)


def put_sums(message, sums):
    row = lax.broadcasted_iota(jnp.int32, (EXTRA, sums.shape[1]), 0)
    parts = jnp.zeros(row.shape, F32)
    for n in range(3):
        part = sums.astype(BF).astype(F32)
        parts = jnp.where(row == n, part, parts)
        sums = sums - part
    message[message.shape[0] - EXTRA :, :] = parts.astype(BF)


def get_sums(message):
    return jnp.sum(message[message.shape[0] - EXTRA :, :].astype(F32), axis=0, keepdims=True)


def share_of(bits):
    return lax.axis_index("x") ^ bits


def call(kernel, name, shapes, inputs, in_specs=None, scratch=(), flops=1_000_000, size=1_000_000, out_specs=None, mib=12, aliases=None):
    return pl.pallas_call(
        kernel,
        out_shape=tuple(shapes),
        in_specs=in_specs or [VMEM] * len(inputs),
        out_specs=out_specs or (VMEM,) * len(shapes),
        scratch_shapes=scratch,
        input_output_aliases=aliases or {},
        compiler_params=params(mib),
        cost_estimate=cost(flops, size),
        name=name,
    )(*inputs)


def edges_kernel(tile, first, second):
    members, cells, _ = tile.shape
    edge = first.shape[0] // members
    odd = is_odd("lat")
    for m in range(members):
        low, high = tile[m, :edge, :], tile[m, cells - edge :, :]
        first[m * edge : (m + 1) * edge, :] = jnp.where(odd, low, high)
        second[m * edge : (m + 1) * edge, :] = jnp.where(odd, high, low)


def picker(lat_rows, cols):
    count = lat_rows * HALO
    row = lax.broadcasted_iota(jnp.int32, (2 * count, lat_rows * cols), 0)
    cell = lax.broadcasted_iota(jnp.int32, (2 * count, lat_rows * cols), 1)
    low = row < count
    at = jnp.where(low, row, row - count)
    wanted = at // HALO * cols + at % HALO + jnp.where(low, 0, cols - HALO)
    return jnp.where(cell == wanted, 1.0, 0.0).astype(BF)


def put_picked(pick, parts, place, out, odd):
    got = jnp.dot(pick, jnp.concatenate(parts, axis=1), preferred_element_type=F32).astype(BF)
    half = got.shape[0] // 2
    levels = got.shape[1] // len(parts)
    low, high = got[:half], got[half:]
    for ref, value in zip(out, (jnp.where(odd, low, high), jnp.where(odd, high, low))):
        for n, at in enumerate(place):
            ref[at : at + half, :] = value[:, n * levels : (n + 1) * levels]


def strips_kernel(cols, tile, *out):
    members, cells, _ = tile.shape
    odd = is_odd("lon")
    block = 16
    pick = picker(block, cols)
    length = cells // cols * HALO
    for start in range(0, members, 2):
        pair = (start, start + 1)
        for row in range(0, cells, block * cols):
            parts = [tile[m, row : row + block * cols, :] for m in pair]
            put_picked(pick, parts, [m * length + row // cols * HALO for m in pair], out, odd)


def strips(tile, cols):
    members, cells, levels = tile.shape
    message = jax.ShapeDtypeStruct((members * (cells // cols) * HALO, levels), BF)
    return call(
        functools.partial(strips_kernel, cols), "strips", [message] * 2, (tile,), flops=300_000_000, size=3_000_000
    )


def corners_kernel(cols, members, first, second, *refs):
    if len(refs) > 2:
        sums, far, around, *out, total = refs
        at, last = lax.axis_index("lat"), lax.axis_size("lat") - 1
        other = jnp.where(jnp.logical_or(at == 0, at == last), around[0:1, :], get_sums(second))
        value = (sums[0:1, :] + get_sums(first)) + (far[0:1, :] + other)
        total[...] = jnp.broadcast_to(value, total.shape)
        for ref in out:
            put_sums(ref, value)
    else:
        out = refs
    odd = is_odd("lon")
    edge, corner = HALO * cols, HALO * HALO
    pick = picker(HALO, cols)
    for start in range(0, members, 2):
        pair = (start, start + 1)
        ends = [south_north(first, second, slice(m * edge, (m + 1) * edge)) for m in pair]
        for n in range(2):
            put_picked(pick, [end[n] for end in ends], [(2 * m + n) * corner for m in pair], out, odd)


def corners(first, second, cols, members, *sums):
    extra = EXTRA if sums else 0
    message = jax.ShapeDtypeStruct((members * 2 * HALO * HALO + extra, first.shape[1]), BF)
    shapes = [message, message] + [jax.ShapeDtypeStruct(v.shape, F32) for v in sums[:1]]
    return call(functools.partial(corners_kernel, cols, members), "corners", shapes, (first, second, *sums))


def shares_kernel(keep, got, *shares):
    size = shares[0].shape[0]
    for bits, out in enumerate(shares):
        rows = pl.ds(pl.multiple_of(share_of(bits) * size, size), size)
        out[...] = (keep[rows, :].astype(F32) + got[rows, :].astype(F32)).astype(BF)


def part_kernel(zero, one, two, three, square, message):
    size = zero.shape[0]
    message[:size, :] = (
        (zero[...].astype(F32) + one[...].astype(F32)) + (two[...].astype(F32) + three[...].astype(F32))
    ).astype(BF)
    put_sums(message, jnp.sum(square[...], axis=0, keepdims=True))


def weight_kernel(message, other, precision, _, out):
    size = precision.shape[0] // 8
    share = lax.axis_index("core") * 4 + lax.axis_index("x")
    mine = precision[pl.ds(pl.multiple_of(share * size, size), size), :]
    increment = message[:size, :].astype(F32) + other[:size, :].astype(F32)
    weighted = mine * increment
    out[:size, :] = weighted.astype(BF)
    put_sums(out, (get_sums(message) + get_sums(other)) + jnp.sum(weighted * increment, axis=0, keepdims=True))


def gather_kernel(zero, one, two, three, out):
    size = zero.shape[0] - EXTRA
    for n, ref in enumerate((zero, one, two, three)):
        out[n * size : (n + 1) * size, :] = ref[:size, :]
    put_sums(out, (get_sums(zero) + get_sums(one)) + (get_sums(two) + get_sums(three)))


def adjoint_of(ensemble, weighted, vertical):
    return lax.dot_general(
        (ensemble.astype(F32) * weighted).astype(BF),
        vertical[...],
        (((1,), (1,)), ((), ())),
        preferred_element_type=F32,
    ).astype(BF)


def level_edges_kernel(mine, other, ensemble, vertical, first, second):
    members, cells, _ = ensemble.shape
    share = cells // 8
    edge = (first.shape[0] - EXTRA) // members
    core, odd = lax.axis_index("core"), is_odd("lat")
    south = pl.ds(pl.multiple_of(share_of(0) * share, edge), edge)
    north = pl.ds(pl.multiple_of(share_of(3) * share + share - edge, edge), edge)
    low_weight = jnp.where(core == 0, mine[south, :], other[south, :]).astype(F32)
    high_weight = jnp.where(core == 0, other[north, :], mine[north, :]).astype(F32)
    for m in range(members):
        low = adjoint_of(ensemble[m, :edge, :], low_weight, vertical)
        high = adjoint_of(ensemble[m, cells - edge :, :], high_weight, vertical)
        first[m * edge : (m + 1) * edge, :] = jnp.where(odd, low, high)
        second[m * edge : (m + 1) * edge, :] = jnp.where(odd, high, low)
    value = get_sums(mine) + get_sums(other)
    put_sums(first, value)
    put_sums(second, value)


def level_kernel(mine, other, ensemble, vertical, adjoint, sums):
    sums[...] = jnp.broadcast_to(get_sums(mine) + get_sums(other), sums.shape)
    members, cells, _ = adjoint.shape
    share = cells // 8
    core = lax.axis_index("core")
    for which, half in ((mine, core), (other, 1 - core)):
        for k in range(4):
            rows = pl.ds(pl.multiple_of((half * 4 + share_of(k)) * share, share), share)
            weighted = which[k * share : (k + 1) * share, :].astype(F32)
            for m in range(members):
                adjoint[m, rows, :] = adjoint_of(ensemble[m, rows, :], weighted, vertical)


def backward_kernel(
    cols, outer, one, two, one_corner, two_corner, band, sums, _, hessian, same, result, west, east, done
):
    members, tile_rows, width, levels = outer.shape
    cells = tile_rows * cols
    batch = 2 * ROWS
    joined((one, two), (one_corner, two_corner), (west, east), members, cols, cells)
    copies = []
    for start in range(0, members, 2):
        pair = (start, start + 1)
        for block in range(tile_rows // ROWS):
            rows = slice(block * ROWS, (block + 1) * ROWS)
            for m, side in zip(pair, sides(band, west, east, pair, block, side_rows(cells, cols))):
                result[m, rows, :, :] = outer[m, rows, :, :] + side.reshape(ROWS, width, levels)
            if (block + 1) * ROWS % batch == 0:
                rows = pl.ds((block + 1) * ROWS - batch, batch)
                for m in pair:
                    for source, target in ((0, 0), (8, cols - 8)):
                        copy = pltpu.make_async_copy(
                            result.at[m, rows, pl.ds(source, 8), :],
                            hessian.at[m, rows, pl.ds(target, 8), :],
                            done.at[len(copies)],
                        )
                        copy.start()
                        copies.append(copy)
    same[...] = sums[...]
    for copy in copies:
        copy.wait()


def finish_kernel(entries, sums, far, one_corner, two_corner, curvature):
    value = (sums[0:1, :] + get_sums(one_corner)) + (far[0:1, :] + get_sums(two_corner))
    curvature[0, 0] = jnp.sum(value) / entries


def exchange(first, second, axis):
    other = swap(axis, 3)
    if axis == "lat":
        other = [(i, j) for i, j in other if abs(i - j) == 1]
    return lax.ppermute(first, axis, swap(axis, 1)), lax.ppermute(second, axis, other)


def per_device(control, ensemble, precision, lat_taps, lon_taps, vertical):
    members, tile_rows, cols, levels = control.shape
    cells = tile_rows * cols
    entries = control.size * lax.axis_size(MEM) * lax.axis_size("lat") * lax.axis_size("lon")
    own, spread = control.reshape(members, cells, levels), ensemble.reshape(members, cells, levels)
    share = cells // 8
    row = jax.ShapeDtypeStruct((8, levels), F32)

    def rows(count):
        return jax.ShapeDtypeStruct((count, levels), BF)

    edge = HALO * cols
    first, second = call(edges_kernel, "edges", [rows(members * edge)] * 2, (own,))
    one, two = exchange(first, second, "lat")
    beside_it = exchange(*strips(own, cols), "lon")
    corner = exchange(*corners(one, two, cols, members), "lon")
    band, band_side = bands(lat_taps, lon_taps, cols, False)
    inner, square = call(
        functools.partial(centre_kernel, cols),
        "centre",
        [jax.ShapeDtypeStruct(own.shape, F32), row],
        (own, one, two, band),
        flops=3_000_000_000,
        size=7_000_000,
    )
    joint = rows(members * side_rows(cells, cols))
    send, west, east = call(
        functools.partial(send_kernel, cols),
        "forward_send",
        [rows(cells // 2), joint, joint],
        (inner, *beside_it, *corner, band_side, vertical, spread),
        flops=700_000_000,
        size=3_000_000,
    )
    (keep,) = call(
        functools.partial(keep_kernel, cols),
        "forward_keep",
        [rows(cells // 2)],
        (inner, west, east, band_side, vertical, spread),
        flops=700_000_000,
        size=3_000_000,
    )

    got = lax.ppermute(send, "core", swap("core", 1))
    zero, one, two, three = call(shares_kernel, "shares", [rows(share)] * 4, (keep, got))
    two, one, three = [lax.ppermute(v, "x", swap("x", k)) for v, k in ((two, 2), (one, 1), (three, 3))]
    band_back, band_side_back = bands(lat_taps, lon_taps, cols, True, three)
    (message,) = call(part_kernel, "part", [rows(share + EXTRA)], (zero, one, two, three, square))
    other = lax.ppermute(message, "zh", swap("zh", 1))
    (zero,) = call(weight_kernel, "weight", [rows(share + EXTRA)], (message, other, precision.reshape(cells, levels), band_side_back))
    two, one, three = [lax.ppermute(zero, "x", swap("x", k)) for k in (2, 1, 3)]
    (message,) = call(gather_kernel, "gather", [rows(cells // 2 + EXTRA)], (zero, one, two, three))
    other = lax.ppermute(message, "core", swap("core", 1))

    message_shape = rows(members * edge + EXTRA)
    first, second = call(
        level_edges_kernel, "level_edges", [message_shape, message_shape], (message, other, spread, vertical)
    )
    adjoint, sums = call(
        level_kernel,
        "level",
        [jax.ShapeDtypeStruct(own.shape, BF), row],
        (message, other, spread, vertical),
        flops=300_000_000,
        size=4_500_000,
    )
    one, two = exchange(first, second, "lat")
    last = lax.axis_size("lat") - 1
    far = lax.ppermute(sums, "lat", swap("lat", 2))
    around = lax.ppermute(sums, "lat", [(0, last), (last, 0)])
    beside_it = exchange(*strips(adjoint, cols), "lon")
    *corner, sums = corners(one, two, cols, members, sums, far, around)
    corner = exchange(*corner, "lon")
    outer_shape = (members, tile_rows, 16, levels)
    hessian, outer, sums = call(
        functools.partial(centre_back_kernel, cols),
        "centre_back",
        [jax.ShapeDtypeStruct(control.shape, F32), jax.ShapeDtypeStruct(outer_shape, F32), row],
        (adjoint, one, two, band_back, own, sums),
        out_specs=(pl.BlockSpec(memory_space=pl.ANY), VMEM, VMEM),
        scratch=(
            pltpu.VMEM((members, tile_rows, cols - 16, levels), F32),
            pltpu.SemaphoreType.DMA((members * tile_rows // (2 * ROWS),)),
        ),
        flops=3_000_000_000,
        size=7_000_000,
    )
    far = lax.ppermute(sums, "lon", swap("lon", 2))
    hessian, sums = call(
        functools.partial(backward_kernel, cols),
        "backward",
        [jax.ShapeDtypeStruct(control.shape, F32), row],
        (outer, *beside_it, *corner, band_side_back, sums, hessian),
        in_specs=[VMEM] * 7 + [pl.BlockSpec(memory_space=pl.ANY)],
        scratch=(
            pltpu.VMEM(outer_shape, F32),
            pltpu.VMEM(joint.shape, BF),
            pltpu.VMEM(joint.shape, BF),
            pltpu.SemaphoreType.DMA((2 * members * tile_rows // (2 * ROWS),)),
        ),
        out_specs=(pl.BlockSpec(memory_space=pl.ANY), VMEM),
        aliases={7: 0},
        flops=1_000_000_000,
        size=9_000_000,
    )
    (curvature,) = call(
        functools.partial(finish_kernel, entries),
        "finish",
        [jax.ShapeDtypeStruct((1, 1), F32)],
        (sums, far, *corner),
        out_specs=(SMEM,),
    )
    return hessian, curvature.reshape(())


def solution(mesh):
    split = Mesh(
        mesh.devices.reshape(2, 4, 2, mesh.shape["lat"], mesh.shape["lon"]),
        ("zh", "x", "core", "lat", "lon"),
    )
    return jax.shard_map(
        per_device,
        mesh=split,
        in_specs=(
            P(MEM, "lat", "lon", None),
            P(MEM, "lat", "lon", None),
            P("lat", "lon", None),
            P(),
            P(),
            P(),
        ),
        out_specs=(P(MEM, "lat", "lon", None), P()),
        check_vma=False,
    )
```

```python
import functools

import jax
import jax.numpy as jnp
from jax import lax
from jax.experimental import pallas as pl
from jax.experimental.pallas import tpu as pltpu
from jax.sharding import Mesh
from jax.sharding import PartitionSpec as P

MEM = ("zh", "x", "core")
BF = jnp.bfloat16
F32 = jnp.float32
HALO = 4
TAPS = 9
ROWS = 8
VMEM = pl.BlockSpec(memory_space=pltpu.VMEM)
SMEM = pl.BlockSpec(memory_space=pltpu.SMEM)
EXTRA = 16


def swap(axis, bits):
    return [(i, i ^ bits) for i in range(lax.axis_size(axis))]


def params(mib=12):
    return pltpu.CompilerParams(vmem_limit_bytes=mib * 2**20)


def cost(flops, size):
    return pl.CostEstimate(flops=flops, bytes_accessed=size, transcendentals=0)


def is_odd(axis):
    return lax.rem(lax.axis_index(axis), 2) == 1


def taps_at(index, taps, flip):
    value = jnp.zeros(index.shape, F32)
    for t in range(TAPS):
        value = jnp.where(index == t, taps[TAPS - 1 - t if flip else t], value)
    return value


def put_halves(out, row, value):
    high = value.astype(BF)
    size = value.shape[0]
    out[row : row + size, :] = high
    out[row + out.shape[0] // 2 : row + out.shape[0] // 2 + size, :] = (value - high.astype(F32)).astype(BF)


def band_kernel(cols, flip, lat_taps, lon_taps, *refs):
    wide, narrow = refs[-2:]
    k = lax.broadcasted_iota(jnp.int32, (cols, wide.shape[1]), 1)
    j = lax.broadcasted_iota(jnp.int32, (cols, wide.shape[1]), 0)
    row, shift = k // cols, k % cols - j + HALO
    k2 = lax.broadcasted_iota(jnp.int32, (16, narrow.shape[1]), 1)
    j2 = lax.broadcasted_iota(jnp.int32, (16, narrow.shape[1]), 0)
    half = narrow.shape[1] // 2
    in_west = k2 < half
    row2 = jnp.where(in_west, k2, k2 - half) // HALO
    column = k2 % HALO
    target = jnp.where(j2 < 8, j2, j2 + cols - 16)
    shift2 = jnp.where(in_west, column, column + cols + HALO) - target
    across = taps_at(shift, lon_taps, flip)
    across2 = taps_at(shift2, lon_taps, flip)
    for i in range(ROWS):
        put_halves(wide, i * cols, taps_at(row - i, lat_taps, flip) * across)
        put_halves(narrow, i * 16, taps_at(row2 - i, lat_taps, flip) * across2)


def bands(lat_taps, lon_taps, cols, flip, *after):
    span = ROWS + 2 * HALO
    wide = jax.ShapeDtypeStruct((2 * ROWS * cols, span * cols), BF)
    narrow = jax.ShapeDtypeStruct((2 * ROWS * 16, 2 * span * HALO), BF)
    return pl.pallas_call(
        functools.partial(band_kernel, cols, flip),
        out_shape=(wide, narrow),
        in_specs=[SMEM, SMEM] + [VMEM] * len(after),
        out_specs=(VMEM,) * 2,
        compiler_params=params(),
        cost_estimate=cost(2_000_000, 600_000),
        name="bands_back" if flip else "bands",
    )(lat_taps, lon_taps, *after)


def south_north(first, second, rows):
    odd = is_odd("lat")
    at = lax.axis_index("lat")
    zero = jnp.zeros((rows.stop - rows.start, first.shape[1]), BF)
    one, two = first[rows, :], second[rows, :]
    south = jnp.where(at == 0, zero, jnp.where(odd, one, two))
    north = jnp.where(at == lax.axis_size("lat") - 1, zero, jnp.where(odd, two, one))
    return south, north


def centre_blocks(cols, own, first, second, band):
    members, cells, levels = own.shape
    size, edge = ROWS * cols, HALO * cols
    for start in range(0, members, 2):
        pair = (start, start + 1)
        edges = [south_north(first, second, slice(m * edge, (m + 1) * edge)) for m in pair]
        for row in range(0, cells, size):
            lo, hi = max(row - edge, 0), min(row + size + edge, cells)
            parts = []
            for m, (south, north) in zip(pair, edges):
                part = [south] if row == 0 else []
                part.append(own[m, lo:hi, :])
                if row + size == cells:
                    part.append(north)
                parts.append(jnp.concatenate(part, axis=0) if len(part) > 1 else part[0])
            both = jnp.dot(band[...], jnp.concatenate(parts, axis=1), preferred_element_type=F32)
            both = both[:size] + both[size:]
            for n, m in enumerate(pair):
                yield m, row, both[:, n * levels : (n + 1) * levels]


def centre_kernel(cols, own, first, second, band, out, square):
    levels = own.shape[2]
    size = ROWS * cols
    total = jnp.zeros((8, levels), F32)
    for m, row, value in centre_blocks(cols, own, first, second, band):
        out[m, row : row + size, :] = value
        c = own[m, row : row + size, :].astype(F32)
        total = total + jnp.sum((c * c).reshape(size // 8, 8, levels), axis=0)
    square[...] = total


def centre_back_kernel(cols, own, first, second, band, control, hessian, outer, middle, done):
    members, cells, levels = own.shape
    size = ROWS * cols
    batch = 2 * ROWS
    copies = []
    for m, row, value in centre_blocks(cols, own, first, second, band):
        value = (control[m, row : row + size, :].astype(F32) + value).reshape(ROWS, cols, levels)
        at = row // cols
        rows = slice(at, at + ROWS)
        middle[m, rows, :, :] = value[:, 8 : cols - 8]
        outer[m, rows, :8, :] = value[:, :8]
        outer[m, rows, 8:, :] = value[:, cols - 8 :]
        if (at + ROWS) % batch == 0:
            rows = pl.ds(at + ROWS - batch, batch)
            copy = pltpu.make_async_copy(
                middle.at[m, rows], hessian.at[m, rows, pl.ds(8, cols - 16), :], done.at[len(copies)]
            )
            copy.start()
            copies.append(copy)
    for copy in copies:
        copy.wait()


def joined(strips, corners, out, members, cols, cells):
    odd = is_odd("lon")
    edge = HALO * HALO
    length = cells // cols * HALO
    for m in range(members):
        at = m * (length + 2 * edge)
        for place, refs, start, size in (
            (at, corners, 2 * m * edge, edge),
            (at + edge, strips, m * length, length),
            (at + edge + length, corners, (2 * m + 1) * edge, edge),
        ):
            one, two = (ref[start : start + size, :] for ref in refs)
            out[0][place : place + size, :] = jnp.where(odd, one, two)
            out[1][place : place + size, :] = jnp.where(odd, two, one)


def side_rows(cells, cols):
    return (cells // cols + 2 * HALO) * HALO


def sides(band, west, east, pair, block, stride):
    count = (ROWS + 2 * HALO) * HALO
    parts = []
    for m in pair:
        at = pl.ds(pl.multiple_of(m * stride + block * ROWS * HALO, 32), count)
        parts.append(jnp.concatenate([west[at, :], east[at, :]], axis=0))
    both = jnp.dot(band[...], jnp.concatenate(parts, axis=1), preferred_element_type=F32)
    size = both.shape[0] // 2
    both = both[:size] + both[size:]
    levels = both.shape[1] // len(pair)
    return [both[:, n * levels : (n + 1) * levels] for n in range(len(pair))]


def with_sides(value, side, cols):
    levels = value.shape[1]
    value = value.reshape(ROWS, cols, levels)
    side = side.reshape(ROWS, 16, levels)
    return jnp.concatenate(
        [value[:, :8] + side[:, :8], value[:, 8 : cols - 8], value[:, cols - 8 :] + side[:, 8:]], axis=1
    ).reshape(ROWS * cols, levels)


def half_forward(cols, half, inner, west, east, band, vertical, ensemble, out):
    members, cells, levels = inner.shape
    size = ROWS * cols
    count = cells // size // 2
    stride = side_rows(cells, cols)
    for n in range(count):
        block = half * count + n
        rows = pl.ds(pl.multiple_of(block * size, size), size)
        increment = jnp.zeros((size, levels), F32)
        for start in range(0, members, 2):
            pair = (start, start + 1)
            for m, side in zip(pair, sides(band, west, east, pair, block, stride)):
                smoothed = with_sides(inner[m, rows, :], side, cols).astype(BF)
                leveled = jnp.dot(smoothed, vertical[...], preferred_element_type=F32)
                increment = increment + ensemble[m, rows, :].astype(F32) * leveled
        out[n * size : (n + 1) * size, :] = increment.astype(BF)


def send_kernel(cols, inner, one, two, one_corner, two_corner, band, vertical, ensemble, out, west, east):
    members, cells, _ = inner.shape
    joined((one, two), (one_corner, two_corner), (west, east), members, cols, cells)
    half_forward(cols, 1 - lax.axis_index("core"), inner, west, east, band, vertical, ensemble, out)


def keep_kernel(cols, inner, west, east, band, vertical, ensemble, out):
    half_forward(cols, lax.axis_index("core"), inner, west, east, band, vertical, ensemble, out)


def put_sums(message, sums):
    row = lax.broadcasted_iota(jnp.int32, (EXTRA, sums.shape[1]), 0)
    parts = jnp.zeros(row.shape, F32)
    for n in range(3):
        part = sums.astype(BF).astype(F32)
        parts = jnp.where(row == n, part, parts)
        sums = sums - part
    message[message.shape[0] - EXTRA :, :] = parts.astype(BF)


def get_sums(message):
    return jnp.sum(message[message.shape[0] - EXTRA :, :].astype(F32), axis=0, keepdims=True)


def share_of(bits):
    return lax.axis_index("x") ^ bits


def call(kernel, name, shapes, inputs, in_specs=None, scratch=(), flops=1_000_000, size=1_000_000, out_specs=None, mib=12, aliases=None):
    return pl.pallas_call(
        kernel,
        out_shape=tuple(shapes),
        in_specs=in_specs or [VMEM] * len(inputs),
        out_specs=out_specs or (VMEM,) * len(shapes),
        scratch_shapes=scratch,
        input_output_aliases=aliases or {},
        compiler_params=params(mib),
        cost_estimate=cost(flops, size),
        name=name,
    )(*inputs)


def edges_kernel(tile, first, second):
    members, cells, _ = tile.shape
    edge = first.shape[0] // members
    odd = is_odd("lat")
    for m in range(members):
        low, high = tile[m, :edge, :], tile[m, cells - edge :, :]
        first[m * edge : (m + 1) * edge, :] = jnp.where(odd, low, high)
        second[m * edge : (m + 1) * edge, :] = jnp.where(odd, high, low)


def picker(lat_rows, cols):
    count = lat_rows * HALO
    row = lax.broadcasted_iota(jnp.int32, (2 * count, lat_rows * cols), 0)
    cell = lax.broadcasted_iota(jnp.int32, (2 * count, lat_rows * cols), 1)
    low = row < count
    at = jnp.where(low, row, row - count)
    wanted = at // HALO * cols + at % HALO + jnp.where(low, 0, cols - HALO)
    return jnp.where(cell == wanted, 1.0, 0.0).astype(BF)


def put_picked(pick, parts, place, out, odd):
    got = jnp.dot(pick, jnp.concatenate(parts, axis=1), preferred_element_type=F32).astype(BF)
    half = got.shape[0] // 2
    levels = got.shape[1] // len(parts)
    low, high = got[:half], got[half:]
    for ref, value in zip(out, (jnp.where(odd, low, high), jnp.where(odd, high, low))):
        for n, at in enumerate(place):
            ref[at : at + half, :] = value[:, n * levels : (n + 1) * levels]


def strips_kernel(cols, tile, *out):
    members, cells, _ = tile.shape
    odd = is_odd("lon")
    block = 16
    pick = picker(block, cols)
    length = cells // cols * HALO
    for start in range(0, members, 2):
        pair = (start, start + 1)
        for row in range(0, cells, block * cols):
            parts = [tile[m, row : row + block * cols, :] for m in pair]
            put_picked(pick, parts, [m * length + row // cols * HALO for m in pair], out, odd)


def strips(tile, cols):
    members, cells, levels = tile.shape
    message = jax.ShapeDtypeStruct((members * (cells // cols) * HALO, levels), BF)
    return call(
        functools.partial(strips_kernel, cols), "strips", [message] * 2, (tile,), flops=300_000_000, size=3_000_000
    )


def corners_kernel(cols, members, first, second, *refs):
    if len(refs) > 2:
        sums, far, *out, total = refs
        value = (sums[0:1, :] + get_sums(first)) + (far[0:1, :] + get_sums(second))
        total[...] = jnp.broadcast_to(value, total.shape)
        for ref in out:
            put_sums(ref, value)
    else:
        out = refs
    odd = is_odd("lon")
    edge, corner = HALO * cols, HALO * HALO
    pick = picker(HALO, cols)
    for start in range(0, members, 2):
        pair = (start, start + 1)
        ends = [south_north(first, second, slice(m * edge, (m + 1) * edge)) for m in pair]
        for n in range(2):
            put_picked(pick, [end[n] for end in ends], [(2 * m + n) * corner for m in pair], out, odd)


def corners(first, second, cols, members, *sums):
    extra = EXTRA if sums else 0
    message = jax.ShapeDtypeStruct((members * 2 * HALO * HALO + extra, first.shape[1]), BF)
    shapes = [message, message] + [jax.ShapeDtypeStruct(v.shape, F32) for v in sums[:1]]
    return call(functools.partial(corners_kernel, cols, members), "corners", shapes, (first, second, *sums))


def shares_kernel(keep, got, *shares):
    size = shares[0].shape[0]
    for bits, out in enumerate(shares):
        rows = pl.ds(pl.multiple_of(share_of(bits) * size, size), size)
        out[...] = (keep[rows, :].astype(F32) + got[rows, :].astype(F32)).astype(BF)


def part_kernel(zero, one, two, three, square, message):
    size = zero.shape[0]
    message[:size, :] = (
        (zero[...].astype(F32) + one[...].astype(F32)) + (two[...].astype(F32) + three[...].astype(F32))
    ).astype(BF)
    put_sums(message, jnp.sum(square[...], axis=0, keepdims=True))


def weight_kernel(message, other, precision, _, out):
    size = precision.shape[0] // 8
    share = lax.axis_index("core") * 4 + lax.axis_index("x")
    mine = precision[pl.ds(pl.multiple_of(share * size, size), size), :]
    increment = message[:size, :].astype(F32) + other[:size, :].astype(F32)
    weighted = mine * increment
    out[:size, :] = weighted.astype(BF)
    put_sums(out, (get_sums(message) + get_sums(other)) + jnp.sum(weighted * increment, axis=0, keepdims=True))


def gather_kernel(zero, one, two, three, out):
    size = zero.shape[0] - EXTRA
    for n, ref in enumerate((zero, one, two, three)):
        out[n * size : (n + 1) * size, :] = ref[:size, :]
    put_sums(out, (get_sums(zero) + get_sums(one)) + (get_sums(two) + get_sums(three)))


def adjoint_of(ensemble, weighted, vertical):
    return lax.dot_general(
        (ensemble.astype(F32) * weighted).astype(BF),
        vertical[...],
        (((1,), (1,)), ((), ())),
        preferred_element_type=F32,
    ).astype(BF)


def level_edges_kernel(mine, other, ensemble, vertical, first, second):
    members, cells, _ = ensemble.shape
    share = cells // 8
    edge = (first.shape[0] - EXTRA) // members
    core, odd = lax.axis_index("core"), is_odd("lat")
    south = pl.ds(pl.multiple_of(share_of(0) * share, edge), edge)
    north = pl.ds(pl.multiple_of(share_of(3) * share + share - edge, edge), edge)
    low_weight = jnp.where(core == 0, mine[south, :], other[south, :]).astype(F32)
    high_weight = jnp.where(core == 0, other[north, :], mine[north, :]).astype(F32)
    for m in range(members):
        low = adjoint_of(ensemble[m, :edge, :], low_weight, vertical)
        high = adjoint_of(ensemble[m, cells - edge :, :], high_weight, vertical)
        first[m * edge : (m + 1) * edge, :] = jnp.where(odd, low, high)
        second[m * edge : (m + 1) * edge, :] = jnp.where(odd, high, low)
    value = get_sums(mine) + get_sums(other)
    put_sums(first, value)
    put_sums(second, value)


def level_kernel(mine, other, ensemble, vertical, adjoint, sums):
    sums[...] = jnp.broadcast_to(get_sums(mine) + get_sums(other), sums.shape)
    members, cells, _ = adjoint.shape
    share = cells // 8
    core = lax.axis_index("core")
    for which, half in ((mine, core), (other, 1 - core)):
        for k in range(4):
            rows = pl.ds(pl.multiple_of((half * 4 + share_of(k)) * share, share), share)
            weighted = which[k * share : (k + 1) * share, :].astype(F32)
            for m in range(members):
                adjoint[m, rows, :] = adjoint_of(ensemble[m, rows, :], weighted, vertical)


def backward_kernel(
    cols, entries, outer, one, two, one_corner, two_corner, band, sums, far, _,
    hessian, curvature, result, west, east, done,
):
    members, tile_rows, width, levels = outer.shape
    cells = tile_rows * cols
    batch = 2 * ROWS
    joined((one, two), (one_corner, two_corner), (west, east), members, cols, cells)
    copies = []
    for start in range(0, members, 2):
        pair = (start, start + 1)
        for block in range(tile_rows // ROWS):
            rows = slice(block * ROWS, (block + 1) * ROWS)
            for m, side in zip(pair, sides(band, west, east, pair, block, side_rows(cells, cols))):
                result[m, rows, :, :] = outer[m, rows, :, :] + side.reshape(ROWS, width, levels)
            if (block + 1) * ROWS % batch == 0:
                rows = pl.ds((block + 1) * ROWS - batch, batch)
                for m in pair:
                    for source, target in ((0, 0), (8, cols - 8)):
                        copy = pltpu.make_async_copy(
                            result.at[m, rows, pl.ds(source, 8), :],
                            hessian.at[m, rows, pl.ds(target, 8), :],
                            done.at[len(copies)],
                        )
                        copy.start()
                        copies.append(copy)
    value = (sums[0:1, :] + get_sums(one_corner)) + (far[0:1, :] + get_sums(two_corner))
    curvature[0, 0] = jnp.sum(value) / entries
    for copy in copies:
        copy.wait()


def exchange(first, second, axis):
    if axis == "lat":
        count = lax.axis_size("zh") * lax.axis_size("lat")
        axis = ("zh", "lat")
    else:
        count = lax.axis_size(axis)
    one = [(i, i ^ 1) for i in range(count)]
    two = [(i, (i + 1 if i % 2 else i - 1) % count) for i in range(count)]
    return lax.ppermute(first, axis, one), lax.ppermute(second, axis, two)


def per_device(control, ensemble, precision, lat_taps, lon_taps, vertical):
    members, tile_rows, cols, levels = control.shape
    cells = tile_rows * cols
    entries = control.size * lax.axis_size(MEM) * lax.axis_size("lat") * lax.axis_size("lon")
    own, spread = control.reshape(members, cells, levels), ensemble.reshape(members, cells, levels)
    share = cells // 8
    row = jax.ShapeDtypeStruct((8, levels), F32)

    def rows(count):
        return jax.ShapeDtypeStruct((count, levels), BF)

    edge = HALO * cols
    first, second = call(edges_kernel, "edges", [rows(members * edge)] * 2, (own,))
    one, two = exchange(first, second, "lat")
    beside_it = exchange(*strips(own, cols), "lon")
    corner = exchange(*corners(one, two, cols, members), "lon")
    band, band_side = bands(lat_taps, lon_taps, cols, False)
    inner, square = call(
        functools.partial(centre_kernel, cols),
        "centre",
        [jax.ShapeDtypeStruct(own.shape, F32), row],
        (own, one, two, band),
        flops=3_000_000_000,
        size=7_000_000,
    )
    joint = rows(members * side_rows(cells, cols))
    send, west, east = call(
        functools.partial(send_kernel, cols),
        "forward_send",
        [rows(cells // 2), joint, joint],
        (inner, *beside_it, *corner, band_side, vertical, spread),
        flops=700_000_000,
        size=3_000_000,
    )
    (keep,) = call(
        functools.partial(keep_kernel, cols),
        "forward_keep",
        [rows(cells // 2)],
        (inner, west, east, band_side, vertical, spread),
        flops=700_000_000,
        size=3_000_000,
    )

    got = lax.ppermute(send, "core", swap("core", 1))
    zero, one, two, three = call(shares_kernel, "shares", [rows(share)] * 4, (keep, got))
    two, one, three = [lax.ppermute(v, "x", swap("x", k)) for v, k in ((two, 2), (one, 1), (three, 3))]
    band_back, band_side_back = bands(lat_taps, lon_taps, cols, True, three)
    (message,) = call(part_kernel, "part", [rows(share + EXTRA)], (zero, one, two, three, square))
    other = lax.ppermute(message, "zh", swap("zh", 1))
    (zero,) = call(weight_kernel, "weight", [rows(share + EXTRA)], (message, other, precision.reshape(cells, levels), band_side_back))
    two, one, three = [lax.ppermute(zero, "x", swap("x", k)) for k in (2, 1, 3)]
    (message,) = call(gather_kernel, "gather", [rows(cells // 2 + EXTRA)], (zero, one, two, three))
    other = lax.ppermute(message, "core", swap("core", 1))

    message_shape = rows(members * edge + EXTRA)
    first, second = call(
        level_edges_kernel, "level_edges", [message_shape, message_shape], (message, other, spread, vertical)
    )
    adjoint, sums = call(
        level_kernel,
        "level",
        [jax.ShapeDtypeStruct(own.shape, BF), row],
        (message, other, spread, vertical),
        flops=300_000_000,
        size=4_500_000,
    )
    one, two = exchange(first, second, "lat")
    far = lax.ppermute(sums, "lat", swap("lat", 2))
    beside_it = exchange(*strips(adjoint, cols), "lon")
    *corner, sums = corners(one, two, cols, members, sums, far)
    corner = exchange(*corner, "lon")
    outer_shape = (members, tile_rows, 16, levels)
    far = lax.ppermute(sums, "lon", swap("lon", 2))
    hessian, outer = call(
        functools.partial(centre_back_kernel, cols),
        "centre_back",
        [jax.ShapeDtypeStruct(control.shape, F32), jax.ShapeDtypeStruct(outer_shape, F32)],
        (adjoint, one, two, band_back, own),
        out_specs=(pl.BlockSpec(memory_space=pl.ANY), VMEM),
        scratch=(
            pltpu.VMEM((members, tile_rows, cols - 16, levels), F32),
            pltpu.SemaphoreType.DMA((members * tile_rows // (2 * ROWS),)),
        ),
        flops=3_000_000_000,
        size=7_000_000,
    )
    hessian, curvature = call(
        functools.partial(backward_kernel, cols, entries),
        "backward",
        [jax.ShapeDtypeStruct(control.shape, F32), jax.ShapeDtypeStruct((1, 1), F32)],
        (outer, *beside_it, *corner, band_side_back, sums, far, hessian),
        in_specs=[VMEM] * 8 + [pl.BlockSpec(memory_space=pl.ANY)],
        scratch=(
            pltpu.VMEM(outer_shape, F32),
            pltpu.VMEM(joint.shape, BF),
            pltpu.VMEM(joint.shape, BF),
            pltpu.SemaphoreType.DMA((2 * members * tile_rows // (2 * ROWS),)),
        ),
        out_specs=(pl.BlockSpec(memory_space=pl.ANY), SMEM),
        aliases={8: 0},
        flops=1_000_000_000,
        size=9_000_000,
    )
    return hessian, curvature.reshape(())


def solution(mesh):
    split = Mesh(
        mesh.devices.reshape(2, 4, 2, mesh.shape["lat"], mesh.shape["lon"]),
        ("zh", "x", "core", "lat", "lon"),
    )
    return jax.shard_map(
        per_device,
        mesh=split,
        in_specs=(
            P(MEM, "lat", "lon", None),
            P(MEM, "lat", "lon", None),
            P("lat", "lon", None),
            P(),
            P(),
            P(),
        ),
        out_specs=(P(MEM, "lat", "lon", None), P()),
        check_vma=False,
    )
```

```python
import functools

import jax
import jax.numpy as jnp
from jax import lax
from jax.experimental import pallas as pl
from jax.experimental.pallas import tpu as pltpu
from jax.sharding import Mesh
from jax.sharding import PartitionSpec as P

MEM = ("zh", "x", "core")
BF = jnp.bfloat16
F32 = jnp.float32
HALO = 4
TAPS = 9
ROWS = 8
VMEM = pl.BlockSpec(memory_space=pltpu.VMEM)
SMEM = pl.BlockSpec(memory_space=pltpu.SMEM)
EXTRA = 16


def swap(axis, bits):
    return [(i, i ^ bits) for i in range(lax.axis_size(axis))]


def params(mib=12):
    return pltpu.CompilerParams(vmem_limit_bytes=mib * 2**20)


def cost(flops, size):
    return pl.CostEstimate(flops=flops, bytes_accessed=size, transcendentals=0)


def is_odd(axis):
    return lax.rem(lax.axis_index(axis), 2) == 1


def taps_at(index, taps, flip):
    value = jnp.zeros(index.shape, F32)
    for t in range(TAPS):
        value = jnp.where(index == t, taps[TAPS - 1 - t if flip else t], value)
    return value


def put_halves(out, row, value):
    high = value.astype(BF)
    size = value.shape[0]
    out[row : row + size, :] = high
    out[row + out.shape[0] // 2 : row + out.shape[0] // 2 + size, :] = (value - high.astype(F32)).astype(BF)


def band_kernel(cols, flip, lat_taps, lon_taps, *refs):
    wide, narrow = refs[-2:]
    k = lax.broadcasted_iota(jnp.int32, (cols, wide.shape[1]), 1)
    j = lax.broadcasted_iota(jnp.int32, (cols, wide.shape[1]), 0)
    row, shift = k // cols, k % cols - j + HALO
    k2 = lax.broadcasted_iota(jnp.int32, (16, narrow.shape[1]), 1)
    j2 = lax.broadcasted_iota(jnp.int32, (16, narrow.shape[1]), 0)
    half = narrow.shape[1] // 2
    in_west = k2 < half
    row2 = jnp.where(in_west, k2, k2 - half) // HALO
    column = k2 % HALO
    target = jnp.where(j2 < 8, j2, j2 + cols - 16)
    shift2 = jnp.where(in_west, column, column + cols + HALO) - target
    across = taps_at(shift, lon_taps, flip)
    across2 = taps_at(shift2, lon_taps, flip)
    for i in range(ROWS):
        put_halves(wide, i * cols, taps_at(row - i, lat_taps, flip) * across)
        put_halves(narrow, i * 16, taps_at(row2 - i, lat_taps, flip) * across2)


def bands(lat_taps, lon_taps, cols, flip, *after):
    span = ROWS + 2 * HALO
    wide = jax.ShapeDtypeStruct((2 * ROWS * cols, span * cols), BF)
    narrow = jax.ShapeDtypeStruct((2 * ROWS * 16, 2 * span * HALO), BF)
    return pl.pallas_call(
        functools.partial(band_kernel, cols, flip),
        out_shape=(wide, narrow),
        in_specs=[SMEM, SMEM] + [VMEM] * len(after),
        out_specs=(VMEM,) * 2,
        compiler_params=params(),
        cost_estimate=cost(2_000_000, 600_000),
        name="bands_back" if flip else "bands",
    )(lat_taps, lon_taps, *after)


def south_north(first, second, rows):
    odd = is_odd("lat")
    at = lax.axis_index("lat")
    zero = jnp.zeros((rows.stop - rows.start, first.shape[1]), BF)
    one, two = first[rows, :], second[rows, :]
    south = jnp.where(at == 0, zero, jnp.where(odd, one, two))
    north = jnp.where(at == lax.axis_size("lat") - 1, zero, jnp.where(odd, two, one))
    return south, north


def centre_blocks(cols, own, first, second, band):
    members, cells, levels = own.shape
    size, edge = ROWS * cols, HALO * cols
    for start in range(0, members, 2):
        pair = (start, start + 1)
        edges = [south_north(first, second, slice(m * edge, (m + 1) * edge)) for m in pair]
        for row in range(0, cells, size):
            lo, hi = max(row - edge, 0), min(row + size + edge, cells)
            parts = []
            for m, (south, north) in zip(pair, edges):
                part = [south] if row == 0 else []
                part.append(own[m, lo:hi, :])
                if row + size == cells:
                    part.append(north)
                parts.append(jnp.concatenate(part, axis=0) if len(part) > 1 else part[0])
            both = jnp.dot(band[...], jnp.concatenate(parts, axis=1), preferred_element_type=F32)
            both = both[:size] + both[size:]
            for n, m in enumerate(pair):
                yield m, row, both[:, n * levels : (n + 1) * levels]


def centre_kernel(cols, own, first, second, band, out, square):
    levels = own.shape[2]
    size = ROWS * cols
    total = jnp.zeros((8, levels), F32)
    for m, row, value in centre_blocks(cols, own, first, second, band):
        out[m, row : row + size, :] = value
        c = own[m, row : row + size, :].astype(F32)
        total = total + jnp.sum((c * c).reshape(size // 8, 8, levels), axis=0)
    square[...] = total


def centre_back_kernel(cols, own, first, second, band, control, hessian, outer, middle, done):
    members, cells, levels = own.shape
    size = ROWS * cols
    batch = ROWS
    copies = []
    for m, row, value in centre_blocks(cols, own, first, second, band):
        value = (control[m, row : row + size, :].astype(F32) + value).reshape(ROWS, cols, levels)
        at = row // cols
        rows = slice(at, at + ROWS)
        middle[m, rows, :, :] = value[:, 8 : cols - 8]
        outer[m, rows, :8, :] = value[:, :8]
        outer[m, rows, 8:, :] = value[:, cols - 8 :]
        if (at + ROWS) % batch == 0:
            rows = pl.ds(at + ROWS - batch, batch)
            copy = pltpu.make_async_copy(
                middle.at[m, rows], hessian.at[m, rows, pl.ds(8, cols - 16), :], done.at[len(copies)]
            )
            copy.start()
            copies.append(copy)
    for copy in copies:
        copy.wait()


def joined(strips, corners, out, members, cols, cells):
    odd = is_odd("lon")
    edge = HALO * HALO
    length = cells // cols * HALO
    for m in members:
        at = m * (length + 2 * edge)
        for place, refs, start, size in (
            (at, corners, 2 * m * edge, edge),
            (at + edge, strips, m * length, length),
            (at + edge + length, corners, (2 * m + 1) * edge, edge),
        ):
            one, two = (ref[start : start + size, :] for ref in refs)
            out[0][place : place + size, :] = jnp.where(odd, one, two)
            out[1][place : place + size, :] = jnp.where(odd, two, one)


def side_rows(cells, cols):
    return (cells // cols + 2 * HALO) * HALO


def sides(band, west, east, pair, block, stride):
    count = (ROWS + 2 * HALO) * HALO
    parts = []
    for m in pair:
        at = pl.ds(pl.multiple_of(m * stride + block * ROWS * HALO, 32), count)
        parts.append(jnp.concatenate([west[at, :], east[at, :]], axis=0))
    both = jnp.dot(band[...], jnp.concatenate(parts, axis=1), preferred_element_type=F32)
    size = both.shape[0] // 2
    both = both[:size] + both[size:]
    levels = both.shape[1] // len(pair)
    return [both[:, n * levels : (n + 1) * levels] for n in range(len(pair))]


def with_sides(value, side, cols):
    levels = value.shape[1]
    value = value.reshape(ROWS, cols, levels)
    side = side.reshape(ROWS, 16, levels)
    return jnp.concatenate(
        [value[:, :8] + side[:, :8], value[:, 8 : cols - 8], value[:, cols - 8 :] + side[:, 8:]], axis=1
    ).reshape(ROWS * cols, levels)


def half_forward(cols, half, inner, west, east, band, vertical, ensemble, out):
    members, cells, levels = inner.shape
    size = ROWS * cols
    count = cells // size // 2
    stride = side_rows(cells, cols)
    for n in range(count):
        block = half * count + n
        rows = pl.ds(pl.multiple_of(block * size, size), size)
        increment = jnp.zeros((size, levels), F32)
        for start in range(0, members, 2):
            pair = (start, start + 1)
            for m, side in zip(pair, sides(band, west, east, pair, block, stride)):
                smoothed = with_sides(inner[m, rows, :], side, cols).astype(BF)
                leveled = jnp.dot(smoothed, vertical[...], preferred_element_type=F32)
                increment = increment + ensemble[m, rows, :].astype(F32) * leveled
        out[n * size : (n + 1) * size, :] = increment.astype(BF)


def send_kernel(cols, inner, one, two, one_corner, two_corner, band, vertical, ensemble, out, west, east):
    members, cells, _ = inner.shape
    joined((one, two), (one_corner, two_corner), (west, east), range(members), cols, cells)
    half_forward(cols, 1 - lax.axis_index("core"), inner, west, east, band, vertical, ensemble, out)


def keep_kernel(cols, inner, west, east, band, vertical, ensemble, out):
    half_forward(cols, lax.axis_index("core"), inner, west, east, band, vertical, ensemble, out)


def put_sums(message, sums):
    row = lax.broadcasted_iota(jnp.int32, (EXTRA, sums.shape[1]), 0)
    parts = jnp.zeros(row.shape, F32)
    for n in range(3):
        part = sums.astype(BF).astype(F32)
        parts = jnp.where(row == n, part, parts)
        sums = sums - part
    message[message.shape[0] - EXTRA :, :] = parts.astype(BF)


def get_sums(message):
    return jnp.sum(message[message.shape[0] - EXTRA :, :].astype(F32), axis=0, keepdims=True)


def share_of(bits):
    return lax.axis_index("x") ^ bits


def call(kernel, name, shapes, inputs, in_specs=None, scratch=(), flops=1_000_000, size=1_000_000, out_specs=None, mib=12, aliases=None):
    return pl.pallas_call(
        kernel,
        out_shape=tuple(shapes),
        in_specs=in_specs or [VMEM] * len(inputs),
        out_specs=out_specs or (VMEM,) * len(shapes),
        scratch_shapes=scratch,
        input_output_aliases=aliases or {},
        compiler_params=params(mib),
        cost_estimate=cost(flops, size),
        name=name,
    )(*inputs)


def picker(lat_rows, cols):
    count = lat_rows * HALO
    row = lax.broadcasted_iota(jnp.int32, (2 * count, lat_rows * cols), 0)
    cell = lax.broadcasted_iota(jnp.int32, (2 * count, lat_rows * cols), 1)
    low = row < count
    at = jnp.where(low, row, row - count)
    wanted = at // HALO * cols + at % HALO + jnp.where(low, 0, cols - HALO)
    return jnp.where(cell == wanted, 1.0, 0.0).astype(BF)


def put_picked(pick, parts, place, out, odd):
    got = jnp.dot(pick, jnp.concatenate(parts, axis=1), preferred_element_type=F32).astype(BF)
    half = got.shape[0] // 2
    levels = got.shape[1] // len(parts)
    low, high = got[:half], got[half:]
    for ref, value in zip(out, (jnp.where(odd, low, high), jnp.where(odd, high, low))):
        for n, at in enumerate(place):
            ref[at : at + half, :] = value[:, n * levels : (n + 1) * levels]


def strips_kernel(cols, tile, *out):
    members, cells, _ = tile.shape
    odd = is_odd("lon")
    block = 16
    pick = picker(block, cols)
    length = cells // cols * HALO
    for start in range(0, members, 2):
        pair = (start, start + 1)
        for row in range(0, cells, block * cols):
            parts = [tile[m, row : row + block * cols, :] for m in pair]
            put_picked(pick, parts, [m * length + row // cols * HALO for m in pair], out, odd)


def strips(tile, cols):
    members, cells, levels = tile.shape
    message = jax.ShapeDtypeStruct((members * (cells // cols) * HALO, levels), BF)
    return call(
        functools.partial(strips_kernel, cols), "strips", [message] * 2, (tile,), flops=300_000_000, size=3_000_000
    )


def corners_kernel(cols, members, first, second, *refs):
    if len(refs) > 2:
        sums, far, *out, total = refs
        value = (sums[0:1, :] + get_sums(first)) + (far[0:1, :] + get_sums(second))
        total[...] = jnp.broadcast_to(value, total.shape)
        for ref in out:
            put_sums(ref, value)
    else:
        out = refs
    odd = is_odd("lon")
    edge, corner = HALO * cols, HALO * HALO
    pick = picker(HALO, cols)
    for start in range(0, members, 2):
        pair = (start, start + 1)
        ends = [south_north(first, second, slice(m * edge, (m + 1) * edge)) for m in pair]
        for n in range(2):
            put_picked(pick, [end[n] for end in ends], [(2 * m + n) * corner for m in pair], out, odd)


def corners(first, second, cols, members, *sums):
    extra = EXTRA if sums else 0
    message = jax.ShapeDtypeStruct((members * 2 * HALO * HALO + extra, first.shape[1]), BF)
    shapes = [message, message] + [jax.ShapeDtypeStruct(v.shape, F32) for v in sums[:1]]
    return call(functools.partial(corners_kernel, cols, members), "corners", shapes, (first, second, *sums))


def shares_kernel(keep, got, *shares):
    size = shares[0].shape[0]
    for bits, out in enumerate(shares):
        rows = pl.ds(pl.multiple_of(share_of(bits) * size, size), size)
        out[...] = (keep[rows, :].astype(F32) + got[rows, :].astype(F32)).astype(BF)


def part_kernel(zero, one, two, three, square, message):
    size = zero.shape[0]
    message[:size, :] = (
        (zero[...].astype(F32) + one[...].astype(F32)) + (two[...].astype(F32) + three[...].astype(F32))
    ).astype(BF)
    put_sums(message, jnp.sum(square[...], axis=0, keepdims=True))


def weight_kernel(message, other, precision, _, out):
    size = precision.shape[0] // 8
    share = lax.axis_index("core") * 4 + lax.axis_index("x")
    mine = precision[pl.ds(pl.multiple_of(share * size, size), size), :]
    increment = message[:size, :].astype(F32) + other[:size, :].astype(F32)
    weighted = mine * increment
    out[:size, :] = weighted.astype(BF)
    put_sums(out, (get_sums(message) + get_sums(other)) + jnp.sum(weighted * increment, axis=0, keepdims=True))


def gather_kernel(zero, one, two, three, out):
    size = zero.shape[0] - EXTRA
    for n, ref in enumerate((zero, one, two, three)):
        out[n * size : (n + 1) * size, :] = ref[:size, :]
    put_sums(out, (get_sums(zero) + get_sums(one)) + (get_sums(two) + get_sums(three)))


def adjoint_of(ensemble, weighted, vertical):
    return lax.dot_general(
        (ensemble.astype(F32) * weighted).astype(BF),
        vertical[...],
        (((1,), (1,)), ((), ())),
        preferred_element_type=F32,
    ).astype(BF)


def level_edges_kernel(mine, other, ensemble, vertical, first, second):
    members, cells, _ = ensemble.shape
    share = cells // 8
    edge = (first.shape[0] - EXTRA) // members
    core, odd = lax.axis_index("core"), is_odd("lat")
    south = pl.ds(pl.multiple_of(share_of(0) * share, edge), edge)
    north = pl.ds(pl.multiple_of(share_of(3) * share + share - edge, edge), edge)
    low_weight = jnp.where(core == 0, mine[south, :], other[south, :]).astype(F32)
    high_weight = jnp.where(core == 0, other[north, :], mine[north, :]).astype(F32)
    for m in range(members):
        low = adjoint_of(ensemble[m, :edge, :], low_weight, vertical)
        high = adjoint_of(ensemble[m, cells - edge :, :], high_weight, vertical)
        first[m * edge : (m + 1) * edge, :] = jnp.where(odd, low, high)
        second[m * edge : (m + 1) * edge, :] = jnp.where(odd, high, low)
    value = get_sums(mine) + get_sums(other)
    put_sums(first, value)
    put_sums(second, value)


def level_kernel(mine, other, ensemble, vertical, adjoint, sums):
    sums[...] = jnp.broadcast_to(get_sums(mine) + get_sums(other), sums.shape)
    members, cells, _ = adjoint.shape
    share = cells // 8
    core = lax.axis_index("core")
    for which, half in ((mine, core), (other, 1 - core)):
        for k in range(4):
            rows = pl.ds(pl.multiple_of((half * 4 + share_of(k)) * share, share), share)
            weighted = which[k * share : (k + 1) * share, :].astype(F32)
            for m in range(members):
                adjoint[m, rows, :] = adjoint_of(ensemble[m, rows, :], weighted, vertical)


def backward_kernel(
    cols, entries, outer, one, two, one_corner, two_corner, band, sums, far, _,
    hessian, curvature, result, west, east, done,
):
    members, tile_rows, width, levels = outer.shape
    cells = tile_rows * cols
    batch = 2 * ROWS
    copies = []
    for start in range(0, members, 2):
        pair = (start, start + 1)
        joined((one, two), (one_corner, two_corner), (west, east), pair, cols, cells)
        for block in range(tile_rows // ROWS):
            rows = slice(block * ROWS, (block + 1) * ROWS)
            for m, side in zip(pair, sides(band, west, east, pair, block, side_rows(cells, cols))):
                result[m, rows, :, :] = outer[m, rows, :, :] + side.reshape(ROWS, width, levels)
            if (block + 1) * ROWS % batch == 0:
                rows = pl.ds((block + 1) * ROWS - batch, batch)
                for m in pair:
                    for source, target in ((0, 0), (8, cols - 8)):
                        copy = pltpu.make_async_copy(
                            result.at[m, rows, pl.ds(source, 8), :],
                            hessian.at[m, rows, pl.ds(target, 8), :],
                            done.at[len(copies)],
                        )
                        copy.start()
                        copies.append(copy)
    value = (sums[0:1, :] + get_sums(one_corner)) + (far[0:1, :] + get_sums(two_corner))
    curvature[0, 0] = jnp.sum(value) / entries
    for copy in copies:
        copy.wait()


def exchange(first, second, axis):
    if axis == "lat":
        count = lax.axis_size("zh") * lax.axis_size("lat")
        axis = ("zh", "lat")
    else:
        count = lax.axis_size(axis)
    one = [(i, i ^ 1) for i in range(count)]
    two = [(i, (i + 1 if i % 2 else i - 1) % count) for i in range(count)]
    return lax.ppermute(first, axis, one), lax.ppermute(second, axis, two)


def per_device(control, ensemble, precision, lat_taps, lon_taps, vertical):
    members, tile_rows, cols, levels = control.shape
    cells = tile_rows * cols
    entries = control.size * lax.axis_size(MEM) * lax.axis_size("lat") * lax.axis_size("lon")
    own, spread = control.reshape(members, cells, levels), ensemble.reshape(members, cells, levels)
    share = cells // 8
    row = jax.ShapeDtypeStruct((8, levels), F32)

    def rows(count):
        return jax.ShapeDtypeStruct((count, levels), BF)

    edge = HALO * cols
    low, high = control[:, :HALO].reshape(-1, levels), control[:, tile_rows - HALO :].reshape(-1, levels)
    odd = is_odd("lat")
    one, two = exchange(jnp.where(odd, low, high), jnp.where(odd, high, low), "lat")
    beside_it = exchange(*strips(own, cols), "lon")
    low, high = corners(one, two, cols, members)
    corner = exchange(low, high, "lon")
    band, band_side = bands(lat_taps, lon_taps, cols, False, low)
    inner, square = call(
        functools.partial(centre_kernel, cols),
        "centre",
        [jax.ShapeDtypeStruct(own.shape, F32), row],
        (own, one, two, band),
        flops=3_000_000_000,
        size=7_000_000,
    )
    joint = rows(members * side_rows(cells, cols))
    send, west, east = call(
        functools.partial(send_kernel, cols),
        "forward_send",
        [rows(cells // 2), joint, joint],
        (inner, *beside_it, *corner, band_side, vertical, spread),
        flops=700_000_000,
        size=3_000_000,
    )
    (keep,) = call(
        functools.partial(keep_kernel, cols),
        "forward_keep",
        [rows(cells // 2)],
        (inner, west, east, band_side, vertical, spread),
        flops=700_000_000,
        size=3_000_000,
    )

    got = lax.ppermute(send, "core", swap("core", 1))
    zero, one, two, three = call(shares_kernel, "shares", [rows(share)] * 4, (keep, got))
    two, one, three = [lax.ppermute(v, "x", swap("x", k)) for v, k in ((two, 2), (one, 1), (three, 3))]
    band_back, band_side_back = bands(lat_taps, lon_taps, cols, True, three)
    (message,) = call(part_kernel, "part", [rows(share + EXTRA)], (zero, one, two, three, square))
    other = lax.ppermute(message, "zh", swap("zh", 1))
    (zero,) = call(weight_kernel, "weight", [rows(share + EXTRA)], (message, other, precision.reshape(cells, levels), band_side_back))
    two, one, three = [lax.ppermute(zero, "x", swap("x", k)) for k in (2, 1, 3)]
    (message,) = call(gather_kernel, "gather", [rows(cells // 2 + EXTRA)], (zero, one, two, three))
    other = lax.ppermute(message, "core", swap("core", 1))

    message_shape = rows(members * edge + EXTRA)
    first, second = call(
        level_edges_kernel, "level_edges", [message_shape, message_shape], (message, other, spread, vertical)
    )
    adjoint, sums = call(
        level_kernel,
        "level",
        [jax.ShapeDtypeStruct(own.shape, BF), row],
        (message, other, spread, vertical),
        flops=300_000_000,
        size=4_500_000,
    )
    one, two = exchange(first, second, "lat")
    far = lax.ppermute(sums, "lat", swap("lat", 2))
    beside_it = exchange(*strips(adjoint, cols), "lon")
    *corner, sums = corners(one, two, cols, members, sums, far)
    corner = exchange(*corner, "lon")
    outer_shape = (members, tile_rows, 16, levels)
    far = lax.ppermute(sums, "lon", swap("lon", 2))
    hessian, outer = call(
        functools.partial(centre_back_kernel, cols),
        "centre_back",
        [jax.ShapeDtypeStruct(control.shape, F32), jax.ShapeDtypeStruct(outer_shape, F32)],
        (adjoint, one, two, band_back, own),
        out_specs=(pl.BlockSpec(memory_space=pl.ANY), VMEM),
        scratch=(
            pltpu.VMEM((members, tile_rows, cols - 16, levels), F32),
            pltpu.SemaphoreType.DMA((members * tile_rows // ROWS,)),
        ),
        flops=3_000_000_000,
        size=7_000_000,
    )
    hessian, curvature = call(
        functools.partial(backward_kernel, cols, entries),
        "backward",
        [jax.ShapeDtypeStruct(control.shape, F32), jax.ShapeDtypeStruct((1, 1), F32)],
        (outer, *beside_it, *corner, band_side_back, sums, far, hessian),
        in_specs=[VMEM] * 8 + [pl.BlockSpec(memory_space=pl.ANY)],
        scratch=(
            pltpu.VMEM(outer_shape, F32),
            pltpu.VMEM(joint.shape, BF),
            pltpu.VMEM(joint.shape, BF),
            pltpu.SemaphoreType.DMA((2 * members * tile_rows // (2 * ROWS),)),
        ),
        out_specs=(pl.BlockSpec(memory_space=pl.ANY), SMEM),
        aliases={8: 0},
        flops=1_000_000_000,
        size=9_000_000,
    )
    return hessian, curvature.reshape(())


def solution(mesh):
    split = Mesh(
        mesh.devices.reshape(2, 4, 2, mesh.shape["lat"], mesh.shape["lon"]),
        ("zh", "x", "core", "lat", "lon"),
    )
    return jax.shard_map(
        per_device,
        mesh=split,
        in_specs=(
            P(MEM, "lat", "lon", None),
            P(MEM, "lat", "lon", None),
            P("lat", "lon", None),
            P(),
            P(),
            P(),
        ),
        out_specs=(P(MEM, "lat", "lon", None), P()),
        check_vma=False,
    )
```

```python
import functools

import jax
import jax.numpy as jnp
from jax import lax
from jax.experimental import pallas as pl
from jax.experimental.pallas import tpu as pltpu
from jax.sharding import Mesh
from jax.sharding import PartitionSpec as P

MEM = ("zh", "x", "core")
BF = jnp.bfloat16
F32 = jnp.float32
HALO = 4
TAPS = 9
ROWS = 8
VMEM = pl.BlockSpec(memory_space=pltpu.VMEM)
SMEM = pl.BlockSpec(memory_space=pltpu.SMEM)
EXTRA = 16


def swap(axis, bits):
    return [(i, i ^ bits) for i in range(lax.axis_size(axis))]


def params(mib=12):
    return pltpu.CompilerParams(vmem_limit_bytes=mib * 2**20)


def cost(flops, size):
    return pl.CostEstimate(flops=flops, bytes_accessed=size, transcendentals=0)


def is_odd(axis):
    return lax.rem(lax.axis_index(axis) + lax.axis_index("core"), 2) == 1


def taps_at(index, taps, flip):
    value = jnp.zeros(index.shape, F32)
    for t in range(TAPS):
        value = jnp.where(index == t, taps[TAPS - 1 - t if flip else t], value)
    return value


def put_halves(out, row, value):
    high = value.astype(BF)
    size = value.shape[0]
    out[row : row + size, :] = high
    out[row + out.shape[0] // 2 : row + out.shape[0] // 2 + size, :] = (value - high.astype(F32)).astype(BF)


def band_kernel(cols, flip, lat_taps, lon_taps, *refs):
    wide, narrow = refs[-2:]
    k = lax.broadcasted_iota(jnp.int32, (cols, wide.shape[1]), 1)
    j = lax.broadcasted_iota(jnp.int32, (cols, wide.shape[1]), 0)
    row, shift = k // cols, k % cols - j + HALO
    k2 = lax.broadcasted_iota(jnp.int32, (16, narrow.shape[1]), 1)
    j2 = lax.broadcasted_iota(jnp.int32, (16, narrow.shape[1]), 0)
    half = narrow.shape[1] // 2
    in_west = k2 < half
    row2 = jnp.where(in_west, k2, k2 - half) // HALO
    column = k2 % HALO
    target = jnp.where(j2 < 8, j2, j2 + cols - 16)
    shift2 = jnp.where(in_west, column, column + cols + HALO) - target
    across = taps_at(shift, lon_taps, flip)
    across2 = taps_at(shift2, lon_taps, flip)
    for i in range(ROWS):
        put_halves(wide, i * cols, taps_at(row - i, lat_taps, flip) * across)
        put_halves(narrow, i * 16, taps_at(row2 - i, lat_taps, flip) * across2)


def bands(lat_taps, lon_taps, cols, flip, *after):
    span = ROWS + 2 * HALO
    wide = jax.ShapeDtypeStruct((2 * ROWS * cols, span * cols), BF)
    narrow = jax.ShapeDtypeStruct((2 * ROWS * 16, 2 * span * HALO), BF)
    return pl.pallas_call(
        functools.partial(band_kernel, cols, flip),
        out_shape=(wide, narrow),
        in_specs=[SMEM, SMEM] + [VMEM] * len(after),
        out_specs=(VMEM,) * 2,
        compiler_params=params(),
        cost_estimate=cost(2_000_000, 600_000),
        name="bands_back" if flip else "bands",
    )(lat_taps, lon_taps, *after)


def south_north(first, second, rows):
    odd = is_odd("lat")
    at = lax.axis_index("lat")
    zero = jnp.zeros((rows.stop - rows.start, first.shape[1]), BF)
    one, two = first[rows, :], second[rows, :]
    south = jnp.where(at == 0, zero, jnp.where(odd, one, two))
    north = jnp.where(at == lax.axis_size("lat") - 1, zero, jnp.where(odd, two, one))
    return south, north


def centre_blocks(cols, own, first, second, band):
    members, cells, levels = own.shape
    size, edge = ROWS * cols, HALO * cols
    for start in range(0, members, 2):
        pair = (start, start + 1)
        edges = [south_north(first, second, slice(m * edge, (m + 1) * edge)) for m in pair]
        for row in range(0, cells, size):
            lo, hi = max(row - edge, 0), min(row + size + edge, cells)
            parts = []
            for m, (south, north) in zip(pair, edges):
                part = [south] if row == 0 else []
                part.append(own[m, lo:hi, :])
                if row + size == cells:
                    part.append(north)
                parts.append(jnp.concatenate(part, axis=0) if len(part) > 1 else part[0])
            both = jnp.dot(band[...], jnp.concatenate(parts, axis=1), preferred_element_type=F32)
            both = both[:size] + both[size:]
            for n, m in enumerate(pair):
                yield m, row, both[:, n * levels : (n + 1) * levels]


def centre_kernel(cols, own, first, second, band, out, square):
    levels = own.shape[2]
    size = ROWS * cols
    total = jnp.zeros((8, levels), F32)
    for m, row, value in centre_blocks(cols, own, first, second, band):
        out[m, row : row + size, :] = value
        c = own[m, row : row + size, :].astype(F32)
        total = total + jnp.sum((c * c).reshape(size // 8, 8, levels), axis=0)
    square[...] = total


def centre_back_kernel(cols, own, first, second, band, control, hessian, outer, middle, done):
    members, cells, levels = own.shape
    size = ROWS * cols
    batch = 2 * ROWS
    copies = []
    for m, row, value in centre_blocks(cols, own, first, second, band):
        value = (control[m, row : row + size, :].astype(F32) + value).reshape(ROWS, cols, levels)
        at = row // cols
        rows = slice(at, at + ROWS)
        middle[m, rows, :, :] = value[:, 8 : cols - 8]
        outer[m, rows, :8, :] = value[:, :8]
        outer[m, rows, 8:, :] = value[:, cols - 8 :]
        if (at + ROWS) % batch == 0:
            rows = pl.ds(at + ROWS - batch, batch)
            copy = pltpu.make_async_copy(
                middle.at[m, rows], hessian.at[m, rows, pl.ds(8, cols - 16), :], done.at[len(copies)]
            )
            copy.start()
            copies.append(copy)
    for copy in copies:
        copy.wait()


def joined(strips, corners, out, members, cols, cells):
    odd = is_odd("lon")
    edge = HALO * HALO
    length = cells // cols * HALO
    for m in range(members):
        at = m * (length + 2 * edge)
        for place, refs, start, size in (
            (at, corners, 2 * m * edge, edge),
            (at + edge, strips, m * length, length),
            (at + edge + length, corners, (2 * m + 1) * edge, edge),
        ):
            one, two = (ref[start : start + size, :] for ref in refs)
            out[0][place : place + size, :] = jnp.where(odd, one, two)
            out[1][place : place + size, :] = jnp.where(odd, two, one)


def side_rows(cells, cols):
    return (cells // cols + 2 * HALO) * HALO


def sides(band, west, east, pair, block, stride):
    count = (ROWS + 2 * HALO) * HALO
    parts = []
    for m in pair:
        at = pl.ds(pl.multiple_of(m * stride + block * ROWS * HALO, 32), count)
        parts.append(jnp.concatenate([west[at, :], east[at, :]], axis=0))
    both = jnp.dot(band[...], jnp.concatenate(parts, axis=1), preferred_element_type=F32)
    size = both.shape[0] // 2
    both = both[:size] + both[size:]
    levels = both.shape[1] // len(pair)
    return [both[:, n * levels : (n + 1) * levels] for n in range(len(pair))]


def with_sides(value, side, cols):
    levels = value.shape[1]
    value = value.reshape(ROWS, cols, levels)
    side = side.reshape(ROWS, 16, levels)
    return jnp.concatenate(
        [value[:, :8] + side[:, :8], value[:, 8 : cols - 8], value[:, cols - 8 :] + side[:, 8:]], axis=1
    ).reshape(ROWS * cols, levels)


def half_forward(cols, half, inner, west, east, band, vertical, ensemble, out):
    members, cells, levels = inner.shape
    size = ROWS * cols
    count = cells // size // 2
    stride = side_rows(cells, cols)
    for n in range(count):
        block = half * count + n
        rows = pl.ds(pl.multiple_of(block * size, size), size)
        increment = jnp.zeros((size, levels), F32)
        for start in range(0, members, 2):
            pair = (start, start + 1)
            for m, side in zip(pair, sides(band, west, east, pair, block, stride)):
                smoothed = with_sides(inner[m, rows, :], side, cols).astype(BF)
                leveled = jnp.dot(smoothed, vertical[...], preferred_element_type=F32)
                increment = increment + ensemble[m, rows, :].astype(F32) * leveled
        out[n * size : (n + 1) * size, :] = increment.astype(BF)


def send_kernel(cols, inner, one, two, one_corner, two_corner, band, vertical, ensemble, out, west, east):
    members, cells, _ = inner.shape
    joined((one, two), (one_corner, two_corner), (west, east), members, cols, cells)
    half_forward(cols, 1 - lax.axis_index("core"), inner, west, east, band, vertical, ensemble, out)


def keep_kernel(cols, inner, west, east, band, vertical, ensemble, out):
    half_forward(cols, lax.axis_index("core"), inner, west, east, band, vertical, ensemble, out)


def put_sums(message, sums):
    row = lax.broadcasted_iota(jnp.int32, (EXTRA, sums.shape[1]), 0)
    parts = jnp.zeros(row.shape, F32)
    for n in range(3):
        part = sums.astype(BF).astype(F32)
        parts = jnp.where(row == n, part, parts)
        sums = sums - part
    message[message.shape[0] - EXTRA :, :] = parts.astype(BF)


def get_sums(message):
    return jnp.sum(message[message.shape[0] - EXTRA :, :].astype(F32), axis=0, keepdims=True)


def share_of(bits):
    return lax.axis_index("x") ^ bits


def by_core(first, second):
    return jnp.where(lax.axis_index("core") == 0, first, second)


def near_sums(one, two):
    one, two = get_sums(one), get_sums(two)
    return by_core(one, two), by_core(two, one)


def call(kernel, name, shapes, inputs, in_specs=None, scratch=(), flops=1_000_000, size=1_000_000, out_specs=None, mib=12, aliases=None):
    return pl.pallas_call(
        kernel,
        out_shape=tuple(shapes),
        in_specs=in_specs or [VMEM] * len(inputs),
        out_specs=out_specs or (VMEM,) * len(shapes),
        scratch_shapes=scratch,
        input_output_aliases=aliases or {},
        compiler_params=params(mib),
        cost_estimate=cost(flops, size),
        name=name,
    )(*inputs)


def edges_kernel(tile, first, second):
    members, cells, _ = tile.shape
    edge = first.shape[0] // members
    odd = is_odd("lat")
    for m in range(members):
        low, high = tile[m, :edge, :], tile[m, cells - edge :, :]
        first[m * edge : (m + 1) * edge, :] = jnp.where(odd, low, high)
        second[m * edge : (m + 1) * edge, :] = jnp.where(odd, high, low)


def picker(lat_rows, cols):
    count = lat_rows * HALO
    row = lax.broadcasted_iota(jnp.int32, (2 * count, lat_rows * cols), 0)
    cell = lax.broadcasted_iota(jnp.int32, (2 * count, lat_rows * cols), 1)
    low = row < count
    at = jnp.where(low, row, row - count)
    wanted = at // HALO * cols + at % HALO + jnp.where(low, 0, cols - HALO)
    return jnp.where(cell == wanted, 1.0, 0.0).astype(BF)


def put_picked(pick, parts, place, out, odd):
    got = jnp.dot(pick, jnp.concatenate(parts, axis=1), preferred_element_type=F32).astype(BF)
    half = got.shape[0] // 2
    levels = got.shape[1] // len(parts)
    low, high = got[:half], got[half:]
    for ref, value in zip(out, (jnp.where(odd, low, high), jnp.where(odd, high, low))):
        for n, at in enumerate(place):
            ref[at : at + half, :] = value[:, n * levels : (n + 1) * levels]


def strips_kernel(cols, tile, *out):
    members, cells, _ = tile.shape
    odd = is_odd("lon")
    block = 16
    pick = picker(block, cols)
    length = cells // cols * HALO
    for start in range(0, members, 2):
        pair = (start, start + 1)
        for row in range(0, cells, block * cols):
            parts = [tile[m, row : row + block * cols, :] for m in pair]
            put_picked(pick, parts, [m * length + row // cols * HALO for m in pair], out, odd)


def strips(tile, cols):
    members, cells, levels = tile.shape
    message = jax.ShapeDtypeStruct((members * (cells // cols) * HALO, levels), BF)
    return call(
        functools.partial(strips_kernel, cols), "strips", [message] * 2, (tile,), flops=300_000_000, size=3_000_000
    )


def corners_kernel(cols, members, first, second, *refs):
    if len(refs) > 2:
        sums, far, *out, total = refs
        one, two = near_sums(first, second)
        value = (sums[0:1, :] + one) + (far[0:1, :] + two)
        total[...] = jnp.broadcast_to(value, total.shape)
        for ref in out:
            put_sums(ref, value)
    else:
        out = refs
    odd = is_odd("lon")
    edge, corner = HALO * cols, HALO * HALO
    pick = picker(HALO, cols)
    for start in range(0, members, 2):
        pair = (start, start + 1)
        ends = [south_north(first, second, slice(m * edge, (m + 1) * edge)) for m in pair]
        for n in range(2):
            put_picked(pick, [end[n] for end in ends], [(2 * m + n) * corner for m in pair], out, odd)


def corners(first, second, cols, members, *sums):
    extra = EXTRA if sums else 0
    message = jax.ShapeDtypeStruct((members * 2 * HALO * HALO + extra, first.shape[1]), BF)
    shapes = [message, message] + [jax.ShapeDtypeStruct(v.shape, F32) for v in sums[:1]]
    return call(functools.partial(corners_kernel, cols, members), "corners", shapes, (first, second, *sums))


def shares_kernel(keep, got, *shares):
    size = shares[0].shape[0]
    for bits, out in zip((0, by_core(1, 3), 2, by_core(3, 1)), shares):
        rows = pl.ds(pl.multiple_of(share_of(bits) * size, size), size)
        out[...] = (keep[rows, :].astype(F32) + got[rows, :].astype(F32)).astype(BF)


def part_kernel(zero, one, two, three, square, message):
    size = zero.shape[0]
    message[:size, :] = (
        (zero[...].astype(F32) + one[...].astype(F32)) + (two[...].astype(F32) + three[...].astype(F32))
    ).astype(BF)
    put_sums(message, jnp.sum(square[...], axis=0, keepdims=True))


def weight_kernel(message, other, precision, _, out):
    size = precision.shape[0] // 8
    share = lax.axis_index("core") * 4 + lax.axis_index("x")
    mine = precision[pl.ds(pl.multiple_of(share * size, size), size), :]
    increment = message[:size, :].astype(F32) + other[:size, :].astype(F32)
    weighted = mine * increment
    out[:size, :] = weighted.astype(BF)
    put_sums(out, (get_sums(message) + get_sums(other)) + jnp.sum(weighted * increment, axis=0, keepdims=True))


def gather_kernel(zero, one, two, three, out):
    size = zero.shape[0] - EXTRA
    for n, ref in ((0, zero), (by_core(1, 3), one), (2, two), (by_core(3, 1), three)):
        out[pl.ds(pl.multiple_of(n * size, size), size), :] = ref[:size, :]
    put_sums(out, (get_sums(zero) + get_sums(one)) + (get_sums(two) + get_sums(three)))


def adjoint_of(ensemble, weighted, vertical):
    return lax.dot_general(
        (ensemble.astype(F32) * weighted).astype(BF),
        vertical[...],
        (((1,), (1,)), ((), ())),
        preferred_element_type=F32,
    ).astype(BF)


def level_edges_kernel(mine, other, ensemble, vertical, first, second):
    members, cells, _ = ensemble.shape
    share = cells // 8
    edge = (first.shape[0] - EXTRA) // members
    core, odd = lax.axis_index("core"), is_odd("lat")
    south = pl.ds(pl.multiple_of(share_of(0) * share, edge), edge)
    north = pl.ds(pl.multiple_of(share_of(3) * share + share - edge, edge), edge)
    low_weight = jnp.where(core == 0, mine[south, :], other[south, :]).astype(F32)
    high_weight = jnp.where(core == 0, other[north, :], mine[north, :]).astype(F32)
    for m in range(members):
        low = adjoint_of(ensemble[m, :edge, :], low_weight, vertical)
        high = adjoint_of(ensemble[m, cells - edge :, :], high_weight, vertical)
        first[m * edge : (m + 1) * edge, :] = jnp.where(odd, low, high)
        second[m * edge : (m + 1) * edge, :] = jnp.where(odd, high, low)
    value = get_sums(mine) + get_sums(other)
    put_sums(first, value)
    put_sums(second, value)


def level_kernel(mine, other, ensemble, vertical, adjoint, sums):
    sums[...] = jnp.broadcast_to(get_sums(mine) + get_sums(other), sums.shape)
    members, cells, _ = adjoint.shape
    share = cells // 8
    core = lax.axis_index("core")
    for which, half in ((mine, core), (other, 1 - core)):
        for k in range(4):
            rows = pl.ds(pl.multiple_of((half * 4 + share_of(k)) * share, share), share)
            weighted = which[k * share : (k + 1) * share, :].astype(F32)
            for m in range(members):
                adjoint[m, rows, :] = adjoint_of(ensemble[m, rows, :], weighted, vertical)


def backward_kernel(
    cols, entries, outer, one, two, one_corner, two_corner, band, sums, far, _,
    hessian, curvature, result, west, east, done,
):
    members, tile_rows, width, levels = outer.shape
    cells = tile_rows * cols
    batch = 2 * ROWS
    joined((one, two), (one_corner, two_corner), (west, east), members, cols, cells)
    copies = []
    for start in range(0, members, 2):
        pair = (start, start + 1)
        for block in range(tile_rows // ROWS):
            rows = slice(block * ROWS, (block + 1) * ROWS)
            for m, side in zip(pair, sides(band, west, east, pair, block, side_rows(cells, cols))):
                result[m, rows, :, :] = outer[m, rows, :, :] + side.reshape(ROWS, width, levels)
            if (block + 1) * ROWS % batch == 0:
                rows = pl.ds((block + 1) * ROWS - batch, batch)
                for m in pair:
                    for source, target in ((0, 0), (8, cols - 8)):
                        copy = pltpu.make_async_copy(
                            result.at[m, rows, pl.ds(source, 8), :],
                            hessian.at[m, rows, pl.ds(target, 8), :],
                            done.at[len(copies)],
                        )
                        copy.start()
                        copies.append(copy)
    near, next_door = near_sums(one_corner, two_corner)
    value = (sums[0:1, :] + near) + (far[0:1, :] + next_door)
    curvature[0, 0] = jnp.sum(value) / entries
    for copy in copies:
        copy.wait()


def exchange(first, second, axis):
    groups = lax.axis_size("zh") if axis == "lat" else 1
    names = ("zh", "core", "lat") if axis == "lat" else ("core", axis)
    size = lax.axis_size(axis)
    count = groups * size

    def place(core, at):
        return (at // size * 2 + core) * size + at % size

    def near(at):
        return at ^ 1

    def next_door(at):
        return (at + 1 if at % 2 else at - 1) % count

    one, two = (
        [(place(core, at), place(core, way(at))) for core, way in enumerate(ways) for at in range(count)]
        for ways in ((near, next_door), (next_door, near))
    )
    return lax.ppermute(first, names, one), lax.ppermute(second, names, two)


def swap_x(value, first, second):
    bits = (first, second)
    return lax.ppermute(
        value,
        ("x", "core"),
        [(2 * i + core, 2 * (i ^ bits[core]) + core) for i in range(lax.axis_size("x")) for core in range(2)],
    )


def per_device(control, ensemble, precision, lat_taps, lon_taps, vertical):
    members, tile_rows, cols, levels = control.shape
    cells = tile_rows * cols
    entries = control.size * lax.axis_size(MEM) * lax.axis_size("lat") * lax.axis_size("lon")
    own, spread = control.reshape(members, cells, levels), ensemble.reshape(members, cells, levels)
    share = cells // 8
    row = jax.ShapeDtypeStruct((8, levels), F32)

    def rows(count):
        return jax.ShapeDtypeStruct((count, levels), BF)

    edge = HALO * cols
    first, second = call(edges_kernel, "edges", [rows(members * edge)] * 2, (own,))
    one, two = exchange(first, second, "lat")
    beside_it = exchange(*strips(own, cols), "lon")
    corner = exchange(*corners(one, two, cols, members), "lon")
    band, band_side = bands(lat_taps, lon_taps, cols, False)
    inner, square = call(
        functools.partial(centre_kernel, cols),
        "centre",
        [jax.ShapeDtypeStruct(own.shape, F32), row],
        (own, one, two, band),
        flops=3_000_000_000,
        size=7_000_000,
    )
    joint = rows(members * side_rows(cells, cols))
    send, west, east = call(
        functools.partial(send_kernel, cols),
        "forward_send",
        [rows(cells // 2), joint, joint],
        (inner, *beside_it, *corner, band_side, vertical, spread),
        flops=700_000_000,
        size=3_000_000,
    )
    (keep,) = call(
        functools.partial(keep_kernel, cols),
        "forward_keep",
        [rows(cells // 2)],
        (inner, west, east, band_side, vertical, spread),
        flops=700_000_000,
        size=3_000_000,
    )

    got = lax.ppermute(send, "core", swap("core", 1))
    zero, one, two, three = call(shares_kernel, "shares", [rows(share)] * 4, (keep, got))
    two, one, three = swap_x(two, 2, 2), swap_x(one, 1, 3), swap_x(three, 3, 1)
    band_back, band_side_back = bands(lat_taps, lon_taps, cols, True, three)
    (message,) = call(part_kernel, "part", [rows(share + EXTRA)], (zero, one, two, three, square))
    other = lax.ppermute(message, "zh", swap("zh", 1))
    (zero,) = call(weight_kernel, "weight", [rows(share + EXTRA)], (message, other, precision.reshape(cells, levels), band_side_back))
    two, one, three = swap_x(zero, 2, 2), swap_x(zero, 1, 3), swap_x(zero, 3, 1)
    (message,) = call(gather_kernel, "gather", [rows(cells // 2 + EXTRA)], (zero, one, two, three))
    other = lax.ppermute(message, "core", swap("core", 1))

    message_shape = rows(members * edge + EXTRA)
    first, second = call(
        level_edges_kernel, "level_edges", [message_shape, message_shape], (message, other, spread, vertical)
    )
    adjoint, sums = call(
        level_kernel,
        "level",
        [jax.ShapeDtypeStruct(own.shape, BF), row],
        (message, other, spread, vertical),
        flops=300_000_000,
        size=4_500_000,
    )
    one, two = exchange(first, second, "lat")
    far = lax.ppermute(sums, "lat", swap("lat", 2))
    beside_it = exchange(*strips(adjoint, cols), "lon")
    *corner, sums = corners(one, two, cols, members, sums, far)
    corner = exchange(*corner, "lon")
    outer_shape = (members, tile_rows, 16, levels)
    far = lax.ppermute(sums, "lon", swap("lon", 2))
    hessian, outer = call(
        functools.partial(centre_back_kernel, cols),
        "centre_back",
        [jax.ShapeDtypeStruct(control.shape, F32), jax.ShapeDtypeStruct(outer_shape, F32)],
        (adjoint, one, two, band_back, own),
        out_specs=(pl.BlockSpec(memory_space=pl.ANY), VMEM),
        scratch=(
            pltpu.VMEM((members, tile_rows, cols - 16, levels), F32),
            pltpu.SemaphoreType.DMA((members * tile_rows // (2 * ROWS),)),
        ),
        flops=3_000_000_000,
        size=7_000_000,
    )
    hessian, curvature = call(
        functools.partial(backward_kernel, cols, entries),
        "backward",
        [jax.ShapeDtypeStruct(control.shape, F32), jax.ShapeDtypeStruct((1, 1), F32)],
        (outer, *beside_it, *corner, band_side_back, sums, far, hessian),
        in_specs=[VMEM] * 8 + [pl.BlockSpec(memory_space=pl.ANY)],
        scratch=(
            pltpu.VMEM(outer_shape, F32),
            pltpu.VMEM(joint.shape, BF),
            pltpu.VMEM(joint.shape, BF),
            pltpu.SemaphoreType.DMA((2 * members * tile_rows // (2 * ROWS),)),
        ),
        out_specs=(pl.BlockSpec(memory_space=pl.ANY), SMEM),
        aliases={8: 0},
        flops=1_000_000_000,
        size=9_000_000,
    )
    return hessian, curvature.reshape(())


def solution(mesh):
    split = Mesh(
        mesh.devices.reshape(2, 4, 2, mesh.shape["lat"], mesh.shape["lon"]),
        ("zh", "x", "core", "lat", "lon"),
    )
    return jax.shard_map(
        per_device,
        mesh=split,
        in_specs=(
            P(MEM, "lat", "lon", None),
            P(MEM, "lat", "lon", None),
            P("lat", "lon", None),
            P(),
            P(),
            P(),
        ),
        out_specs=(P(MEM, "lat", "lon", None), P()),
        check_vma=False,
    )
```

```python
import functools

import jax
import jax.numpy as jnp
from jax import lax
from jax.experimental import pallas as pl
from jax.experimental.pallas import tpu as pltpu
from jax.sharding import Mesh
from jax.sharding import PartitionSpec as P

MEM = ("zh", "x", "core")
BF = jnp.bfloat16
F32 = jnp.float32
HALO = 4
TAPS = 9
ROWS = 8
VMEM = pl.BlockSpec(memory_space=pltpu.VMEM)
SMEM = pl.BlockSpec(memory_space=pltpu.SMEM)
EXTRA = 16


def swap(axis, bits):
    return [(i, i ^ bits) for i in range(lax.axis_size(axis))]


def params(mib=12):
    return pltpu.CompilerParams(vmem_limit_bytes=mib * 2**20)


def cost(flops, size):
    return pl.CostEstimate(flops=flops, bytes_accessed=size, transcendentals=0)


def is_odd(axis):
    return lax.rem(lax.axis_index(axis), 2) == 1


def taps_at(index, taps, flip):
    value = jnp.zeros(index.shape, F32)
    for t in range(TAPS):
        value = jnp.where(index == t, taps[TAPS - 1 - t if flip else t], value)
    return value


def put_halves(out, row, value):
    high = value.astype(BF)
    size = value.shape[0]
    out[row : row + size, :] = high
    out[row + out.shape[0] // 2 : row + out.shape[0] // 2 + size, :] = (value - high.astype(F32)).astype(BF)


def band_kernel(cols, flip, lat_taps, lon_taps, *refs):
    wide, narrow = refs[-2:]
    k = lax.broadcasted_iota(jnp.int32, (cols, wide.shape[1]), 1)
    j = lax.broadcasted_iota(jnp.int32, (cols, wide.shape[1]), 0)
    row, shift = k // cols, k % cols - j + HALO
    k2 = lax.broadcasted_iota(jnp.int32, (16, narrow.shape[1]), 1)
    j2 = lax.broadcasted_iota(jnp.int32, (16, narrow.shape[1]), 0)
    half = narrow.shape[1] // 2
    in_west = k2 < half
    row2 = jnp.where(in_west, k2, k2 - half) // HALO
    column = k2 % HALO
    target = jnp.where(j2 < 8, j2, j2 + cols - 16)
    shift2 = jnp.where(in_west, column, column + cols + HALO) - target
    across = taps_at(shift, lon_taps, flip)
    across2 = taps_at(shift2, lon_taps, flip)
    for i in range(ROWS):
        put_halves(wide, i * cols, taps_at(row - i, lat_taps, flip) * across)
        put_halves(narrow, i * 16, taps_at(row2 - i, lat_taps, flip) * across2)


def bands(lat_taps, lon_taps, cols, flip, *after):
    span = ROWS + 2 * HALO
    wide = jax.ShapeDtypeStruct((2 * ROWS * cols, span * cols), BF)
    narrow = jax.ShapeDtypeStruct((2 * ROWS * 16, 2 * span * HALO), BF)
    return pl.pallas_call(
        functools.partial(band_kernel, cols, flip),
        out_shape=(wide, narrow),
        in_specs=[SMEM, SMEM] + [VMEM] * len(after),
        out_specs=(VMEM,) * 2,
        compiler_params=params(),
        cost_estimate=cost(2_000_000, 600_000),
        name="bands_back" if flip else "bands",
    )(lat_taps, lon_taps, *after)


def south_north(first, second, rows):
    odd = is_odd("lat")
    at = lax.axis_index("lat")
    zero = jnp.zeros((rows.stop - rows.start, first.shape[1]), BF)
    one, two = first[rows, :], second[rows, :]
    south = jnp.where(at == 0, zero, jnp.where(odd, one, two))
    north = jnp.where(at == lax.axis_size("lat") - 1, zero, jnp.where(odd, two, one))
    return south, north


def centre_blocks(cols, own, first, second, band):
    members, cells, levels = own.shape
    size, edge = ROWS * cols, HALO * cols
    for start in range(0, members, 2):
        pair = (start, start + 1)
        edges = [south_north(first, second, slice(m * edge, (m + 1) * edge)) for m in pair]
        for row in range(0, cells, size):
            lo, hi = max(row - edge, 0), min(row + size + edge, cells)
            parts = []
            for m, (south, north) in zip(pair, edges):
                part = [south] if row == 0 else []
                part.append(own[m, lo:hi, :])
                if row + size == cells:
                    part.append(north)
                parts.append(jnp.concatenate(part, axis=0) if len(part) > 1 else part[0])
            both = jnp.dot(band[...], jnp.concatenate(parts, axis=1), preferred_element_type=F32)
            both = both[:size] + both[size:]
            for n, m in enumerate(pair):
                yield m, row, both[:, n * levels : (n + 1) * levels]


def centre_kernel(cols, own, first, second, band, out, square):
    levels = own.shape[2]
    size = ROWS * cols
    total = jnp.zeros((8, levels), F32)
    for m, row, value in centre_blocks(cols, own, first, second, band):
        out[m, row : row + size, :] = value
        c = own[m, row : row + size, :].astype(F32)
        total = total + jnp.sum((c * c).reshape(size // 8, 8, levels), axis=0)
    square[...] = total


def centre_back_kernel(cols, own, first, second, band, control, hessian, outer, rest, middle, done):
    members, cells, levels = own.shape
    size = ROWS * cols
    batch = 2 * ROWS
    copies = []
    for m, row, value in centre_blocks(cols, own, first, second, band):
        value = (control[m, row : row + size, :].astype(F32) + value).reshape(ROWS, cols, levels)
        at = row // cols
        rows = slice(at, at + ROWS)
        late = m >= members // 2
        place = rest if late else middle
        place[m % (members // 2), rows, :, :] = value[:, 8 : cols - 8]
        outer[m, rows, :8, :] = value[:, :8]
        outer[m, rows, 8:, :] = value[:, cols - 8 :]
        if not late and (at + ROWS) % batch == 0:
            rows = pl.ds(at + ROWS - batch, batch)
            copy = pltpu.make_async_copy(
                middle.at[m, rows], hessian.at[m, rows, pl.ds(8, cols - 16), :], done.at[len(copies)]
            )
            copy.start()
            copies.append(copy)
    for copy in copies:
        copy.wait()


def joined(strips, corners, out, members, cols, cells):
    odd = is_odd("lon")
    edge = HALO * HALO
    length = cells // cols * HALO
    for m in range(members):
        at = m * (length + 2 * edge)
        for place, refs, start, size in (
            (at, corners, 2 * m * edge, edge),
            (at + edge, strips, m * length, length),
            (at + edge + length, corners, (2 * m + 1) * edge, edge),
        ):
            one, two = (ref[start : start + size, :] for ref in refs)
            out[0][place : place + size, :] = jnp.where(odd, one, two)
            out[1][place : place + size, :] = jnp.where(odd, two, one)


def side_rows(cells, cols):
    return (cells // cols + 2 * HALO) * HALO


def sides(band, west, east, pair, block, stride):
    count = (ROWS + 2 * HALO) * HALO
    parts = []
    for m in pair:
        at = pl.ds(pl.multiple_of(m * stride + block * ROWS * HALO, 32), count)
        parts.append(jnp.concatenate([west[at, :], east[at, :]], axis=0))
    both = jnp.dot(band[...], jnp.concatenate(parts, axis=1), preferred_element_type=F32)
    size = both.shape[0] // 2
    both = both[:size] + both[size:]
    levels = both.shape[1] // len(pair)
    return [both[:, n * levels : (n + 1) * levels] for n in range(len(pair))]


def with_sides(value, side, cols):
    levels = value.shape[1]
    value = value.reshape(ROWS, cols, levels)
    side = side.reshape(ROWS, 16, levels)
    return jnp.concatenate(
        [value[:, :8] + side[:, :8], value[:, 8 : cols - 8], value[:, cols - 8 :] + side[:, 8:]], axis=1
    ).reshape(ROWS * cols, levels)


def half_forward(cols, half, inner, west, east, band, vertical, ensemble, out):
    members, cells, levels = inner.shape
    size = ROWS * cols
    count = cells // size // 2
    stride = side_rows(cells, cols)
    for n in range(count):
        block = half * count + n
        rows = pl.ds(pl.multiple_of(block * size, size), size)
        increment = jnp.zeros((size, levels), F32)
        for start in range(0, members, 2):
            pair = (start, start + 1)
            for m, side in zip(pair, sides(band, west, east, pair, block, stride)):
                smoothed = with_sides(inner[m, rows, :], side, cols).astype(BF)
                leveled = jnp.dot(smoothed, vertical[...], preferred_element_type=F32)
                increment = increment + ensemble[m, rows, :].astype(F32) * leveled
        out[n * size : (n + 1) * size, :] = increment.astype(BF)


def send_kernel(cols, inner, one, two, one_corner, two_corner, band, vertical, ensemble, out, west, east):
    members, cells, _ = inner.shape
    joined((one, two), (one_corner, two_corner), (west, east), members, cols, cells)
    half_forward(cols, 1 - lax.axis_index("core"), inner, west, east, band, vertical, ensemble, out)


def keep_kernel(cols, inner, west, east, band, vertical, ensemble, out):
    half_forward(cols, lax.axis_index("core"), inner, west, east, band, vertical, ensemble, out)


def put_sums(message, sums):
    row = lax.broadcasted_iota(jnp.int32, (EXTRA, sums.shape[1]), 0)
    parts = jnp.zeros(row.shape, F32)
    for n in range(3):
        part = sums.astype(BF).astype(F32)
        parts = jnp.where(row == n, part, parts)
        sums = sums - part
    message[message.shape[0] - EXTRA :, :] = parts.astype(BF)


def get_sums(message):
    return jnp.sum(message[message.shape[0] - EXTRA :, :].astype(F32), axis=0, keepdims=True)


def share_of(bits):
    return lax.axis_index("x") ^ bits


def call(kernel, name, shapes, inputs, in_specs=None, scratch=(), flops=1_000_000, size=1_000_000, out_specs=None, mib=12, aliases=None):
    return pl.pallas_call(
        kernel,
        out_shape=tuple(shapes),
        in_specs=in_specs or [VMEM] * len(inputs),
        out_specs=out_specs or (VMEM,) * len(shapes),
        scratch_shapes=scratch,
        input_output_aliases=aliases or {},
        compiler_params=params(mib),
        cost_estimate=cost(flops, size),
        name=name,
    )(*inputs)


def edges_kernel(tile, first, second):
    members, cells, _ = tile.shape
    edge = first.shape[0] // members
    odd = is_odd("lat")
    for m in range(members):
        low, high = tile[m, :edge, :], tile[m, cells - edge :, :]
        first[m * edge : (m + 1) * edge, :] = jnp.where(odd, low, high)
        second[m * edge : (m + 1) * edge, :] = jnp.where(odd, high, low)


def picker(lat_rows, cols):
    count = lat_rows * HALO
    row = lax.broadcasted_iota(jnp.int32, (2 * count, lat_rows * cols), 0)
    cell = lax.broadcasted_iota(jnp.int32, (2 * count, lat_rows * cols), 1)
    low = row < count
    at = jnp.where(low, row, row - count)
    wanted = at // HALO * cols + at % HALO + jnp.where(low, 0, cols - HALO)
    return jnp.where(cell == wanted, 1.0, 0.0).astype(BF)


def put_picked(pick, parts, place, out, odd):
    got = jnp.dot(pick, jnp.concatenate(parts, axis=1), preferred_element_type=F32).astype(BF)
    half = got.shape[0] // 2
    levels = got.shape[1] // len(parts)
    low, high = got[:half], got[half:]
    for ref, value in zip(out, (jnp.where(odd, low, high), jnp.where(odd, high, low))):
        for n, at in enumerate(place):
            ref[at : at + half, :] = value[:, n * levels : (n + 1) * levels]


def strips_kernel(cols, tile, *out):
    members, cells, _ = tile.shape
    odd = is_odd("lon")
    block = 16
    pick = picker(block, cols)
    length = cells // cols * HALO
    for start in range(0, members, 2):
        pair = (start, start + 1)
        for row in range(0, cells, block * cols):
            parts = [tile[m, row : row + block * cols, :] for m in pair]
            put_picked(pick, parts, [m * length + row // cols * HALO for m in pair], out, odd)


def strips(tile, cols):
    members, cells, levels = tile.shape
    message = jax.ShapeDtypeStruct((members * (cells // cols) * HALO, levels), BF)
    return call(
        functools.partial(strips_kernel, cols), "strips", [message] * 2, (tile,), flops=300_000_000, size=3_000_000
    )


def corners_kernel(cols, members, first, second, *refs):
    if len(refs) > 2:
        sums, far, *out, total = refs
        value = (sums[0:1, :] + get_sums(first)) + (far[0:1, :] + get_sums(second))
        total[...] = jnp.broadcast_to(value, total.shape)
        for ref in out:
            put_sums(ref, value)
    else:
        out = refs
    odd = is_odd("lon")
    edge, corner = HALO * cols, HALO * HALO
    pick = picker(HALO, cols)
    for start in range(0, members, 2):
        pair = (start, start + 1)
        ends = [south_north(first, second, slice(m * edge, (m + 1) * edge)) for m in pair]
        for n in range(2):
            put_picked(pick, [end[n] for end in ends], [(2 * m + n) * corner for m in pair], out, odd)


def corners(first, second, cols, members, *sums):
    extra = EXTRA if sums else 0
    message = jax.ShapeDtypeStruct((members * 2 * HALO * HALO + extra, first.shape[1]), BF)
    shapes = [message, message] + [jax.ShapeDtypeStruct(v.shape, F32) for v in sums[:1]]
    return call(functools.partial(corners_kernel, cols, members), "corners", shapes, (first, second, *sums))


def shares_kernel(keep, got, *shares):
    size = shares[0].shape[0]
    for bits, out in enumerate(shares):
        rows = pl.ds(pl.multiple_of(share_of(bits) * size, size), size)
        out[...] = (keep[rows, :].astype(F32) + got[rows, :].astype(F32)).astype(BF)


def part_kernel(zero, one, two, three, square, message):
    size = zero.shape[0]
    message[:size, :] = (
        (zero[...].astype(F32) + one[...].astype(F32)) + (two[...].astype(F32) + three[...].astype(F32))
    ).astype(BF)
    put_sums(message, jnp.sum(square[...], axis=0, keepdims=True))


def weight_kernel(message, other, precision, _, out):
    size = precision.shape[0] // 8
    share = lax.axis_index("core") * 4 + lax.axis_index("x")
    mine = precision[pl.ds(pl.multiple_of(share * size, size), size), :]
    increment = message[:size, :].astype(F32) + other[:size, :].astype(F32)
    weighted = mine * increment
    out[:size, :] = weighted.astype(BF)
    put_sums(out, (get_sums(message) + get_sums(other)) + jnp.sum(weighted * increment, axis=0, keepdims=True))


def gather_kernel(zero, one, two, three, out):
    size = zero.shape[0] - EXTRA
    for n, ref in enumerate((zero, one, two, three)):
        out[n * size : (n + 1) * size, :] = ref[:size, :]
    put_sums(out, (get_sums(zero) + get_sums(one)) + (get_sums(two) + get_sums(three)))


def adjoint_of(ensemble, weighted, vertical):
    return lax.dot_general(
        (ensemble.astype(F32) * weighted).astype(BF),
        vertical[...],
        (((1,), (1,)), ((), ())),
        preferred_element_type=F32,
    ).astype(BF)


def level_edges_kernel(mine, other, ensemble, vertical, first, second):
    members, cells, _ = ensemble.shape
    share = cells // 8
    edge = (first.shape[0] - EXTRA) // members
    core, odd = lax.axis_index("core"), is_odd("lat")
    south = pl.ds(pl.multiple_of(share_of(0) * share, edge), edge)
    north = pl.ds(pl.multiple_of(share_of(3) * share + share - edge, edge), edge)
    low_weight = jnp.where(core == 0, mine[south, :], other[south, :]).astype(F32)
    high_weight = jnp.where(core == 0, other[north, :], mine[north, :]).astype(F32)
    for m in range(members):
        low = adjoint_of(ensemble[m, :edge, :], low_weight, vertical)
        high = adjoint_of(ensemble[m, cells - edge :, :], high_weight, vertical)
        first[m * edge : (m + 1) * edge, :] = jnp.where(odd, low, high)
        second[m * edge : (m + 1) * edge, :] = jnp.where(odd, high, low)
    value = get_sums(mine) + get_sums(other)
    put_sums(first, value)
    put_sums(second, value)


def level_kernel(cols, mine, other, ensemble, vertical, adjoint, sums, *out):
    sums[...] = jnp.broadcast_to(get_sums(mine) + get_sums(other), sums.shape)
    members, cells, _ = adjoint.shape
    share = cells // 8
    core = lax.axis_index("core")
    for which, half in ((mine, core), (other, 1 - core)):
        for k in range(4):
            rows = pl.ds(pl.multiple_of((half * 4 + share_of(k)) * share, share), share)
            weighted = which[k * share : (k + 1) * share, :].astype(F32)
            for m in range(members):
                adjoint[m, rows, :] = adjoint_of(ensemble[m, rows, :], weighted, vertical)
    strips_kernel(cols, adjoint, *out)


def backward_kernel(
    cols, entries, outer, rest, one, two, one_corner, two_corner, band, sums, far, _,
    hessian, curvature, result, west, east, done,
):
    members, tile_rows, width, levels = outer.shape
    cells = tile_rows * cols
    batch = 2 * ROWS
    copies = []
    for m in range(members // 2, members):
        copy = pltpu.make_async_copy(
            rest.at[m - members // 2], hessian.at[m, :, pl.ds(8, cols - 16), :], done.at[len(copies)]
        )
        copy.start()
        copies.append(copy)
    joined((one, two), (one_corner, two_corner), (west, east), members, cols, cells)
    for start in range(0, members, 2):
        pair = (start, start + 1)
        for block in range(tile_rows // ROWS):
            rows = slice(block * ROWS, (block + 1) * ROWS)
            for m, side in zip(pair, sides(band, west, east, pair, block, side_rows(cells, cols))):
                result[m, rows, :, :] = outer[m, rows, :, :] + side.reshape(ROWS, width, levels)
            if (block + 1) * ROWS % batch == 0:
                rows = pl.ds((block + 1) * ROWS - batch, batch)
                for m in pair:
                    for source, target in ((0, 0), (8, cols - 8)):
                        copy = pltpu.make_async_copy(
                            result.at[m, rows, pl.ds(source, 8), :],
                            hessian.at[m, rows, pl.ds(target, 8), :],
                            done.at[len(copies)],
                        )
                        copy.start()
                        copies.append(copy)
    value = (sums[0:1, :] + get_sums(one_corner)) + (far[0:1, :] + get_sums(two_corner))
    curvature[0, 0] = jnp.sum(value) / entries
    for copy in copies:
        copy.wait()


def exchange(first, second, axis):
    if axis == "lat":
        count = lax.axis_size("zh") * lax.axis_size("lat")
        axis = ("zh", "lat")
    else:
        count = lax.axis_size(axis)
    one = [(i, i ^ 1) for i in range(count)]
    two = [(i, (i + 1 if i % 2 else i - 1) % count) for i in range(count)]
    return lax.ppermute(first, axis, one), lax.ppermute(second, axis, two)


def per_device(control, ensemble, precision, lat_taps, lon_taps, vertical):
    members, tile_rows, cols, levels = control.shape
    cells = tile_rows * cols
    entries = control.size * lax.axis_size(MEM) * lax.axis_size("lat") * lax.axis_size("lon")
    own, spread = control.reshape(members, cells, levels), ensemble.reshape(members, cells, levels)
    share = cells // 8
    row = jax.ShapeDtypeStruct((8, levels), F32)

    def rows(count):
        return jax.ShapeDtypeStruct((count, levels), BF)

    edge = HALO * cols
    first, second = call(edges_kernel, "edges", [rows(members * edge)] * 2, (own,))
    one, two = exchange(first, second, "lat")
    beside_it = exchange(*strips(own, cols), "lon")
    corner = exchange(*corners(one, two, cols, members), "lon")
    band, band_side = bands(lat_taps, lon_taps, cols, False)
    inner, square = call(
        functools.partial(centre_kernel, cols),
        "centre",
        [jax.ShapeDtypeStruct(own.shape, F32), row],
        (own, one, two, band),
        flops=3_000_000_000,
        size=7_000_000,
    )
    joint = rows(members * side_rows(cells, cols))
    send, west, east = call(
        functools.partial(send_kernel, cols),
        "forward_send",
        [rows(cells // 2), joint, joint],
        (inner, *beside_it, *corner, band_side, vertical, spread),
        flops=700_000_000,
        size=3_000_000,
    )
    (keep,) = call(
        functools.partial(keep_kernel, cols),
        "forward_keep",
        [rows(cells // 2)],
        (inner, west, east, band_side, vertical, spread),
        flops=700_000_000,
        size=3_000_000,
    )

    got = lax.ppermute(send, "core", swap("core", 1))
    zero, one, two, three = call(shares_kernel, "shares", [rows(share)] * 4, (keep, got))
    two, one, three = [lax.ppermute(v, "x", swap("x", k)) for v, k in ((two, 2), (one, 1), (three, 3))]
    band_back, band_side_back = bands(lat_taps, lon_taps, cols, True, three)
    (message,) = call(part_kernel, "part", [rows(share + EXTRA)], (zero, one, two, three, square))
    other = lax.ppermute(message, "zh", swap("zh", 1))
    (zero,) = call(weight_kernel, "weight", [rows(share + EXTRA)], (message, other, precision.reshape(cells, levels), band_side_back))
    two, one, three = [lax.ppermute(zero, "x", swap("x", k)) for k in (2, 1, 3)]
    (message,) = call(gather_kernel, "gather", [rows(cells // 2 + EXTRA)], (zero, one, two, three))
    other = lax.ppermute(message, "core", swap("core", 1))

    message_shape = rows(members * edge + EXTRA)
    first, second = call(
        level_edges_kernel, "level_edges", [message_shape, message_shape], (message, other, spread, vertical)
    )
    adjoint, sums, low, high = call(
        functools.partial(level_kernel, cols),
        "level",
        [jax.ShapeDtypeStruct(own.shape, BF), row] + [rows(members * tile_rows * HALO)] * 2,
        (message, other, spread, vertical),
        flops=300_000_000,
        size=4_500_000,
    )
    one, two = exchange(first, second, "lat")
    far = lax.ppermute(sums, "lat", swap("lat", 2))
    beside_it = exchange(low, high, "lon")
    *corner, sums = corners(one, two, cols, members, sums, far)
    corner = exchange(*corner, "lon")
    outer_shape = (members, tile_rows, 16, levels)
    far = lax.ppermute(sums, "lon", swap("lon", 2))
    rest_shape = (members // 2, tile_rows, cols - 16, levels)
    hessian, outer, rest = call(
        functools.partial(centre_back_kernel, cols),
        "centre_back",
        [jax.ShapeDtypeStruct(control.shape, F32), jax.ShapeDtypeStruct(outer_shape, F32), jax.ShapeDtypeStruct(rest_shape, F32)],
        (adjoint, one, two, band_back, own),
        out_specs=(pl.BlockSpec(memory_space=pl.ANY), VMEM, VMEM),
        scratch=(
            pltpu.VMEM(rest_shape, F32),
            pltpu.SemaphoreType.DMA((members // 2 * tile_rows // (2 * ROWS),)),
        ),
        flops=3_000_000_000,
        size=7_000_000,
    )
    hessian, curvature = call(
        functools.partial(backward_kernel, cols, entries),
        "backward",
        [jax.ShapeDtypeStruct(control.shape, F32), jax.ShapeDtypeStruct((1, 1), F32)],
        (outer, rest, *beside_it, *corner, band_side_back, sums, far, hessian),
        in_specs=[VMEM] * 9 + [pl.BlockSpec(memory_space=pl.ANY)],
        scratch=(
            pltpu.VMEM(outer_shape, F32),
            pltpu.VMEM(joint.shape, BF),
            pltpu.VMEM(joint.shape, BF),
            pltpu.SemaphoreType.DMA((2 * members * tile_rows // (2 * ROWS) + members // 2,)),
        ),
        out_specs=(pl.BlockSpec(memory_space=pl.ANY), SMEM),
        aliases={9: 0},
        flops=1_000_000_000,
        size=9_000_000,
    )
    return hessian, curvature.reshape(())


def solution(mesh):
    split = Mesh(
        mesh.devices.reshape(2, 4, 2, mesh.shape["lat"], mesh.shape["lon"]),
        ("zh", "x", "core", "lat", "lon"),
    )
    return jax.shard_map(
        per_device,
        mesh=split,
        in_specs=(
            P(MEM, "lat", "lon", None),
            P(MEM, "lat", "lon", None),
            P("lat", "lon", None),
            P(),
            P(),
            P(),
        ),
        out_specs=(P(MEM, "lat", "lon", None), P()),
        check_vma=False,
    )
```
